512 devices in a mesh: dp: 64 (over z, x), mp: 8 (over y, core).
Axes of the slice: x: 4, y: 4, z: 16, core: 2. Of those that a mesh axis runs over, the one named last changes fastest.
Arguments:
- activations: bfloat16 [8, 512, 16384], P(None, 'mp', 'dp'), may hold values from -16 to 16
- out_grads: bfloat16 [16384, 6144], P('dp'), may hold values from -16 to 16
- owners: int32 [96], replicated, may hold values from 0 to 63, as said below
- live_rows: int32 [96], replicated, may hold values from 64 to 512
- left_stat: float32 [64, 2, 512, 512], P('dp', None, 'mp'), may hold values from -6 to 6
- right_stat: float32 [64, 2, 512, 512], P('dp', None, 'mp'), may hold values from -6 to 6
- left_root: bfloat16 [64, 2, 512, 512], P('dp', None, 'mp'), may hold values from -1 to 2
- right_root: bfloat16 [64, 2, 512, 512], P('dp', None, 'mp'), may hold values from -1 to 2
- grad_acc: float32 [64, 2, 512, 512], P('dp', None, 'mp'), may hold values from 0.05 to 2
Outputs:
- left_new: float32 [64, 2, 512, 512], P('dp', None, 'mp')
- right_new: float32 [64, 2, 512, 512], P('dp', None, 'mp')
- acc_new: float32 [64, 2, 512, 512], P('dp', None, 'mp')
- directions: bfloat16 [64, 2, 512, 512], P('dp')
The draws below stay inside these ranges and needn't reach their ends.
Inputs may be any that keep to these rules, and one draw needn't show every extreme that they name: `owners`: no owner index appears more than 2 times, and some owner appears exactly 2 times.
All inputs are finite; a program needn't handle non-finite values.
Results may differ from the reference program's by a relative error of at most 0.0064.
Values may be sent and summed in bfloat16 or wider, within the bound.
No kernel may reach another device: no remote copies, remote signals or barrier semaphores. Data moves between devices by JAX's collectives and lax.ppermute only.
A program may use at most 128 MiB of HBM per device.

```python
import math
import jax
import jax.numpy as jnp
from jax import lax

S = 512
TOK_DEV = 256
BR = 8
SLOTS = 2
BC = 12
NB = 96
TOKENS = 16384
N_DP = 64


def spread_scale(key_scale, dims_all):
    return jnp.exp(jax.random.uniform(key_scale, dims_all, jnp.float32, math.log(0.4), math.log(4.0)))


def draw_activations(key, part):
    key = jax.random.fold_in(key, 11)
    key_scale, key_values = jax.random.split(key, 2)
    dims_all = (BR, S, TOKENS)
    row_scale = spread_scale(key_scale, (BR, S, 1))
    values = jnp.clip(jax.random.normal(key_values, dims_all, jnp.float32), -4.0, 4.0)
    return (values * row_scale).astype(jnp.bfloat16)


def draw_out_grads(key, part):
    key = jax.random.fold_in(key, 13)
    key_scale, key_values = jax.random.split(key, 2)
    dims_all = (TOKENS, BC * S)
    column_scale = spread_scale(key_scale, (1, BC * S))
    values = jnp.clip(jax.random.normal(key_values, dims_all, jnp.float32), -4.0, 4.0)
    return (values * column_scale * (1.0 / math.sqrt(TOKENS))).astype(jnp.bfloat16)


def root_matrix(noise):
    dims_all = (N_DP, SLOTS, S, S)
    diagonal = (lax.broadcasted_iota(jnp.int32, dims_all, 2) == lax.broadcasted_iota(jnp.int32, dims_all, 3)).astype(jnp.float32)
    return (diagonal + 0.5 * noise * (1.0 / math.sqrt(S))).astype(jnp.bfloat16)


def draw_left_root(key, part):
    key = jax.random.fold_in(key, 21)
    dims_all = (N_DP, SLOTS, S, S)
    noise = jnp.clip(jax.random.normal(key, dims_all, jnp.float32), -4.0, 4.0)
    return root_matrix(noise)


def draw_right_root(key, part):
    key = jax.random.fold_in(key, 23)
    dims_all = (N_DP, SLOTS, S, S)
    noise = jnp.clip(jax.random.normal(key, dims_all, jnp.float32), -4.0, 4.0)
    return root_matrix(noise)


def draw_owners(key, part):
    key = jax.random.fold_in(key, 41)
    key_order, key_spot, key_turn = jax.random.split(key, 3)
    slot_total = N_DP * SLOTS
    slot_order = jax.random.permutation(key_order, slot_total).astype(jnp.int32)
    first_id = slot_order[0]
    partner = first_id + 1 - 2 * (first_id % 2)
    where_is = jnp.argmax(slot_order == partner).astype(jnp.int32)
    spot_index = jax.random.randint(key_spot, (), 1, NB).astype(jnp.int32)
    moved_id = slot_order[spot_index]
    slot_order = slot_order.at[where_is].set(moved_id).at[spot_index].set(partner)
    turn_shift = jax.random.randint(key_turn, (), 0, NB).astype(jnp.int32)
    pick_index = (jnp.arange(NB, dtype=jnp.int32) + turn_shift) % NB
    return (slot_order[:NB] // SLOTS)[pick_index].astype(jnp.int32)


def touch_ends(values, own_key, low, top_value):
    shape = values.shape
    spot = [jax.random.randint(jax.random.fold_in(own_key, axis), (), 0, shape[axis]) for axis in range(len(shape))]
    values = values.at[tuple(spot)].set(low)
    longest = shape.index(max(shape))
    spot[longest] = (spot[longest] + 1) % shape[longest]
    return values.at[tuple(spot)].set(top_value)


def block_levels(rng, extent, cuts, least, top_value):
    def one(position, blocks):
        draws = jax.random.uniform(jax.random.fold_in(jax.random.fold_in(rng, 6), position), (blocks,), jnp.float32, least / len(cuts), top_value / len(cuts))
        return jnp.repeat(jnp.exp(draws), extent[position] // blocks).reshape((-1,) + (1,) * (len(extent) - position - 1))

    loudness = one(*cuts[0])
    for cut in cuts[1:]:
        loudness = loudness * one(*cut)
    return loudness


def scatter_about(stream_key, dims, spread, reach, cuts=(), held_as=jnp.bfloat16):
    factor_of = block_levels(stream_key, dims, cuts, -0.22, 0.18) if cuts else 1.0
    array = jax.random.normal(stream_key, dims, jnp.float32) * spread * factor_of
    return jnp.minimum(jnp.maximum(array, -reach), reach).astype(held_as)


def setup_inputs(seed: int = 0) -> dict:
    keys = jax.random.split(jax.random.key(seed), 10)
    return {
        "activations": draw_activations(jax.random.fold_in(keys[9], 71), 0),
        "out_grads": draw_out_grads(jax.random.fold_in(keys[9], 71), 0),
        "owners": draw_owners(jax.random.fold_in(keys[9], 71), 0),
        "live_rows": touch_ends(jax.random.randint(keys[3], (NB,), S // 8, S + 1), jax.random.fold_in(keys[3], 1), S // 8, S).astype(jnp.int32),
        "left_stat": scatter_about(keys[4], (N_DP, SLOTS, S, S), 1.0, 6.0, ((0, 64), (2, 8)), jnp.float32),
        "right_stat": scatter_about(keys[5], (N_DP, SLOTS, S, S), 1.0, 6.0, ((0, 64), (2, 8)), jnp.float32),
        "left_root": draw_left_root(jax.random.fold_in(keys[9], 71), 0),
        "right_root": draw_right_root(jax.random.fold_in(keys[9], 71), 0),
        "grad_acc": jnp.clip(jnp.exp(math.log(2.0) - 3.6888794 * jax.random.uniform(keys[8], (N_DP, SLOTS, S, S), jnp.float32) ** block_levels(keys[8], (N_DP, SLOTS, S, S), ((0, 64), (2, 8)), -0.2, 0.2)), 0.05, 2.0),
    }


STAT_DECAY = 0.9
GRAFT_EPS = 1e-06

def slot_targets(owners, slot_count):
    block_count = owners.shape[0]
    same_owner = owners[:, None] == owners[None, :]
    earlier = lax.broadcasted_iota(jnp.int32, (block_count, block_count), 1) < lax.broadcasted_iota(jnp.int32, (block_count, block_count), 0)
    ranked = lax.optimization_barrier(jnp.sum(jnp.where(same_owner & earlier, 1, 0), axis=1)).astype(jnp.int32)
    return owners.astype(jnp.int32) * slot_count + ranked

def reference(activations, out_grads, owners, live_rows, left_stat, right_stat, left_root, right_root, grad_acc):
    block_count = owners.shape[0]
    column_blocks = out_grads.shape[1] // S

    def add_replica(replica, totals):
        start_tok = (replica * TOK_DEV).astype(jnp.int32)
        acts_part = lax.dynamic_slice_in_dim(activations, start_tok, TOK_DEV, 2).astype(jnp.float32)
        grads_part = lax.dynamic_slice_in_dim(out_grads, start_tok, TOK_DEV, 0).astype(jnp.float32)
        product = jnp.einsum('irt,tc->irc', acts_part, grads_part)
        rounded = lax.optimization_barrier(product.astype(jnp.bfloat16))
        return totals + rounded.astype(jnp.float32)
    summed = lax.fori_loop(0, N_DP, add_replica, jnp.zeros((BR, S, column_blocks * S), jnp.float32))
    grad_sum = summed.reshape(BR, S, column_blocks, S).transpose(0, 2, 1, 3).reshape(block_count, S, S)
    row_ids = lax.broadcasted_iota(jnp.int32, (block_count, S, 1), 1)
    row_mask = row_ids < live_rows.astype(jnp.int32)[:, None, None]
    grad_sum = jnp.where(row_mask, grad_sum, jnp.float32(0.0))
    grad_half = grad_sum.astype(jnp.bfloat16)
    grad_wide = grad_half.astype(jnp.float32)
    targets = slot_targets(owners, SLOTS)
    flat_count = N_DP * SLOTS

    def flatten_slots(values):
        return values.reshape(flat_count, S, S)
    left_old = flatten_slots(left_stat)[targets]
    right_old = flatten_slots(right_stat)[targets]
    acc_old = flatten_slots(grad_acc)[targets]
    lroot_blocks = flatten_slots(left_root)[targets].astype(jnp.float32)
    rroot_blocks = flatten_slots(right_root)[targets].astype(jnp.float32)
    left_gram = jnp.einsum('bik,bjk->bij', grad_wide, grad_wide)
    right_gram = jnp.einsum('bki,bkj->bij', grad_wide, grad_wide)
    left_blocks = STAT_DECAY * left_old + (1.0 - STAT_DECAY) * left_gram / S
    right_blocks = STAT_DECAY * right_old + (1.0 - STAT_DECAY) * right_gram / S
    acc_blocks = acc_old + grad_sum * grad_sum
    grafted = grad_sum / (jnp.sqrt(acc_blocks) + GRAFT_EPS)
    half_prod = jnp.einsum('bik,bjk->bij', grad_wide, rroot_blocks)
    half_round = lax.optimization_barrier(half_prod.astype(jnp.bfloat16))
    raw_dir = jnp.einsum('bik,bkj->bij', lroot_blocks, half_round.astype(jnp.float32))
    raw_dir = jnp.where(row_mask, raw_dir, jnp.float32(0.0))
    factor = jnp.sqrt(lax.optimization_barrier(jnp.sum(grafted * grafted, axis=(1, 2)))) / jnp.sqrt(lax.optimization_barrier(jnp.sum(raw_dir * raw_dir, axis=(1, 2))) + GRAFT_EPS)
    dir_blocks = (factor[:, None, None] * raw_dir).astype(jnp.bfloat16)
    full_shape = (N_DP, SLOTS, S, S)
    left_new = flatten_slots(left_stat).at[targets].set(left_blocks).reshape(full_shape)
    right_new = flatten_slots(right_stat).at[targets].set(right_blocks).reshape(full_shape)
    acc_new = flatten_slots(grad_acc).at[targets].set(acc_blocks).reshape(full_shape)
    directions = jnp.zeros((flat_count, S, S), jnp.bfloat16).at[targets].set(dir_blocks).reshape(full_shape)
    return (left_new, right_new, acc_new, directions)
```

```python
import jax
import jax.numpy as jnp
from jax import lax
from jax.experimental import pallas as pl
from jax.experimental.pallas import tpu as pltpu
from jax.sharding import Mesh, PartitionSpec as P

STAT_DECAY = 0.9
GRAFT_EPS = 1e-06
HALF = jnp.bfloat16
WIDE = jnp.float32
NZ, NX, NC = 16, 4, 2
PARAMS = pltpu.CompilerParams(vmem_limit_bytes=24 * 1024 * 1024)


def slot_targets(owners, slot_count):
    block_count = owners.shape[0]
    same_owner = owners[:, None] == owners[None, :]
    earlier = lax.broadcasted_iota(jnp.int32, (block_count, block_count), 1) < lax.broadcasted_iota(
        jnp.int32, (block_count, block_count), 0
    )
    ranked = jnp.sum(jnp.where(same_owner & earlier, 1, 0), axis=1).astype(jnp.int32)
    return owners * slot_count + ranked


def ring(count, step):
    return [(i, (i + step) % count) for i in range(count)]


def iota(shape, dim):
    return lax.broadcasted_iota(jnp.int32, shape, dim)


def dot(a, b, dims=((1,), (0,))):
    return lax.dot_general(a, b, (dims, ((), ())), preferred_element_type=WIDE)


def order_rows(activations, place):
    block_rows, rows, toks = activations.shape
    part = block_rows // 2
    count = part * rows
    per_z = rows // NZ

    def kernel(place_ref, a_ref, o_ref):
        z, c = place_ref[0], place_ref[1]
        m, k = iota((count, count), 0), iota((count, count), 1)
        block = m % part
        row = (m // part) % per_z
        tail = m // (part * per_z)
        dist = 4 * (tail % 4) + 2 * ((tail // 4) % 2) + tail // 8
        for half in range(2):
            goal = jnp.bitwise_and(z + dist if half == 0 else z - dist, NZ - 1)
            pick = (block * rows + goal * per_z + row == k).astype(WIDE).astype(HALF)
            values = a_ref[half * part : (half + 1) * part].reshape(count, toks)
            moved = dot(pick, values).astype(HALF)
            turned = jnp.concatenate([moved[:, toks // 2 :], moved[:, : toks // 2]], axis=1)
            o_ref[half * count : (half + 1) * count, :] = jnp.where(c == 1, turned, moved)

    return pl.pallas_call(
        kernel,
        out_shape=jax.ShapeDtypeStruct((2 * count, toks), HALF),
        in_specs=[pl.BlockSpec(memory_space=pltpu.SMEM), pl.BlockSpec(memory_space=pltpu.VMEM)],
        out_specs=pl.BlockSpec(memory_space=pltpu.VMEM),
        compiler_params=PARAMS,
    )(place, activations)


def split_columns(out_grads, core):
    toks, columns = out_grads.shape
    half, width = toks // NC, columns // NX

    def kernel(core_ref, b_ref, o_ref):
        o_ref[0] = b_ref[...]

    return pl.pallas_call(
        kernel,
        out_shape=jax.ShapeDtypeStruct((NX, half, width), HALF),
        grid_spec=pltpu.PrefetchScalarGridSpec(
            num_scalar_prefetch=1,
            grid=(NX,),
            in_specs=[pl.BlockSpec((half, width), lambda i, core_ref: (core_ref[0], i))],
            out_specs=pl.BlockSpec((1, half, width), lambda i, core_ref: (i, 0, 0)),
        ),
        compiler_params=PARAMS,
    )(core, out_grads)


def partial_products(acts, mine, other):
    sources, rows, toks = acts.shape
    half, width = mine.shape[1:]
    tile = width // 6
    part = rows // 4

    def kernel(a_ref, m_ref, o_ref, ka_ref, sa_ref, kb_ref, sb_ref):
        total = None
        for s in range(sources):
            both = jnp.concatenate([m_ref[s], o_ref[s]], axis=0)
            term = dot(a_ref[s], both)
            total = term if total is None else total + term
        ka_ref[...] = total[:part]
        sa_ref[...] = total[part : 2 * part].astype(HALF)
        kb_ref[...] = total[2 * part : 3 * part]
        sb_ref[...] = total[3 * part :].astype(HALF)

    out_block = pl.BlockSpec((part, tile), lambda n: (0, n))
    return pl.pallas_call(
        kernel,
        grid=(6,),
        out_shape=[
            jax.ShapeDtypeStruct((part, width), WIDE),
            jax.ShapeDtypeStruct((part, width), HALF),
        ]
        * 2,
        in_specs=[
            pl.BlockSpec((sources, rows, toks), lambda n: (0, 0, 0)),
            pl.BlockSpec((sources, half, tile), lambda n: (0, 0, n)),
            pl.BlockSpec((sources, half, tile), lambda n: (0, 0, n)),
        ],
        out_specs=[out_block] * 4,
        compiler_params=PARAMS,
    )(acts, mine, other)


def pick_blocks(chosen, sums, block_size):
    sources, rows, width = sums.shape
    columns = width // block_size
    out_rows = chosen.shape[0]
    tile = out_rows // 2

    def kernel(p_ref, s_ref, o_ref):
        total = None
        for x in range(sources):
            for j in range(columns):
                at = (x * columns + j) * rows
                term = dot(p_ref[:, at : at + rows], s_ref[x, :, j * block_size : (j + 1) * block_size])
                total = term if total is None else total + term
        o_ref[...] = total.astype(HALF)

    return pl.pallas_call(
        kernel,
        grid=(2,),
        out_shape=jax.ShapeDtypeStruct((out_rows, block_size), HALF),
        in_specs=[
            pl.BlockSpec((tile, chosen.shape[1]), lambda n: (n, 0)),
            pl.BlockSpec(sums.shape, lambda n: (0, 0, 0)),
        ],
        out_specs=pl.BlockSpec((tile, block_size), lambda n: (n, 0)),
        compiler_params=PARAMS,
    )(chosen, sums)


def finish_sum(limits, pieces, acc):
    slots, rows, block_size = acc.shape
    per_z = rows // NZ
    total_rows = slots * rows
    piece_rows = pieces.shape[0]

    def kernel(lim_ref, p_ref, a_ref, g_ref, n_ref):
        m, k = iota((total_rows, piece_rows), 0), iota((total_rows, piece_rows), 1)
        row = k % per_z
        piece = (k // per_z) % 4
        slot = (k // (4 * per_z)) % slots
        source = k // (4 * per_z * slots)
        goal = jnp.bitwise_and(source + 4 * piece, NZ - 1)
        adds = (slot * rows + goal * per_z + row == m).astype(WIDE).astype(HALF)
        grad = dot(adds, p_ref[...])
        lane = iota((16, block_size), 1)
        extra_row = iota((16, block_size), 0)
        extra = jnp.zeros((16, block_size), WIDE)
        for s in range(slots):
            live = iota((rows, block_size), 0) < lim_ref[s]
            own = jnp.where(live, grad[s * rows : (s + 1) * rows], 0.0)
            new = a_ref[s] + own * own
            n_ref[s] = new
            grafted = own / (jnp.sqrt(new) + GRAFT_EPS)
            norm = jnp.sum(jnp.sum(grafted * grafted, axis=0, keepdims=True), axis=1, keepdims=True)
            high = norm.astype(HALF).astype(WIDE)
            middle = (norm - high).astype(HALF).astype(WIDE)
            low = norm - high - middle
            spread = jnp.where(lane == 0, high, jnp.where(lane == 1, middle, jnp.where(lane == 2, low, 0.0)))
            extra = jnp.where(extra_row == s, spread, extra)
            g_ref[s * rows : (s + 1) * rows, :] = own.astype(HALF)
        g_ref[total_rows:, :] = extra.astype(HALF)

    vmem = pl.BlockSpec(memory_space=pltpu.VMEM)
    return pl.pallas_call(
        kernel,
        out_shape=[
            jax.ShapeDtypeStruct((total_rows + 16, block_size), HALF),
            jax.ShapeDtypeStruct(acc.shape, WIDE),
        ],
        in_specs=[pl.BlockSpec(memory_space=pltpu.SMEM), vmem, vmem],
        out_specs=[vmem, vmem],
        compiler_params=PARAMS,
    )(limits, pieces, acc)


def update(facts, mine, other, left_root, right_root, left_stat, right_stat):
    ny = mine.shape[0]
    slots, rows, block_size = left_stat.shape
    all_rows = mine.shape[1]

    def kernel(f_ref, m_ref, o_ref, lr_ref, rr_ref, ls_ref, rs_ref, ln_ref, rn_ref, d_ref):
        s = pl.program_id(0)
        core, own_y, own_mp = f_ref[0], f_ref[1], f_ref[2]
        live, taken = f_ref[3 + s], f_ref[5 + s]
        at = pl.ds(pl.multiple_of(s * rows, rows), rows)
        parts = []
        norm = jnp.zeros((1, 1), WIDE)
        tail_row = iota((16, block_size), 0) == s
        for y in range(ny):
            a, b = m_ref[y, at, :], o_ref[y, at, :]
            parts += [jnp.where(core == 0, a, b), jnp.where(core == 0, b, a)]
            for ref in (m_ref, o_ref):
                tail = jnp.where(tail_row, ref[y, slots * rows : all_rows, :].astype(WIDE), 0.0)
                norm += jnp.sum(jnp.sum(tail, axis=0, keepdims=True), axis=1, keepdims=True)
        grad = jnp.concatenate(parts, axis=0)
        prod = dot(grad, rr_ref[0], ((1,), (1,))).astype(HALF)
        raw = dot(lr_ref[0], prod)
        raw = jnp.where(iota(raw.shape, 0) < live, raw, 0.0)
        raw_sq = jnp.sum(jnp.sum(raw * raw, axis=0, keepdims=True), axis=1, keepdims=True)
        factor = jnp.sqrt(norm) / jnp.sqrt(raw_sq + GRAFT_EPS)
        d_ref[0] = jnp.where(taken == 1, factor * raw, 0.0).astype(HALF)
        own = m_ref[own_y, at, :]
        left_cols = dot(own, grad, ((1,), (1,)))
        own_columns = (iota((block_size, rows), 0) == own_mp * rows + iota((block_size, rows), 1)).astype(WIDE)
        columns = dot(grad, own_columns.astype(HALF)).astype(HALF)
        right_rows = dot(columns, grad, ((0,), (0,)))
        for old_ref, value, new_ref in ((ls_ref, left_cols, ln_ref), (rs_ref, right_rows, rn_ref)):
            old = old_ref[0]
            fresh = STAT_DECAY * old + (1.0 - STAT_DECAY) * value / block_size
            new_ref[0] = jnp.where(taken == 1, fresh, old)

    whole = pl.BlockSpec((ny, all_rows, block_size), lambda s: (0, 0, 0))
    square = pl.BlockSpec((1, block_size, block_size), lambda s: (s, 0, 0))
    strip = pl.BlockSpec((1, rows, block_size), lambda s: (s, 0, 0))
    return pl.pallas_call(
        kernel,
        grid=(slots,),
        out_shape=[
            jax.ShapeDtypeStruct(left_stat.shape, WIDE),
            jax.ShapeDtypeStruct(right_stat.shape, WIDE),
            jax.ShapeDtypeStruct(left_root.shape, HALF),
        ],
        in_specs=[
            pl.BlockSpec(memory_space=pltpu.SMEM),
            whole,
            whole,
            square,
            square,
            strip,
            strip,
        ],
        out_specs=[strip, strip, square],
        compiler_params=PARAMS,
    )(facts, mine, other, left_root, right_root, left_stat, right_stat)


def body(
    activations,
    out_grads,
    owners,
    live_rows,
    left_stat,
    right_stat,
    left_root,
    right_root,
    grad_acc,
):
    z, x, y, c = (lax.axis_index(name) for name in ("z", "x", "y", "c"))
    block_rows, rows, toks = activations.shape
    block_size = left_stat.shape[3]
    slots = left_stat.shape[1]
    block_count = owners.shape[0]
    per_z = rows // NZ
    columns = out_grads.shape[1] // block_size // NX
    half_rows = block_rows // 2
    my_owner = z * NX + x
    my_mp = y * NC + c
    my_rows = my_mp * rows

    left_full = lax.all_gather(left_root[0], ("y", "c"), axis=1, tiled=True)
    right_full = lax.all_gather(right_root[0], ("y", "c"), axis=1, tiled=True)

    pieces = split_columns(out_grads, c.reshape(1).astype(jnp.int32))
    mine = lax.all_to_all(pieces, "x", 0, 0, tiled=True)
    other = lax.ppermute(mine, "c", ring(NC, 1))
    acts = order_rows(activations, jnp.stack([z, c]).astype(jnp.int32))
    acts, mine = lax.optimization_barrier((acts, mine))
    acts = lax.all_gather(acts, "x", axis=0, tiled=False)
    keep_a, send_a, keep_b, send_b = partial_products(acts, mine, other)

    for step in (1, 2):
        got_a = lax.ppermute(send_a, "z", ring(NZ, step))
        got_b = lax.ppermute(send_b, "z", ring(NZ, -step))
        keep_a, keep_b = keep_a + got_a, keep_b + got_b
        if step == 1:
            part = keep_a.shape[0] // 2
            send_a, send_b = keep_a[part:].astype(HALF), keep_b[part:].astype(HALF)
            keep_a, keep_b = keep_a[:part], keep_b[:part]
    sums = jnp.concatenate([keep_a, keep_b], axis=0).astype(HALF)
    sums = lax.all_gather(sums, "x", axis=0, tiled=False)

    targets = slot_targets(owners, slots)
    by_block = targets.reshape(2, half_rows, NX, columns).transpose(2, 3, 0, 1)[:, :, :, None, None, :]
    shape = (NX, columns, 2, 4, per_z, half_rows)
    owner = by_block // slots
    piece = iota(shape, 3)
    piece = jnp.where(iota(shape, 2) == 0, piece, (4 - piece) % 4)
    code = (((owner // NX) * slots + by_block % slots) * 4 + piece) * per_z + iota(shape, 4)
    code = jnp.where(owner % NX == x, code, -1).reshape(1, -1)
    out_rows = NZ * slots * 4 * per_z
    chosen = (code == iota((out_rows, 1), 0)).astype(HALF)

    picked = pick_blocks(chosen, sums, block_size).reshape(NZ, out_rows // NZ, block_size)
    arrived = lax.all_to_all(picked, "z", 0, 0, tiled=True).reshape(out_rows, block_size)

    wanted = my_owner * slots + iota((slots, block_count), 0)
    matched = targets[None, :] == wanted
    occupied = jnp.any(matched, axis=1).astype(jnp.int32)
    live_mine = jnp.sum(jnp.where(matched, live_rows[None, :], 0), axis=1).astype(jnp.int32)
    own_rows, acc_next = finish_sum(live_mine - my_rows, arrived, grad_acc[0])
    rows_mine = lax.all_gather(own_rows, "y", axis=0, tiled=False)
    rows_other = lax.ppermute(rows_mine, "c", ring(NC, 1))
    facts = jnp.concatenate([jnp.stack([c, y, my_mp]).astype(jnp.int32), live_mine, occupied])
    left_next, right_next, directions = update(
        facts, rows_mine, rows_other, left_full, right_full, left_stat[0], right_stat[0]
    )
    return (left_next[None], right_next[None], acc_next[None], directions[None])


def solution(mesh):
    dp, mp = mesh.devices.shape
    parts = Mesh(mesh.devices.reshape(NZ, NX, mp // NC, NC), ("z", "x", "y", "c"))
    owner, strip = ("z", "x"), ("y", "c")
    state = P(owner, None, strip, None)
    return jax.shard_map(
        body,
        mesh=parts,
        in_specs=(P(None, strip, owner), P(owner, None), P(), P(), state, state, state, state, state),
        out_specs=(state, state, state, P(owner, None, None, None)),
        check_vma=False,
    )
```

```python
import jax
import jax.numpy as jnp
from jax import lax
from jax.experimental import pallas as pl
from jax.experimental.pallas import tpu as pltpu
from jax.sharding import Mesh, PartitionSpec as P

STAT_DECAY = 0.9
GRAFT_EPS = 1e-06
HALF = jnp.bfloat16
WIDE = jnp.float32
NZ, NX, NC = 16, 4, 2
TILES = 6
Y_STEPS = (0, 1, 3, 2)
PARAMS = pltpu.CompilerParams(vmem_limit_bytes=16 * 1024 * 1024)


def slot_targets(owners, slot_count):
    block_count = owners.shape[0]
    same_owner = owners[:, None] == owners[None, :]
    earlier = lax.broadcasted_iota(jnp.int32, (block_count, block_count), 1) < lax.broadcasted_iota(
        jnp.int32, (block_count, block_count), 0
    )
    ranked = jnp.sum(jnp.where(same_owner & earlier, 1, 0), axis=1).astype(jnp.int32)
    return owners * slot_count + ranked


def ring(count, step):
    return [(i, (i + step) % count) for i in range(count)]


def iota(shape, dim):
    return lax.broadcasted_iota(jnp.int32, shape, dim)


def dot(a, b, dims=((1,), (0,))):
    return lax.dot_general(a, b, (dims, ((), ())), preferred_element_type=WIDE)


def prepare(activations, out_grads, place):
    block_rows, rows, toks = activations.shape
    part = block_rows // 2
    per_z = rows // NZ
    count = part * rows
    small = count // 2
    half = toks // NC
    width = out_grads.shape[1] // NX
    tile = width // TILES

    def kernel(place_ref, a_ref, b_ref, after_ref, before_ref, across_ref, acts, sems, row_sems):
        z, x, c = place_ref[0], place_ref[1], place_ref[2]
        targets = ((after_ref, 1), (before_ref, 3), (across_ref, 2))
        tok = pl.ds(pl.multiple_of(c * half, half), half)
        copies = []
        for i, (ref, step) in enumerate(targets):
            begin = jnp.bitwise_and(x + step, NX - 1) * width
            for n in range(TILES):
                at = pl.ds(pl.multiple_of(begin + n * tile, tile), tile)
                to = pl.ds(2 * count + n * half, half)
                copies.append(pltpu.make_async_copy(b_ref.at[tok, at], ref.at[to, :], sems.at[i, n]))
        for copy in copies:
            copy.start()
        m, k = iota((small, count), 0), iota((small, count), 1)
        block = m % part
        row = (m // part) % per_z
        tail = m // (part * per_z)
        high = 2 * (tail // 4) + 4 * ((tail // 2) % 2) + 8 * (tail % 2)
        for side in range(2):
            values = a_ref[side * part : (side + 1) * part].reshape(count, toks)
            for odd in range(2):
                dist = high + odd
                goal = jnp.bitwise_and(z + dist if side == 0 else z - dist, NZ - 1)
                pick = (block * rows + goal * per_z + row == k).astype(WIDE).astype(HALF)
                moved = dot(pick, values).astype(HALF)
                turned = jnp.concatenate([moved[:, half:], moved[:, :half]], axis=1)
                at = (1 - odd) * count + side * small
                acts[at : at + small, :] = jnp.where(c == 1, turned, moved)
        last = [
            pltpu.make_async_copy(acts, ref.at[pl.ds(0, 2 * count), :], row_sems.at[i])
            for i, (ref, _) in enumerate(targets)
        ]
        for copy in last:
            copy.start()
        for copy in copies + last:
            copy.wait()

    any_place = pl.BlockSpec(memory_space=pl.ANY)
    return pl.pallas_call(
        kernel,
        out_shape=[jax.ShapeDtypeStruct((2 * count + TILES * half, toks), HALF)] * 3,
        in_specs=[
            pl.BlockSpec(memory_space=pltpu.SMEM),
            pl.BlockSpec(memory_space=pltpu.VMEM),
            any_place,
        ],
        out_specs=[any_place] * 3,
        scratch_shapes=[
            pltpu.VMEM((2 * count, toks), HALF),
            pltpu.SemaphoreType.DMA((3, TILES)),
            pltpu.SemaphoreType.DMA((3,)),
        ],
        compiler_params=pltpu.CompilerParams(vmem_limit_bytes=60 * 1024 * 1024),
    )(place, activations, out_grads)


def partial_products(place, own, out_grads, arrived, swapped, odd):
    toks, tile = out_grads.shape[0], own.shape[1]
    half = toks // NC
    total_rows = own.shape[0] - TILES * half
    count = total_rows // 2
    kind = HALF if odd else WIDE

    def kernel(place_ref, *refs):
        rows_refs, mine, other, (one_ref, two_ref) = refs[:4], refs[4:8], refs[8:12], refs[12:]
        total = None
        for i in range(NX):
            term = dot(rows_refs[i][...], jnp.concatenate([mine[i][...], other[i][...]], axis=0))
            total = term if total is None else total + term
        one_ref[...] = total[: count // 2].astype(kind)
        two_ref[...] = total[count // 2 :].astype(kind)

    rows = pl.BlockSpec((count, tile), lambda n, place_ref: (0 if odd else 1, 0))
    columns = pl.BlockSpec((half, tile), lambda n, place_ref: (total_rows // half + n, 0))
    own_half = pl.BlockSpec((half, tile), lambda n, place_ref: (place_ref[2], place_ref[1] * TILES + n))
    other_half = pl.BlockSpec((half, tile), lambda n, place_ref: (1 - place_ref[2], place_ref[1] * TILES + n))
    return pl.pallas_call(
        kernel,
        out_shape=[jax.ShapeDtypeStruct((count // 2, TILES * tile), kind)] * 2,
        grid_spec=pltpu.PrefetchScalarGridSpec(
            num_scalar_prefetch=1,
            grid=(TILES,),
            in_specs=[rows] * 4 + [own_half] + [columns] * 3 + [other_half] + [columns] * 3,
            out_specs=[pl.BlockSpec((count // 2, tile), lambda n, place_ref: (0, n))] * 2,
        ),
        compiler_params=PARAMS,
    )(place, own, *arrived, out_grads, *arrived, out_grads, *swapped)


def pick_blocks(chosen, sums, block_size):
    sources, rows, width = sums.shape
    columns = width // block_size
    out_rows = chosen.shape[0]
    tile = out_rows // 2

    def kernel(p_ref, s_ref, o_ref):
        total = None
        for pair in range(sources // 2):
            depth = 2 * columns * rows
            pieces = [
                s_ref[x, :, j * block_size : (j + 1) * block_size]
                for x in (2 * pair, 2 * pair + 1)
                for j in range(columns)
            ]
            term = dot(p_ref[:, pair * depth : (pair + 1) * depth], jnp.concatenate(pieces, axis=0))
            total = term if total is None else total + term
        o_ref[...] = total.astype(HALF)

    return pl.pallas_call(
        kernel,
        grid=(2,),
        out_shape=jax.ShapeDtypeStruct((out_rows, block_size), HALF),
        in_specs=[
            pl.BlockSpec((tile, chosen.shape[1]), lambda n: (n, 0)),
            pl.BlockSpec(sums.shape, lambda n: (0, 0, 0)),
        ],
        out_specs=pl.BlockSpec((tile, block_size), lambda n: (n, 0)),
        compiler_params=PARAMS,
    )(chosen, sums)


def finish_sum(limits, pieces, acc):
    slots, rows, block_size = acc.shape
    per_z = rows // NZ
    total_rows = slots * rows
    piece_rows = pieces.shape[0]

    def kernel(lim_ref, p_ref, a_ref, g_ref, n_ref):
        m, k = iota((total_rows, piece_rows), 0), iota((total_rows, piece_rows), 1)
        row = k % per_z
        piece = (k // per_z) % 2
        slot = (k // (2 * per_z)) % slots
        source = k // (2 * per_z * slots)
        goal = jnp.bitwise_and(source + 8 * piece, NZ - 1)
        adds = (slot * rows + goal * per_z + row == m).astype(WIDE).astype(HALF)
        grad = dot(adds, p_ref[...])
        lane = iota((16, block_size), 1)
        extra_row = iota((16, block_size), 0)
        extra = jnp.zeros((16, block_size), WIDE)
        for s in range(slots):
            live = iota((rows, block_size), 0) < lim_ref[s]
            own = jnp.where(live, grad[s * rows : (s + 1) * rows], 0.0)
            new = a_ref[s] + own * own
            n_ref[s] = new
            grafted = own / (jnp.sqrt(new) + GRAFT_EPS)
            norm = jnp.sum(jnp.sum(grafted * grafted, axis=0, keepdims=True), axis=1, keepdims=True)
            high = norm.astype(HALF).astype(WIDE)
            middle = (norm - high).astype(HALF).astype(WIDE)
            low = norm - high - middle
            spread = jnp.where(lane == 0, high, jnp.where(lane == 1, middle, jnp.where(lane == 2, low, 0.0)))
            extra = jnp.where(extra_row == s, spread, extra)
            g_ref[s * rows : (s + 1) * rows, :] = own.astype(HALF)
        g_ref[total_rows:, :] = extra.astype(HALF)

    vmem = pl.BlockSpec(memory_space=pltpu.VMEM)
    return pl.pallas_call(
        kernel,
        out_shape=[
            jax.ShapeDtypeStruct((total_rows + 16, block_size), HALF),
            jax.ShapeDtypeStruct(acc.shape, WIDE),
        ],
        in_specs=[pl.BlockSpec(memory_space=pltpu.SMEM), vmem, vmem],
        out_specs=[vmem, vmem],
        compiler_params=PARAMS,
    )(limits, pieces, acc)


def update(facts, mine, other, roots_mine, roots_other, left_stat, right_stat):
    ny = mine.shape[0]
    slots, rows, block_size = left_stat.shape
    all_rows = mine.shape[1]

    def kernel(f_ref, m_ref, o_ref, *refs):
        root_refs, (t_ref, ls_ref, rs_ref, ln_ref, rn_ref, d_ref, roots) = refs[:ny], refs[ny:]
        s = pl.program_id(0)
        core, own_y, own_mp = f_ref[0], f_ref[1], f_ref[2]
        live, taken = f_ref[3 + s], f_ref[5 + s]
        at = pl.ds(pl.multiple_of(s * rows, rows), rows)
        for i, step in enumerate(Y_STEPS[:ny]):
            source = lax.rem(own_y + step, ny) * NC
            for ref, who in ((root_refs[i], core), (t_ref.at[i], 1 - core)):
                to = pl.ds(pl.multiple_of((source + who) * rows, rows), rows)
                for kind in range(2):
                    roots[kind, to, :] = ref[kind, 0]
        parts = []
        norm = jnp.zeros((1, 1), WIDE)
        tail_row = iota((16, block_size), 0) == s
        for y in range(ny):
            a, b = m_ref[y, at, :], o_ref[y, at, :]
            parts += [jnp.where(core == 0, a, b), jnp.where(core == 0, b, a)]
            for ref in (m_ref, o_ref):
                tail = jnp.where(tail_row, ref[y, slots * rows : all_rows, :].astype(WIDE), 0.0)
                norm += jnp.sum(jnp.sum(tail, axis=0, keepdims=True), axis=1, keepdims=True)
        grad = jnp.concatenate(parts, axis=0)
        prod = dot(grad, roots[1], ((1,), (1,))).astype(HALF)
        raw = dot(roots[0], prod)
        raw = jnp.where(iota(raw.shape, 0) < live, raw, 0.0)
        raw_sq = jnp.sum(jnp.sum(raw * raw, axis=0, keepdims=True), axis=1, keepdims=True)
        factor = jnp.sqrt(norm) / jnp.sqrt(raw_sq + GRAFT_EPS)
        d_ref[0] = jnp.where(taken == 1, factor * raw, 0.0).astype(HALF)
        own = m_ref[own_y, at, :]
        left_cols = dot(own, grad, ((1,), (1,)))
        own_columns = (iota((block_size, rows), 0) == own_mp * rows + iota((block_size, rows), 1)).astype(WIDE)
        columns = dot(grad, own_columns.astype(HALF)).astype(HALF)
        right_rows = dot(columns, grad, ((0,), (0,)))
        for old_ref, value, new_ref in ((ls_ref, left_cols, ln_ref), (rs_ref, right_rows, rn_ref)):
            old = old_ref[0]
            fresh = STAT_DECAY * old + (1.0 - STAT_DECAY) * value / block_size
            new_ref[0] = jnp.where(taken == 1, fresh, old)

    whole = pl.BlockSpec((ny, all_rows, block_size), lambda s: (0, 0, 0))
    square = pl.BlockSpec((1, block_size, block_size), lambda s: (s, 0, 0))
    strip = pl.BlockSpec((1, rows, block_size), lambda s: (s, 0, 0))
    return pl.pallas_call(
        kernel,
        grid=(slots,),
        out_shape=[
            jax.ShapeDtypeStruct(left_stat.shape, WIDE),
            jax.ShapeDtypeStruct(right_stat.shape, WIDE),
            jax.ShapeDtypeStruct((slots, block_size, block_size), HALF),
        ],
        in_specs=[pl.BlockSpec(memory_space=pltpu.SMEM), whole, whole]
        + [pl.BlockSpec((2, 1, rows, block_size), lambda s: (0, s, 0, 0))] * ny
        + [pl.BlockSpec((ny, 2, 1, rows, block_size), lambda s: (0, 0, s, 0, 0)), strip, strip],
        out_specs=[strip, strip, square],
        scratch_shapes=[pltpu.VMEM((2, block_size, block_size), HALF)],
        compiler_params=PARAMS,
    )(facts, mine, other, *roots_mine, roots_other, left_stat, right_stat)


def body(
    activations,
    out_grads,
    owners,
    live_rows,
    left_stat,
    right_stat,
    left_root,
    right_root,
    grad_acc,
):
    z, x, y, c = (lax.axis_index(name) for name in ("z", "x", "y", "c"))
    block_rows, rows, toks = activations.shape
    block_size = left_stat.shape[3]
    slots = left_stat.shape[1]
    block_count = owners.shape[0]
    per_z = rows // NZ
    columns = out_grads.shape[1] // block_size // NX
    half_rows = block_rows // 2
    my_owner = z * NX + x
    my_mp = y * NC + c
    my_rows = my_mp * rows

    place = jnp.stack([z, x, c]).astype(jnp.int32)
    pieces = prepare(activations, out_grads, place)
    arrived = [lax.ppermute(piece, "x", ring(NX, step)) for piece, step in zip(pieces, (1, -1, 2))]
    swapped = [lax.ppermute(piece, "c", ring(NC, 1)) for piece in arrived]
    send_a, send_b = partial_products(place, pieces[0], out_grads, arrived, swapped, True)
    keep_a, keep_b = partial_products(place, pieces[0], out_grads, arrived, swapped, False)

    for step in (1, 2, 4):
        got_a = lax.ppermute(send_a, "z", ring(NZ, step))
        got_b = lax.ppermute(send_b, "z", ring(NZ, -step))
        keep_a, keep_b = keep_a + got_a, keep_b + got_b
        if step < 4:
            part = keep_a.shape[0] // 2
            send_a, send_b = keep_a[part:].astype(HALF), keep_b[part:].astype(HALF)
            keep_a, keep_b = keep_a[:part], keep_b[:part]
    sums = jnp.concatenate([keep_a, keep_b], axis=0).astype(HALF)
    sums = lax.all_gather(sums, "x", axis=0, tiled=False)

    targets = slot_targets(owners, slots)
    by_block = targets.reshape(2, half_rows, NX, columns).transpose(2, 3, 0, 1)[:, :, :, None, None, :]
    shape = (NX, columns, 2, 2, per_z, half_rows)
    owner = by_block // slots
    code = (((owner // NX) * slots + by_block % slots) * 2 + iota(shape, 3)) * per_z + iota(shape, 4)
    code = jnp.where(owner % NX == x, code, -1).reshape(1, -1)
    out_rows = NZ * slots * 2 * per_z
    chosen = (code == iota((out_rows, 1), 0)).astype(HALF)

    picked = pick_blocks(chosen, sums, block_size).reshape(NZ, out_rows // NZ, block_size)
    picked, left_root, right_root = lax.optimization_barrier((picked, left_root, right_root))
    roots = jnp.concatenate([left_root, right_root], axis=0)
    ny = lax.axis_size("y")
    roots_mine = [roots] + [lax.ppermute(roots, "y", ring(ny, -step)) for step in Y_STEPS[1:ny]]
    roots_other = lax.ppermute(jnp.stack(roots_mine), "c", ring(NC, 1))
    arrived = lax.all_to_all(picked, "z", 0, 0, tiled=True).reshape(out_rows, block_size)

    wanted = my_owner * slots + iota((slots, block_count), 0)
    matched = targets[None, :] == wanted
    occupied = jnp.any(matched, axis=1).astype(jnp.int32)
    live_mine = jnp.sum(jnp.where(matched, live_rows[None, :], 0), axis=1).astype(jnp.int32)
    own_rows, acc_next = finish_sum(live_mine - my_rows, arrived, grad_acc[0])
    rows_mine = lax.all_gather(own_rows, "y", axis=0, tiled=False)
    rows_other = lax.ppermute(rows_mine, "c", ring(NC, 1))
    facts = jnp.concatenate([jnp.stack([c, y, my_mp]).astype(jnp.int32), live_mine, occupied])
    left_next, right_next, directions = update(
        facts, rows_mine, rows_other, roots_mine, roots_other, left_stat[0], right_stat[0]
    )
    return (left_next[None], right_next[None], acc_next[None], directions[None])


def solution(mesh):
    dp, mp = mesh.devices.shape
    parts = Mesh(mesh.devices.reshape(NZ, NX, mp // NC, NC), ("z", "x", "y", "c"))
    owner, strip = ("z", "x"), ("y", "c")
    state = P(owner, None, strip, None)
    return jax.shard_map(
        body,
        mesh=parts,
        in_specs=(P(None, strip, owner), P(owner, None), P(), P(), state, state, state, state, state),
        out_specs=(state, state, state, P(owner, None, None, None)),
        check_vma=False,
    )
```

```python
import jax
import jax.numpy as jnp
from jax import lax
from jax.experimental import pallas as pl
from jax.experimental.pallas import tpu as pltpu
from jax.sharding import Mesh, PartitionSpec as P

STAT_DECAY = 0.9
GRAFT_EPS = 1e-06
HALF = jnp.bfloat16
WIDE = jnp.float32
NZ, NX, NC = 16, 4, 2
TILES = 6
PREP_LIMIT = 60
Y_STEPS = (0, 1, 3, 2)
PARAMS = pltpu.CompilerParams(vmem_limit_bytes=8 * 1024 * 1024)


def slot_targets(owners, slot_count):
    block_count = owners.shape[0]
    same_owner = owners[:, None] == owners[None, :]
    earlier = lax.broadcasted_iota(jnp.int32, (block_count, block_count), 1) < lax.broadcasted_iota(
        jnp.int32, (block_count, block_count), 0
    )
    ranked = jnp.sum(jnp.where(same_owner & earlier, 1, 0), axis=1).astype(jnp.int32)
    return owners * slot_count + ranked


def ring(count, step):
    return [(i, (i + step) % count) for i in range(count)]


def iota(shape, dim):
    return lax.broadcasted_iota(jnp.int32, shape, dim)


def dot(a, b, dims=((1,), (0,))):
    return lax.dot_general(a, b, (dims, ((), ())), preferred_element_type=WIDE)


def prepare(activations, out_grads, place):
    block_rows, rows, toks = activations.shape
    part = block_rows // 2
    per_z = rows // NZ
    count = part * rows
    small = count // 2
    half = toks // NC
    width = out_grads.shape[1] // NX
    tile = width // TILES

    def kernel(place_ref, a_ref, b_ref, own_b_ref, *out_refs):
        z, c, step = place_ref[0], place_ref[2], pl.program_id(0)
        own_ref = out_refs[-1]

        @pl.when(step == 0)
        def _():
            m, k = iota((small, count), 0), iota((small, count), 1)
            block = m % part
            row = (m // part) % per_z
            tail = m // (part * per_z)
            high = 2 * (tail // 4) + 4 * ((tail // 2) % 2) + 8 * (tail % 2)
            for side in range(2):
                values = a_ref[side * part : (side + 1) * part].reshape(count, toks)
                for odd in range(2):
                    dist = high + odd
                    goal = jnp.bitwise_and(z + dist if side == 0 else z - dist, NZ - 1)
                    pick = (block * rows + goal * per_z + row == k).astype(WIDE).astype(HALF)
                    moved = dot(pick, values).astype(HALF)
                    turned = jnp.concatenate([moved[:, half:], moved[:, :half]], axis=1)
                    at = (1 - odd) * count + side * small
                    for ref in out_refs:
                        ref[at : at + small, :] = jnp.where(c == 1, turned, moved)

            for n in range(TILES):
                for side, who in enumerate((c, 1 - c)):
                    at = 2 * count + (2 * n + side) * half
                    tok = pl.ds(pl.multiple_of(who * half, half), half)
                    own_ref[at : at + half, :] = own_b_ref[tok, n * tile : (n + 1) * tile]

        for i, ref in enumerate(out_refs[:3]):

            @pl.when(step == i)
            def _():
                for n in range(TILES):
                    at = 2 * count + n * half
                    ref[at : at + half, :] = b_ref[:, n * tile : (n + 1) * tile]

    piece = (2 * count + TILES * half, toks)
    own = (2 * count + TILES * toks, toks)
    return pl.pallas_call(
        kernel,
        out_shape=[jax.ShapeDtypeStruct(shape, HALF) for shape in (piece, piece, piece, own)],
        grid_spec=pltpu.PrefetchScalarGridSpec(
            num_scalar_prefetch=1,
            grid=(3,),
            in_specs=[
                pl.BlockSpec(activations.shape, lambda i, place_ref: (0, 0, 0)),
                pl.BlockSpec((half, width), lambda i, place_ref: (place_ref[2], place_ref[3 + i])),
                pl.BlockSpec((toks, width), lambda i, place_ref: (0, place_ref[1])),
            ],
            out_specs=[pl.BlockSpec(piece, lambda i, place_ref: (0, 0))] * 3
            + [pl.BlockSpec(own, lambda i, place_ref: (0, 0))],
        ),
        compiler_params=pltpu.CompilerParams(vmem_limit_bytes=PREP_LIMIT * 1024 * 1024),
    )(place, activations, out_grads, out_grads)


def partial_products(own, arrived, swapped, odd):
    toks = own.shape[1]
    half = toks // NC
    total_rows = own.shape[0] - TILES * toks
    count = total_rows // 2
    kind = HALF if odd else WIDE
    group = 2

    def kernel(*refs):
        rows_refs, own_ref, mine, other, (one_ref, two_ref) = refs[:4], refs[4], refs[5:8], refs[8:11], refs[11:]
        for n in range(group):
            at = slice(n * half, (n + 1) * half)
            total = dot(rows_refs[0][...], own_ref[n * toks : (n + 1) * toks, :])
            for rows_ref, m_ref, o_ref in zip(rows_refs[1:], mine, other):
                total += dot(rows_ref[...], jnp.concatenate([m_ref[at, :], o_ref[at, :]], axis=0))
            to = slice(n * toks, (n + 1) * toks)
            one_ref[:, to] = total[: count // 2].astype(kind)
            two_ref[:, to] = total[count // 2 :].astype(kind)

    rows = pl.BlockSpec((count, toks), lambda n: (0 if odd else 1, 0))
    columns = pl.BlockSpec((group * half, toks), lambda n: (total_rows // (group * half) + n, 0))
    own_columns = pl.BlockSpec((group * toks, toks), lambda n: (total_rows // (group * toks) + n, 0))
    return pl.pallas_call(
        kernel,
        grid=(TILES // group,),
        out_shape=[jax.ShapeDtypeStruct((count // 2, TILES * toks), kind)] * 2,
        in_specs=[rows] * 4 + [own_columns] + [columns] * 6,
        out_specs=[pl.BlockSpec((count // 2, group * toks), lambda n: (0, n))] * 2,
        compiler_params=PARAMS,
    )(own, *arrived, own, *arrived, *swapped)


def pick_blocks(chosen, sums, block_size):
    sources, rows, width = sums.shape
    columns = width // block_size
    out_rows = chosen.shape[0]
    tile = out_rows // 2

    def kernel(p_ref, s_ref, o_ref):
        total = None
        for pair in range(sources // 2):
            depth = 2 * columns * rows
            pieces = [
                s_ref[x, :, j * block_size : (j + 1) * block_size]
                for x in (2 * pair, 2 * pair + 1)
                for j in range(columns)
            ]
            term = dot(p_ref[:, pair * depth : (pair + 1) * depth], jnp.concatenate(pieces, axis=0))
            total = term if total is None else total + term
        o_ref[...] = total.astype(HALF)

    return pl.pallas_call(
        kernel,
        grid=(2,),
        out_shape=jax.ShapeDtypeStruct((out_rows, block_size), HALF),
        in_specs=[
            pl.BlockSpec((tile, chosen.shape[1]), lambda n: (n, 0)),
            pl.BlockSpec(sums.shape, lambda n: (0, 0, 0)),
        ],
        out_specs=pl.BlockSpec((tile, block_size), lambda n: (n, 0)),
        compiler_params=PARAMS,
    )(chosen, sums)


def finish_sum(limits, pieces, acc):
    slots, rows, block_size = acc.shape
    per_z = rows // NZ
    total_rows = slots * rows
    piece_rows = pieces.shape[0]

    def kernel(lim_ref, p_ref, a_ref, g_ref, n_ref):
        m, k = iota((total_rows, piece_rows), 0), iota((total_rows, piece_rows), 1)
        row = k % per_z
        piece = (k // per_z) % 2
        slot = (k // (2 * per_z)) % slots
        source = k // (2 * per_z * slots)
        goal = jnp.bitwise_and(source + 8 * piece, NZ - 1)
        adds = (slot * rows + goal * per_z + row == m).astype(WIDE).astype(HALF)
        grad = dot(adds, p_ref[...])
        lane = iota((16, block_size), 1)
        extra_row = iota((16, block_size), 0)
        extra = jnp.zeros((16, block_size), WIDE)
        for s in range(slots):
            live = iota((rows, block_size), 0) < lim_ref[s]
            own = jnp.where(live, grad[s * rows : (s + 1) * rows], 0.0)
            new = a_ref[s] + own * own
            n_ref[s] = new
            grafted = own / (jnp.sqrt(new) + GRAFT_EPS)
            norm = jnp.sum(jnp.sum(grafted * grafted, axis=0, keepdims=True), axis=1, keepdims=True)
            high = norm.astype(HALF).astype(WIDE)
            middle = (norm - high).astype(HALF).astype(WIDE)
            low = norm - high - middle
            spread = jnp.where(lane == 0, high, jnp.where(lane == 1, middle, jnp.where(lane == 2, low, 0.0)))
            extra = jnp.where(extra_row == s, spread, extra)
            g_ref[s * rows : (s + 1) * rows, :] = own.astype(HALF)
        g_ref[total_rows:, :] = extra.astype(HALF)

    vmem = pl.BlockSpec(memory_space=pltpu.VMEM)
    return pl.pallas_call(
        kernel,
        out_shape=[
            jax.ShapeDtypeStruct((total_rows + 16, block_size), HALF),
            jax.ShapeDtypeStruct(acc.shape, WIDE),
        ],
        in_specs=[pl.BlockSpec(memory_space=pltpu.SMEM), vmem, vmem],
        out_specs=[vmem, vmem],
        compiler_params=PARAMS,
    )(limits, pieces, acc)


def update(facts, mine, other, roots_mine, roots_other, left_stat, right_stat):
    ny = mine.shape[0]
    slots, rows, block_size = left_stat.shape
    all_rows = mine.shape[1]

    def kernel(f_ref, m_ref, o_ref, *refs):
        root_refs, (t_ref, ls_ref, rs_ref, ln_ref, rn_ref, d_ref, roots) = refs[:ny], refs[ny:]
        s = pl.program_id(0)
        core, own_y, own_mp = f_ref[0], f_ref[1], f_ref[2]
        live, taken = f_ref[3 + s], f_ref[5 + s]
        at = pl.ds(pl.multiple_of(s * rows, rows), rows)
        for i, step in enumerate(Y_STEPS[:ny]):
            source = lax.rem(own_y + step, ny) * NC
            for ref, who in ((root_refs[i], core), (t_ref.at[i], 1 - core)):
                to = pl.ds(pl.multiple_of((source + who) * rows, rows), rows)
                for kind in range(2):
                    roots[kind, to, :] = ref[kind, 0]
        parts = []
        norm = jnp.zeros((1, 1), WIDE)
        tail_row = iota((16, block_size), 0) == s
        for y in range(ny):
            a, b = m_ref[y, at, :], o_ref[y, at, :]
            parts += [jnp.where(core == 0, a, b), jnp.where(core == 0, b, a)]
            for ref in (m_ref, o_ref):
                tail = jnp.where(tail_row, ref[y, slots * rows : all_rows, :].astype(WIDE), 0.0)
                norm += jnp.sum(jnp.sum(tail, axis=0, keepdims=True), axis=1, keepdims=True)
        grad = jnp.concatenate(parts, axis=0)
        prod = dot(grad, roots[1], ((1,), (1,))).astype(HALF)
        raw = dot(roots[0], prod)
        raw = jnp.where(iota(raw.shape, 0) < live, raw, 0.0)
        raw_sq = jnp.sum(jnp.sum(raw * raw, axis=0, keepdims=True), axis=1, keepdims=True)
        factor = jnp.sqrt(norm) / jnp.sqrt(raw_sq + GRAFT_EPS)
        d_ref[0] = jnp.where(taken == 1, factor * raw, 0.0).astype(HALF)
        own = m_ref[own_y, at, :]
        left_cols = dot(own, grad, ((1,), (1,)))
        own_columns = (iota((block_size, rows), 0) == own_mp * rows + iota((block_size, rows), 1)).astype(WIDE)
        columns = dot(grad, own_columns.astype(HALF)).astype(HALF)
        right_rows = dot(columns, grad, ((0,), (0,)))
        for old_ref, value, new_ref in ((ls_ref, left_cols, ln_ref), (rs_ref, right_rows, rn_ref)):
            old = old_ref[0]
            fresh = STAT_DECAY * old + (1.0 - STAT_DECAY) * value / block_size
            new_ref[0] = jnp.where(taken == 1, fresh, old)

    whole = pl.BlockSpec((ny, all_rows, block_size), lambda s: (0, 0, 0))
    square = pl.BlockSpec((1, block_size, block_size), lambda s: (s, 0, 0))
    strip = pl.BlockSpec((1, rows, block_size), lambda s: (s, 0, 0))
    return pl.pallas_call(
        kernel,
        grid=(slots,),
        out_shape=[
            jax.ShapeDtypeStruct(left_stat.shape, WIDE),
            jax.ShapeDtypeStruct(right_stat.shape, WIDE),
            jax.ShapeDtypeStruct((slots, block_size, block_size), HALF),
        ],
        in_specs=[pl.BlockSpec(memory_space=pltpu.SMEM), whole, whole]
        + [pl.BlockSpec((2, 1, rows, block_size), lambda s: (0, s, 0, 0))] * ny
        + [pl.BlockSpec((ny, 2, 1, rows, block_size), lambda s: (0, 0, s, 0, 0)), strip, strip],
        out_specs=[strip, strip, square],
        scratch_shapes=[pltpu.VMEM((2, block_size, block_size), HALF)],
        compiler_params=PARAMS,
    )(facts, mine, other, *roots_mine, roots_other, left_stat, right_stat)


def body(
    activations,
    out_grads,
    owners,
    live_rows,
    left_stat,
    right_stat,
    left_root,
    right_root,
    grad_acc,
):
    z, x, y, c = (lax.axis_index(name) for name in ("z", "x", "y", "c"))
    block_rows, rows, toks = activations.shape
    block_size = left_stat.shape[3]
    slots = left_stat.shape[1]
    block_count = owners.shape[0]
    per_z = rows // NZ
    columns = out_grads.shape[1] // block_size // NX
    half_rows = block_rows // 2
    my_owner = z * NX + x
    my_mp = y * NC + c
    my_rows = my_mp * rows

    place = jnp.stack([z, x, c] + [jnp.bitwise_and(x + step, NX - 1) for step in (1, 3, 2)]).astype(jnp.int32)
    *pieces, own = prepare(activations, out_grads, place)
    arrived = [lax.ppermute(piece, "x", ring(NX, step)) for piece, step in zip(pieces, (1, -1, 2))]
    swapped = [lax.ppermute(piece, "c", ring(NC, 1)) for piece in arrived]

    first, left_root, right_root = lax.optimization_barrier((arrived[0], left_root, right_root))
    roots = jnp.concatenate([left_root, right_root], axis=0)
    ny = lax.axis_size("y")
    roots_mine = [roots] + [lax.ppermute(roots, "y", ring(ny, -step)) for step in Y_STEPS[1:ny]]
    arrived[0], *roots_mine = lax.optimization_barrier((first, *roots_mine))
    roots_other = lax.ppermute(jnp.stack(roots_mine), "c", ring(NC, 1))

    send_a, send_b = partial_products(own, arrived, swapped, True)
    keep_a, keep_b = partial_products(own, arrived, swapped, False)

    for step in (1, 2, 4):
        got_a = lax.ppermute(send_a, "z", ring(NZ, step))
        got_b = lax.ppermute(send_b, "z", ring(NZ, -step))
        keep_a, keep_b = keep_a + got_a, keep_b + got_b
        if step < 4:
            part = keep_a.shape[0] // 2
            send_a, send_b = keep_a[part:].astype(HALF), keep_b[part:].astype(HALF)
            keep_a, keep_b = keep_a[:part], keep_b[:part]
    sums = jnp.concatenate([keep_a, keep_b], axis=0).astype(HALF)
    sums = lax.all_gather(sums, "x", axis=0, tiled=False)

    targets = slot_targets(owners, slots)
    by_block = targets.reshape(2, half_rows, NX, columns).transpose(2, 3, 0, 1)[:, :, :, None, None, :]
    shape = (NX, columns, 2, 2, per_z, half_rows)
    owner = by_block // slots
    code = (((owner // NX) * slots + by_block % slots) * 2 + iota(shape, 3)) * per_z + iota(shape, 4)
    code = jnp.where(owner % NX == x, code, -1).reshape(1, -1)
    out_rows = NZ * slots * 2 * per_z
    chosen = (code == iota((out_rows, 1), 0)).astype(HALF)

    picked = pick_blocks(chosen, sums, block_size).reshape(NZ, out_rows // NZ, block_size)
    arrived = lax.all_to_all(picked, "z", 0, 0, tiled=True).reshape(out_rows, block_size)

    wanted = my_owner * slots + iota((slots, block_count), 0)
    matched = targets[None, :] == wanted
    occupied = jnp.any(matched, axis=1).astype(jnp.int32)
    live_mine = jnp.sum(jnp.where(matched, live_rows[None, :], 0), axis=1).astype(jnp.int32)
    own_rows, acc_next = finish_sum(live_mine - my_rows, arrived, grad_acc[0])
    rows_mine = lax.all_gather(own_rows, "y", axis=0, tiled=False)
    rows_other = lax.ppermute(rows_mine, "c", ring(NC, 1))
    facts = jnp.concatenate([jnp.stack([c, y, my_mp]).astype(jnp.int32), live_mine, occupied])
    left_next, right_next, directions = update(
        facts, rows_mine, rows_other, roots_mine, roots_other, left_stat[0], right_stat[0]
    )
    return (left_next[None], right_next[None], acc_next[None], directions[None])


def solution(mesh):
    dp, mp = mesh.devices.shape
    parts = Mesh(mesh.devices.reshape(NZ, NX, mp // NC, NC), ("z", "x", "y", "c"))
    owner, strip = ("z", "x"), ("y", "c")
    state = P(owner, None, strip, None)
    return jax.shard_map(
        body,
        mesh=parts,
        in_specs=(P(None, strip, owner), P(owner, None), P(), P(), state, state, state, state, state),
        out_specs=(state, state, state, P(owner, None, None, None)),
        check_vma=False,
    )
```

```python
import jax
import jax.numpy as jnp
from jax import lax
from jax.experimental import pallas as pl
from jax.experimental.pallas import tpu as pltpu
from jax.sharding import Mesh, PartitionSpec as P

STAT_DECAY = 0.9
GRAFT_EPS = 1e-06
HALF = jnp.bfloat16
WIDE = jnp.float32
NZ, NX, NC = 16, 4, 2
TILES = 6
ROOMY = pltpu.CompilerParams(vmem_limit_bytes=60 * 1024 * 1024)
PARAMS = pltpu.CompilerParams(vmem_limit_bytes=8 * 1024 * 1024)


def slot_targets(owners, slot_count):
    block_count = owners.shape[0]
    same_owner = owners[:, None] == owners[None, :]
    earlier = lax.broadcasted_iota(jnp.int32, (block_count, block_count), 1) < lax.broadcasted_iota(
        jnp.int32, (block_count, block_count), 0
    )
    ranked = jnp.sum(jnp.where(same_owner & earlier, 1, 0), axis=1).astype(jnp.int32)
    return owners * slot_count + ranked


def ring(count, step):
    return [(i, (i + step) % count) for i in range(count)]


def iota(shape, dim):
    return lax.broadcasted_iota(jnp.int32, shape, dim)


def dot(a, b, dims=((1,), (0,))):
    return lax.dot_general(a, b, (dims, ((), ())), preferred_element_type=WIDE)


def prepare(activations, out_grads, place):
    block_rows, rows, toks = activations.shape
    part = block_rows // 2
    per_z = rows // NZ
    count = part * rows
    small = count // 2
    half = toks // NC
    width = out_grads.shape[1] // NX
    tile = width // TILES

    def kernel(place_ref, a_ref, b_ref, *out_refs):
        z, c, step = place_ref[0], place_ref[2], pl.program_id(0)

        @pl.when(step == 0)
        def _():
            m, k = iota((small, count), 0), iota((small, count), 1)
            block = m % part
            row = (m // part) % per_z
            tail = m // (part * per_z)
            high = 2 * (tail // 4) + 4 * ((tail // 2) % 2) + 8 * (tail % 2)
            for side in range(2):
                values = a_ref[side * part : (side + 1) * part].reshape(count, toks)
                for odd in range(2):
                    dist = high + odd
                    goal = jnp.bitwise_and(z + dist if side == 0 else z - dist, NZ - 1)
                    pick = (block * rows + goal * per_z + row == k).astype(WIDE).astype(HALF)
                    moved = dot(pick, values).astype(HALF)
                    turned = jnp.concatenate([moved[:, half:], moved[:, :half]], axis=1)
                    at = (1 - odd) * count + side * small
                    for ref in out_refs:
                        ref[at : at + small, :] = jnp.where(c == 1, turned, moved)

        for i, ref in enumerate(out_refs):

            @pl.when(step == i)
            def _():
                for n in range(TILES):
                    at = 2 * count + n * half
                    ref[at : at + half, :] = b_ref[:, n * tile : (n + 1) * tile]

    piece = (2 * count + TILES * half, toks)
    return pl.pallas_call(
        kernel,
        out_shape=[jax.ShapeDtypeStruct(piece, HALF)] * 3,
        grid_spec=pltpu.PrefetchScalarGridSpec(
            num_scalar_prefetch=1,
            grid=(3,),
            in_specs=[
                pl.BlockSpec(activations.shape, lambda i, place_ref: (0, 0, 0)),
                pl.BlockSpec((half, width), lambda i, place_ref: (place_ref[2], place_ref[3 + i])),
            ],
            out_specs=[pl.BlockSpec(piece, lambda i, place_ref: (0, 0))] * 3,
        ),
        compiler_params=ROOMY,
    )(place, activations, out_grads)


def own_part(piece, out_grads, place):
    toks = out_grads.shape[0]
    half = toks // NC
    width = out_grads.shape[1] // NX
    tile = width // TILES
    count = piece.shape[0] - TILES * half

    def kernel(place_ref, p_ref, b_ref, o_ref):
        c = place_ref[2]
        o_ref[:count, :] = p_ref[...]
        for n in range(TILES):
            for side, who in enumerate((c, 1 - c)):
                at = count + (2 * n + side) * half
                tok = pl.ds(pl.multiple_of(who * half, half), half)
                o_ref[at : at + half, :] = b_ref[tok, n * tile : (n + 1) * tile]

    own = (count + TILES * toks, tile)
    return pl.pallas_call(
        kernel,
        out_shape=jax.ShapeDtypeStruct(own, HALF),
        grid_spec=pltpu.PrefetchScalarGridSpec(
            num_scalar_prefetch=1,
            grid=(1,),
            in_specs=[
                pl.BlockSpec((count, tile), lambda i, place_ref: (0, 0)),
                pl.BlockSpec((toks, width), lambda i, place_ref: (0, place_ref[1])),
            ],
            out_specs=pl.BlockSpec(own, lambda i, place_ref: (0, 0)),
        ),
        compiler_params=ROOMY,
    )(place, piece, out_grads)


def partial_products(own, arrived, swapped, odd):
    toks = own.shape[1]
    half = toks // NC
    total_rows = own.shape[0] - TILES * toks
    count = total_rows // 2
    kind = HALF if odd else WIDE
    group = 2

    def kernel(*refs):
        rows_refs, own_ref, mine, other, (one_ref, two_ref) = refs[:4], refs[4], refs[5:8], refs[8:11], refs[11:]
        for n in range(group):
            at = slice(n * half, (n + 1) * half)
            total = dot(rows_refs[0][...], own_ref[n * toks : (n + 1) * toks, :])
            for rows_ref, m_ref, o_ref in zip(rows_refs[1:], mine, other):
                total += dot(rows_ref[...], jnp.concatenate([m_ref[at, :], o_ref[at, :]], axis=0))
            to = slice(n * toks, (n + 1) * toks)
            one_ref[:, to] = total[: count // 2].astype(kind)
            two_ref[:, to] = total[count // 2 :].astype(kind)

    rows = pl.BlockSpec((count, toks), lambda n: (0 if odd else 1, 0))
    columns = pl.BlockSpec((group * half, toks), lambda n: (total_rows // (group * half) + n, 0))
    own_columns = pl.BlockSpec((group * toks, toks), lambda n: (total_rows // (group * toks) + n, 0))
    return pl.pallas_call(
        kernel,
        grid=(TILES // group,),
        out_shape=[jax.ShapeDtypeStruct((count // 2, TILES * toks), kind)] * 2,
        in_specs=[rows] * 4 + [own_columns] + [columns] * 6,
        out_specs=[pl.BlockSpec((count // 2, group * toks), lambda n: (0, n))] * 2,
        compiler_params=PARAMS,
    )(own, *arrived, own, *arrived, *swapped)


def pick_blocks(chosen, sums, block_size):
    sources, rows, width = sums.shape
    columns = width // block_size
    out_rows = chosen.shape[0]
    tile = out_rows // 2

    def kernel(p_ref, s_ref, o_ref):
        total = None
        for pair in range(sources // 2):
            depth = 2 * columns * rows
            pieces = [
                s_ref[x, :, j * block_size : (j + 1) * block_size]
                for x in (2 * pair, 2 * pair + 1)
                for j in range(columns)
            ]
            term = dot(p_ref[:, pair * depth : (pair + 1) * depth], jnp.concatenate(pieces, axis=0))
            total = term if total is None else total + term
        o_ref[...] = total.astype(HALF)

    return pl.pallas_call(
        kernel,
        grid=(2,),
        out_shape=jax.ShapeDtypeStruct((out_rows, block_size), HALF),
        in_specs=[
            pl.BlockSpec((tile, chosen.shape[1]), lambda n: (n, 0)),
            pl.BlockSpec(sums.shape, lambda n: (0, 0, 0)),
        ],
        out_specs=pl.BlockSpec((tile, block_size), lambda n: (n, 0)),
        compiler_params=PARAMS,
    )(chosen, sums)


def finish_sum(limits, pieces, acc):
    slots, rows, block_size = acc.shape
    per_z = rows // NZ
    total_rows = slots * rows
    piece_rows = pieces.shape[0]

    def kernel(lim_ref, p_ref, a_ref, g_ref, n_ref):
        m, k = iota((total_rows, piece_rows), 0), iota((total_rows, piece_rows), 1)
        row = k % per_z
        piece = (k // per_z) % 2
        slot = (k // (2 * per_z)) % slots
        source = k // (2 * per_z * slots)
        goal = jnp.bitwise_and(source + 8 * piece, NZ - 1)
        adds = (slot * rows + goal * per_z + row == m).astype(WIDE).astype(HALF)
        grad = dot(adds, p_ref[...])
        lane = iota((16, block_size), 1)
        extra_row = iota((16, block_size), 0)
        extra = jnp.zeros((16, block_size), WIDE)
        for s in range(slots):
            live = iota((rows, block_size), 0) < lim_ref[s]
            own = jnp.where(live, grad[s * rows : (s + 1) * rows], 0.0)
            new = a_ref[s] + own * own
            n_ref[s] = new
            grafted = own / (jnp.sqrt(new) + GRAFT_EPS)
            norm = jnp.sum(jnp.sum(grafted * grafted, axis=0, keepdims=True), axis=1, keepdims=True)
            high = norm.astype(HALF).astype(WIDE)
            middle = (norm - high).astype(HALF).astype(WIDE)
            low = norm - high - middle
            spread = jnp.where(lane == 0, high, jnp.where(lane == 1, middle, jnp.where(lane == 2, low, 0.0)))
            extra = jnp.where(extra_row == s, spread, extra)
            g_ref[s * rows : (s + 1) * rows, :] = own.astype(HALF)
        g_ref[total_rows:, :] = extra.astype(HALF)

    vmem = pl.BlockSpec(memory_space=pltpu.VMEM)
    return pl.pallas_call(
        kernel,
        out_shape=[
            jax.ShapeDtypeStruct((total_rows + 16, block_size), HALF),
            jax.ShapeDtypeStruct(acc.shape, WIDE),
        ],
        in_specs=[pl.BlockSpec(memory_space=pltpu.SMEM), vmem, vmem],
        out_specs=[vmem, vmem],
        compiler_params=PARAMS,
    )(limits, pieces, acc)


def update(facts, mine, other, roots_mine, roots_other, left_stat, right_stat):
    ny = mine.shape[0]
    slots, rows, block_size = left_stat.shape
    all_rows = mine.shape[1]

    def kernel(f_ref, m_ref, o_ref, rm_ref, ro_ref, ls_ref, rs_ref, ln_ref, rn_ref, d_ref, roots):
        s = pl.program_id(0)
        core, own_y, own_mp = f_ref[0], f_ref[1], f_ref[2]
        live, taken = f_ref[3 + s], f_ref[5 + s]
        at = pl.ds(pl.multiple_of(s * rows, rows), rows)
        for i in range(ny):
            source = jnp.bitwise_xor(own_y, i) * NC
            for ref, who in ((rm_ref, core), (ro_ref, 1 - core)):
                to = pl.ds(pl.multiple_of((source + who) * rows, rows), rows)
                for kind in range(2):
                    roots[kind, to, :] = ref[i, kind, 0]
        parts = []
        norm = jnp.zeros((1, 1), WIDE)
        tail_row = iota((16, block_size), 0) == s
        for y in range(ny):
            a, b = m_ref[y, at, :], o_ref[y, at, :]
            parts += [jnp.where(core == 0, a, b), jnp.where(core == 0, b, a)]
            for ref in (m_ref, o_ref):
                tail = jnp.where(tail_row, ref[y, slots * rows : all_rows, :].astype(WIDE), 0.0)
                norm += jnp.sum(jnp.sum(tail, axis=0, keepdims=True), axis=1, keepdims=True)
        grad = jnp.concatenate(parts, axis=0)
        prod = dot(grad, roots[1], ((1,), (1,))).astype(HALF)
        raw = dot(roots[0], prod)
        raw = jnp.where(iota(raw.shape, 0) < live, raw, 0.0)
        raw_sq = jnp.sum(jnp.sum(raw * raw, axis=0, keepdims=True), axis=1, keepdims=True)
        factor = jnp.sqrt(norm) / jnp.sqrt(raw_sq + GRAFT_EPS)
        d_ref[0] = jnp.where(taken == 1, factor * raw, 0.0).astype(HALF)
        own = m_ref[own_y, at, :]
        left_cols = dot(own, grad, ((1,), (1,)))
        own_columns = (iota((block_size, rows), 0) == own_mp * rows + iota((block_size, rows), 1)).astype(WIDE)
        columns = dot(grad, own_columns.astype(HALF)).astype(HALF)
        right_rows = dot(columns, grad, ((0,), (0,)))
        for old_ref, value, new_ref in ((ls_ref, left_cols, ln_ref), (rs_ref, right_rows, rn_ref)):
            old = old_ref[0]
            fresh = STAT_DECAY * old + (1.0 - STAT_DECAY) * value / block_size
            new_ref[0] = jnp.where(taken == 1, fresh, old)

    whole = pl.BlockSpec((ny, all_rows, block_size), lambda s: (0, 0, 0))
    square = pl.BlockSpec((1, block_size, block_size), lambda s: (s, 0, 0))
    strip = pl.BlockSpec((1, rows, block_size), lambda s: (s, 0, 0))
    return pl.pallas_call(
        kernel,
        grid=(slots,),
        out_shape=[
            jax.ShapeDtypeStruct(left_stat.shape, WIDE),
            jax.ShapeDtypeStruct(right_stat.shape, WIDE),
            jax.ShapeDtypeStruct((slots, block_size, block_size), HALF),
        ],
        in_specs=[pl.BlockSpec(memory_space=pltpu.SMEM), whole, whole]
        + [pl.BlockSpec((ny, 2, 1, rows, block_size), lambda s: (0, 0, s, 0, 0))] * 2
        + [strip, strip],
        out_specs=[strip, strip, square],
        scratch_shapes=[pltpu.VMEM((2, block_size, block_size), HALF)],
        compiler_params=PARAMS,
    )(facts, mine, other, roots_mine, roots_other, left_stat, right_stat)


def body(
    activations,
    out_grads,
    owners,
    live_rows,
    left_stat,
    right_stat,
    left_root,
    right_root,
    grad_acc,
):
    z, x, y, c = (lax.axis_index(name) for name in ("z", "x", "y", "c"))
    block_rows, rows, toks = activations.shape
    block_size = left_stat.shape[3]
    slots = left_stat.shape[1]
    block_count = owners.shape[0]
    per_z = rows // NZ
    columns = out_grads.shape[1] // block_size // NX
    half_rows = block_rows // 2
    my_owner = z * NX + x
    my_mp = y * NC + c
    my_rows = my_mp * rows

    place = jnp.stack([z, x, c] + [jnp.bitwise_and(x + step, NX - 1) for step in (1, 3, 2)]).astype(jnp.int32)
    pieces = prepare(activations, out_grads, place)
    arrived = [lax.ppermute(piece, "x", ring(NX, step)) for piece, step in zip(pieces, (1, -1, 2))]
    own = own_part(pieces[0], out_grads, place)
    swapped = [lax.ppermute(piece, "c", ring(NC, 1)) for piece in arrived]

    own, left_root, right_root = lax.optimization_barrier((own, left_root, right_root))
    ny = lax.axis_size("y")
    roots = jnp.stack([left_root[0], right_root[0]])[None]
    for step in (1, 2):
        if step < ny:
            roots_from = lax.ppermute(roots, "y", [(i, i ^ step) for i in range(ny)])
            roots = jnp.concatenate([roots, roots_from], axis=0)

    targets = slot_targets(owners, slots)
    by_block = targets.reshape(2, half_rows, NX, columns).transpose(2, 3, 0, 1)[:, :, :, None, None, :]
    shape = (NX, columns, 2, 2, per_z, half_rows)
    owner = by_block // slots
    code = (((owner // NX) * slots + by_block % slots) * 2 + iota(shape, 3)) * per_z + iota(shape, 4)
    code = jnp.where(owner % NX == x, code, -1).reshape(1, -1)
    out_rows = NZ * slots * 2 * per_z
    chosen = (code == iota((out_rows, 1), 0)).astype(HALF)
    own, roots, chosen = lax.optimization_barrier((own, roots, chosen))
    roots_other = lax.ppermute(roots, "c", ring(NC, 1))

    sent = partial_products(own, arrived, swapped, True)
    kept = partial_products(own, arrived, swapped, False)

    sums = []
    for way, out, keep in ((1, sent[0], kept[0]), (-1, sent[1], kept[1])):
        got = [lax.ppermute(out, "z", ring(NZ, way))]
        for step in (2, 4):
            part = got[-1].shape[0] // 2
            out = keep[part : 2 * part]
            for rows_in in got:
                out = out + rows_in[part : 2 * part]
            got.append(lax.ppermute(out.astype(HALF), "z", ring(NZ, way * step)))
        part = got[-1].shape[0]
        total = keep[:part]
        for rows_in in got:
            total = total + rows_in[:part]
        sums.append(total.astype(HALF))
    sums = lax.all_gather(jnp.concatenate(sums, axis=0), "x", axis=0, tiled=False)

    picked = pick_blocks(chosen, sums, block_size).reshape(NZ, out_rows // NZ, block_size)
    arrived = lax.all_to_all(picked, "z", 0, 0, tiled=True).reshape(out_rows, block_size)

    wanted = my_owner * slots + iota((slots, block_count), 0)
    matched = targets[None, :] == wanted
    occupied = jnp.any(matched, axis=1).astype(jnp.int32)
    live_mine = jnp.sum(jnp.where(matched, live_rows[None, :], 0), axis=1).astype(jnp.int32)
    own_rows, acc_next = finish_sum(live_mine - my_rows, arrived, grad_acc[0])
    rows_mine = lax.all_gather(own_rows, "y", axis=0, tiled=False)
    rows_other = lax.ppermute(rows_mine, "c", ring(NC, 1))
    facts = jnp.concatenate([jnp.stack([c, y, my_mp]).astype(jnp.int32), live_mine, occupied])
    left_next, right_next, directions = update(
        facts, rows_mine, rows_other, roots, roots_other, left_stat[0], right_stat[0]
    )
    return (left_next[None], right_next[None], acc_next[None], directions[None])


def solution(mesh):
    dp, mp = mesh.devices.shape
    parts = Mesh(mesh.devices.reshape(NZ, NX, mp // NC, NC), ("z", "x", "y", "c"))
    owner, strip = ("z", "x"), ("y", "c")
    state = P(owner, None, strip, None)
    return jax.shard_map(
        body,
        mesh=parts,
        in_specs=(P(None, strip, owner), P(owner, None), P(), P(), state, state, state, state, state),
        out_specs=(state, state, state, P(owner, None, None, None)),
        check_vma=False,
    )
```

```python
import jax
import jax.numpy as jnp
from jax import lax
from jax.experimental import pallas as pl
from jax.experimental.pallas import tpu as pltpu
from jax.sharding import Mesh, PartitionSpec as P

STAT_DECAY = 0.9
GRAFT_EPS = 1e-06
HALF = jnp.bfloat16
WIDE = jnp.float32
NZ, NX, NC = 16, 4, 2
TILES = 6
ROOMY = pltpu.CompilerParams(vmem_limit_bytes=60 * 1024 * 1024)
PARAMS = pltpu.CompilerParams(vmem_limit_bytes=8 * 1024 * 1024)


def slot_targets(owners, slot_count):
    block_count = owners.shape[0]
    same_owner = owners[:, None] == owners[None, :]
    earlier = lax.broadcasted_iota(jnp.int32, (block_count, block_count), 1) < lax.broadcasted_iota(
        jnp.int32, (block_count, block_count), 0
    )
    ranked = jnp.sum(jnp.where(same_owner & earlier, 1, 0), axis=1).astype(jnp.int32)
    return owners * slot_count + ranked


def ring(count, step):
    return [(i, (i + step) % count) for i in range(count)]


def iota(shape, dim):
    return lax.broadcasted_iota(jnp.int32, shape, dim)


def dot(a, b, dims=((1,), (0,))):
    return lax.dot_general(a, b, (dims, ((), ())), preferred_element_type=WIDE)


def prepare(activations, out_grads, place):
    block_rows, rows, toks = activations.shape
    part = block_rows // 2
    per_z = rows // NZ
    count = part * rows
    small = count // 2
    half = toks // NC
    width = out_grads.shape[1] // NX
    tile = width // TILES

    def kernel(place_ref, a_ref, b_ref, *refs):
        out_refs, (held, sems, out_sems) = refs[:3], refs[3:]
        z, c = place_ref[0], place_ref[2]
        tok = pl.ds(pl.multiple_of(c * half, half), half)
        copies = []
        for i in range(3):
            begin = place_ref[3 + i] * width
            for n in range(TILES):
                at = pl.ds(pl.multiple_of(begin + n * tile, tile), tile)
                to = pl.ds(2 * count + n * half, half)
                copies.append(pltpu.make_async_copy(b_ref.at[tok, at], held.at[i, to, :], sems.at[i, n]))
        for copy in copies:
            copy.start()
        m, k = iota((small, count), 0), iota((small, count), 1)
        block = m % part
        row = (m // part) % per_z
        tail = m // (part * per_z)
        high = 2 * (tail // 4) + 4 * ((tail // 2) % 2) + 8 * (tail % 2)
        for side in range(2):
            values = a_ref[side * part : (side + 1) * part].reshape(count, toks)
            for odd in range(2):
                dist = high + odd
                goal = jnp.bitwise_and(z + dist if side == 0 else z - dist, NZ - 1)
                pick = (block * rows + goal * per_z + row == k).astype(WIDE).astype(HALF)
                moved = dot(pick, values).astype(HALF)
                turned = jnp.concatenate([moved[:, half:], moved[:, :half]], axis=1)
                at = (1 - odd) * count + side * small
                ordered = jnp.where(c == 1, turned, moved)
                for i in range(3):
                    held[i, at : at + small, :] = ordered
        last = [pltpu.make_async_copy(held.at[i], out_refs[i], out_sems.at[i]) for i in range(3)]
        for i in range(3):
            for copy in copies[i * TILES : (i + 1) * TILES]:
                copy.wait()
            last[i].start()
        for copy in last:
            copy.wait()

    piece = (2 * count + TILES * half, toks)
    any_place = pl.BlockSpec(memory_space=pl.ANY)
    return pl.pallas_call(
        kernel,
        out_shape=[jax.ShapeDtypeStruct(piece, HALF)] * 3,
        in_specs=[
            pl.BlockSpec(memory_space=pltpu.SMEM),
            pl.BlockSpec(memory_space=pltpu.VMEM),
            any_place,
        ],
        out_specs=[any_place] * 3,
        scratch_shapes=[
            pltpu.VMEM((3, *piece), HALF),
            pltpu.SemaphoreType.DMA((3, TILES)),
            pltpu.SemaphoreType.DMA((3,)),
        ],
        compiler_params=ROOMY,
    )(place, activations, out_grads)


def own_part(piece, out_grads, place):
    toks = out_grads.shape[0]
    half = toks // NC
    width = out_grads.shape[1] // NX
    tile = width // TILES
    count = piece.shape[0] - TILES * half

    def kernel(place_ref, p_ref, b_ref, o_ref):
        c = place_ref[2]
        o_ref[:count, :] = p_ref[...]
        for n in range(TILES):
            for side, who in enumerate((c, 1 - c)):
                at = count + (2 * n + side) * half
                tok = pl.ds(pl.multiple_of(who * half, half), half)
                o_ref[at : at + half, :] = b_ref[tok, n * tile : (n + 1) * tile]

    own = (count + TILES * toks, tile)
    return pl.pallas_call(
        kernel,
        out_shape=jax.ShapeDtypeStruct(own, HALF),
        grid_spec=pltpu.PrefetchScalarGridSpec(
            num_scalar_prefetch=1,
            grid=(1,),
            in_specs=[
                pl.BlockSpec((count, tile), lambda i, place_ref: (0, 0)),
                pl.BlockSpec((toks, width), lambda i, place_ref: (0, place_ref[1])),
            ],
            out_specs=pl.BlockSpec(own, lambda i, place_ref: (0, 0)),
        ),
        compiler_params=ROOMY,
    )(place, piece, out_grads)


def partial_products(own, arrived, swapped, odd):
    toks = own.shape[1]
    half = toks // NC
    total_rows = own.shape[0] - TILES * toks
    count = total_rows // 2
    kind = HALF if odd else WIDE
    group = 2

    def kernel(*refs):
        rows_refs, own_ref, mine, other, (one_ref, two_ref) = refs[:4], refs[4], refs[5:8], refs[8:11], refs[11:]
        for n in range(group):
            at = slice(n * half, (n + 1) * half)
            total = dot(rows_refs[0][...], own_ref[n * toks : (n + 1) * toks, :])
            for rows_ref, m_ref, o_ref in zip(rows_refs[1:], mine, other):
                total += dot(rows_ref[...], jnp.concatenate([m_ref[at, :], o_ref[at, :]], axis=0))
            to = slice(n * toks, (n + 1) * toks)
            one_ref[:, to] = total[: count // 2].astype(kind)
            two_ref[:, to] = total[count // 2 :].astype(kind)

    rows = pl.BlockSpec((count, toks), lambda n: (0 if odd else 1, 0))
    columns = pl.BlockSpec((group * half, toks), lambda n: (total_rows // (group * half) + n, 0))
    own_columns = pl.BlockSpec((group * toks, toks), lambda n: (total_rows // (group * toks) + n, 0))
    return pl.pallas_call(
        kernel,
        grid=(TILES // group,),
        out_shape=[jax.ShapeDtypeStruct((count // 2, TILES * toks), kind)] * 2,
        in_specs=[rows] * 4 + [own_columns] + [columns] * 6,
        out_specs=[pl.BlockSpec((count // 2, group * toks), lambda n: (0, n))] * 2,
        compiler_params=PARAMS,
    )(own, *arrived, own, *arrived, *swapped)


def pick_blocks(chosen, sums, block_size):
    sources, rows, width = sums.shape
    columns = width // block_size
    out_rows = chosen.shape[0]
    tile = out_rows // 2

    def kernel(p_ref, s_ref, o_ref):
        total = None
        for pair in range(sources // 2):
            depth = 2 * columns * rows
            pieces = [
                s_ref[x, :, j * block_size : (j + 1) * block_size]
                for x in (2 * pair, 2 * pair + 1)
                for j in range(columns)
            ]
            term = dot(p_ref[:, pair * depth : (pair + 1) * depth], jnp.concatenate(pieces, axis=0))
            total = term if total is None else total + term
        o_ref[...] = total.astype(HALF)

    return pl.pallas_call(
        kernel,
        grid=(2,),
        out_shape=jax.ShapeDtypeStruct((out_rows, block_size), HALF),
        in_specs=[
            pl.BlockSpec((tile, chosen.shape[1]), lambda n: (n, 0)),
            pl.BlockSpec(sums.shape, lambda n: (0, 0, 0)),
        ],
        out_specs=pl.BlockSpec((tile, block_size), lambda n: (n, 0)),
        compiler_params=PARAMS,
    )(chosen, sums)


def finish_sum(limits, pieces, acc):
    slots, rows, block_size = acc.shape
    per_z = rows // NZ
    total_rows = slots * rows
    piece_rows = pieces.shape[0]

    def kernel(lim_ref, p_ref, a_ref, g_ref, n_ref):
        m, k = iota((total_rows, piece_rows), 0), iota((total_rows, piece_rows), 1)
        row = k % per_z
        piece = (k // per_z) % 2
        slot = (k // (2 * per_z)) % slots
        source = k // (2 * per_z * slots)
        goal = jnp.bitwise_and(source + 8 * piece, NZ - 1)
        adds = (slot * rows + goal * per_z + row == m).astype(WIDE).astype(HALF)
        grad = dot(adds, p_ref[...])
        lane = iota((16, block_size), 1)
        extra_row = iota((16, block_size), 0)
        extra = jnp.zeros((16, block_size), WIDE)
        for s in range(slots):
            live = iota((rows, block_size), 0) < lim_ref[s]
            own = jnp.where(live, grad[s * rows : (s + 1) * rows], 0.0)
            new = a_ref[s] + own * own
            n_ref[s] = new
            grafted = own / (jnp.sqrt(new) + GRAFT_EPS)
            norm = jnp.sum(jnp.sum(grafted * grafted, axis=0, keepdims=True), axis=1, keepdims=True)
            high = norm.astype(HALF).astype(WIDE)
            middle = (norm - high).astype(HALF).astype(WIDE)
            low = norm - high - middle
            spread = jnp.where(lane == 0, high, jnp.where(lane == 1, middle, jnp.where(lane == 2, low, 0.0)))
            extra = jnp.where(extra_row == s, spread, extra)
            g_ref[s * rows : (s + 1) * rows, :] = own.astype(HALF)
        g_ref[total_rows:, :] = extra.astype(HALF)

    vmem = pl.BlockSpec(memory_space=pltpu.VMEM)
    return pl.pallas_call(
        kernel,
        out_shape=[
            jax.ShapeDtypeStruct((total_rows + 16, block_size), HALF),
            jax.ShapeDtypeStruct(acc.shape, WIDE),
        ],
        in_specs=[pl.BlockSpec(memory_space=pltpu.SMEM), vmem, vmem],
        out_specs=[vmem, vmem],
        compiler_params=PARAMS,
    )(limits, pieces, acc)


def update(facts, mine, other, roots_mine, roots_other, left_stat, right_stat):
    ny = mine.shape[0]
    slots, rows, block_size = left_stat.shape
    all_rows = mine.shape[1]

    def kernel(f_ref, m_ref, o_ref, rm_ref, ro_ref, ls_ref, rs_ref, ln_ref, rn_ref, d_ref, roots):
        s = pl.program_id(0)
        core, own_y, own_mp = f_ref[0], f_ref[1], f_ref[2]
        live, taken = f_ref[3 + s], f_ref[5 + s]
        at = pl.ds(pl.multiple_of(s * rows, rows), rows)
        for i in range(ny):
            source = jnp.bitwise_xor(own_y, i) * NC
            for ref, who in ((rm_ref, core), (ro_ref, 1 - core)):
                to = pl.ds(pl.multiple_of((source + who) * rows, rows), rows)
                for kind in range(2):
                    roots[kind, to, :] = ref[i, kind, 0]
        parts = []
        norm = jnp.zeros((1, 1), WIDE)
        tail_row = iota((16, block_size), 0) == s
        for y in range(ny):
            a, b = m_ref[y, at, :], o_ref[y, at, :]
            parts += [jnp.where(core == 0, a, b), jnp.where(core == 0, b, a)]
            for ref in (m_ref, o_ref):
                tail = jnp.where(tail_row, ref[y, slots * rows : all_rows, :].astype(WIDE), 0.0)
                norm += jnp.sum(jnp.sum(tail, axis=0, keepdims=True), axis=1, keepdims=True)
        grad = jnp.concatenate(parts, axis=0)
        prod = dot(grad, roots[1], ((1,), (1,))).astype(HALF)
        raw = dot(roots[0], prod)
        raw = jnp.where(iota(raw.shape, 0) < live, raw, 0.0)
        raw_sq = jnp.sum(jnp.sum(raw * raw, axis=0, keepdims=True), axis=1, keepdims=True)
        factor = jnp.sqrt(norm) / jnp.sqrt(raw_sq + GRAFT_EPS)
        d_ref[0] = jnp.where(taken == 1, factor * raw, 0.0).astype(HALF)
        own = m_ref[own_y, at, :]
        left_cols = dot(own, grad, ((1,), (1,)))
        own_columns = (iota((block_size, rows), 0) == own_mp * rows + iota((block_size, rows), 1)).astype(WIDE)
        columns = dot(grad, own_columns.astype(HALF)).astype(HALF)
        right_rows = dot(columns, grad, ((0,), (0,)))
        for old_ref, value, new_ref in ((ls_ref, left_cols, ln_ref), (rs_ref, right_rows, rn_ref)):
            old = old_ref[0]
            fresh = STAT_DECAY * old + (1.0 - STAT_DECAY) * value / block_size
            new_ref[0] = jnp.where(taken == 1, fresh, old)

    whole = pl.BlockSpec((ny, all_rows, block_size), lambda s: (0, 0, 0))
    square = pl.BlockSpec((1, block_size, block_size), lambda s: (s, 0, 0))
    strip = pl.BlockSpec((1, rows, block_size), lambda s: (s, 0, 0))
    return pl.pallas_call(
        kernel,
        grid=(slots,),
        out_shape=[
            jax.ShapeDtypeStruct(left_stat.shape, WIDE),
            jax.ShapeDtypeStruct(right_stat.shape, WIDE),
            jax.ShapeDtypeStruct((slots, block_size, block_size), HALF),
        ],
        in_specs=[pl.BlockSpec(memory_space=pltpu.SMEM), whole, whole]
        + [pl.BlockSpec((ny, 2, 1, rows, block_size), lambda s: (0, 0, s, 0, 0))] * 2
        + [strip, strip],
        out_specs=[strip, strip, square],
        scratch_shapes=[pltpu.VMEM((2, block_size, block_size), HALF)],
        compiler_params=PARAMS,
    )(facts, mine, other, roots_mine, roots_other, left_stat, right_stat)


def body(
    activations,
    out_grads,
    owners,
    live_rows,
    left_stat,
    right_stat,
    left_root,
    right_root,
    grad_acc,
):
    z, x, y, c = (lax.axis_index(name) for name in ("z", "x", "y", "c"))
    block_rows, rows, toks = activations.shape
    block_size = left_stat.shape[3]
    slots = left_stat.shape[1]
    block_count = owners.shape[0]
    per_z = rows // NZ
    columns = out_grads.shape[1] // block_size // NX
    half_rows = block_rows // 2
    my_owner = z * NX + x
    my_mp = y * NC + c
    my_rows = my_mp * rows

    place = jnp.stack([z, x, c] + [jnp.bitwise_and(x + step, NX - 1) for step in (1, 3, 2)]).astype(jnp.int32)
    pieces = prepare(activations, out_grads, place)
    arrived = [lax.ppermute(piece, "x", ring(NX, step)) for piece, step in zip(pieces, (1, -1, 2))]

    piece_own, owners = lax.optimization_barrier((pieces[0], owners))
    targets = slot_targets(owners, slots)
    by_block = targets.reshape(2, half_rows, NX, columns).transpose(2, 3, 0, 1)[:, :, :, None, None, :]
    shape = (NX, columns, 2, 2, per_z, half_rows)
    owner = by_block // slots
    code = (((owner // NX) * slots + by_block % slots) * 2 + iota(shape, 3)) * per_z + iota(shape, 4)
    code = jnp.where(owner % NX == x, code, -1).reshape(1, -1)
    out_rows = NZ * slots * 2 * per_z
    chosen = (code == iota((out_rows, 1), 0)).astype(HALF)
    piece_own, chosen = lax.optimization_barrier((piece_own, chosen))
    own = own_part(piece_own, out_grads, place)

    own, left_root, right_root = lax.optimization_barrier((own, left_root, right_root))
    ny = lax.axis_size("y")
    roots = jnp.stack([left_root[0], right_root[0]])[None]
    for step in (1, 2):
        if step < ny:
            came = lax.ppermute(roots, "y", [(i, i ^ step) for i in range(ny)])
            roots = jnp.concatenate([roots, came], axis=0)
    own, roots = lax.optimization_barrier((own, roots))
    swapped = [lax.ppermute(piece, "c", ring(NC, 1)) for piece in arrived]
    roots_other = lax.ppermute(roots, "c", ring(NC, 1))

    sent = partial_products(own, arrived, swapped, True)
    kept = partial_products(own, arrived, swapped, False)

    sums = []
    for way, out, keep in ((1, sent[0], kept[0]), (-1, sent[1], kept[1])):
        got = [lax.ppermute(out, "z", ring(NZ, way))]
        for step in (2, 4):
            part = got[-1].shape[0] // 2
            out = keep[part : 2 * part]
            for rows_in in got:
                out = out + rows_in[part : 2 * part]
            got.append(lax.ppermute(out.astype(HALF), "z", ring(NZ, way * step)))
        part = got[-1].shape[0]
        total = keep[:part]
        for rows_in in got:
            total = total + rows_in[:part]
        sums.append(total.astype(HALF))
    sums = lax.all_gather(jnp.concatenate(sums, axis=0), "x", axis=0, tiled=False)

    picked = pick_blocks(chosen, sums, block_size).reshape(NZ, out_rows // NZ, block_size)
    arrived = lax.all_to_all(picked, "z", 0, 0, tiled=True).reshape(out_rows, block_size)

    wanted = my_owner * slots + iota((slots, block_count), 0)
    matched = targets[None, :] == wanted
    occupied = jnp.any(matched, axis=1).astype(jnp.int32)
    live_mine = jnp.sum(jnp.where(matched, live_rows[None, :], 0), axis=1).astype(jnp.int32)
    own_rows, acc_next = finish_sum(live_mine - my_rows, arrived, grad_acc[0])
    rows_mine = lax.all_gather(own_rows, "y", axis=0, tiled=False)
    rows_other = lax.ppermute(rows_mine, "c", ring(NC, 1))
    facts = jnp.concatenate([jnp.stack([c, y, my_mp]).astype(jnp.int32), live_mine, occupied])
    left_next, right_next, directions = update(
        facts, rows_mine, rows_other, roots, roots_other, left_stat[0], right_stat[0]
    )
    return (left_next[None], right_next[None], acc_next[None], directions[None])


def solution(mesh):
    dp, mp = mesh.devices.shape
    parts = Mesh(mesh.devices.reshape(NZ, NX, mp // NC, NC), ("z", "x", "y", "c"))
    owner, strip = ("z", "x"), ("y", "c")
    state = P(owner, None, strip, None)
    return jax.shard_map(
        body,
        mesh=parts,
        in_specs=(P(None, strip, owner), P(owner, None), P(), P(), state, state, state, state, state),
        out_specs=(state, state, state, P(owner, None, None, None)),
        check_vma=False,
    )
```

```python
import jax
import jax.numpy as jnp
from jax import lax
from jax.experimental import pallas as pl
from jax.experimental.pallas import tpu as pltpu
from jax.sharding import Mesh, PartitionSpec as P

STAT_DECAY = 0.9
GRAFT_EPS = 1e-06
HALF = jnp.bfloat16
WIDE = jnp.float32
NZ, NX, NC = 16, 4, 2
TILES = 6
CHUNKS = 2
ROOMY = pltpu.CompilerParams(vmem_limit_bytes=60 * 1024 * 1024)
PARAMS = pltpu.CompilerParams(vmem_limit_bytes=8 * 1024 * 1024)


def slot_targets(owners, slot_count):
    block_count = owners.shape[0]
    same_owner = owners[:, None] == owners[None, :]
    earlier = lax.broadcasted_iota(jnp.int32, (block_count, block_count), 1) < lax.broadcasted_iota(
        jnp.int32, (block_count, block_count), 0
    )
    ranked = jnp.sum(jnp.where(same_owner & earlier, 1, 0), axis=1).astype(jnp.int32)
    return owners * slot_count + ranked


def ring(count, step):
    return [(i, (i + step) % count) for i in range(count)]


def iota(shape, dim):
    return lax.broadcasted_iota(jnp.int32, shape, dim)


def dot(a, b, dims=((1,), (0,))):
    return lax.dot_general(a, b, (dims, ((), ())), preferred_element_type=WIDE)


def prepare(activations, out_grads, place):
    block_rows, rows, toks = activations.shape
    part = block_rows // 2
    per_z = rows // NZ
    count = part * rows
    small = count // 2
    half = toks // NC
    width = out_grads.shape[1] // NX
    tile = width // TILES

    def kernel(place_ref, a_ref, b_ref, *refs):
        out_refs, (held, sems, out_sems) = refs[:3], refs[3:]
        z, c = place_ref[0], place_ref[2]
        tok = pl.ds(pl.multiple_of(c * half, half), half)
        copies = []
        for i in range(3):
            begin = place_ref[3 + i] * width
            for n in range(TILES):
                at = pl.ds(pl.multiple_of(begin + n * tile, tile), tile)
                to = pl.ds(2 * count + n * half, half)
                copies.append(pltpu.make_async_copy(b_ref.at[tok, at], held.at[i, to, :], sems.at[i, n]))
        for copy in copies:
            copy.start()
        m, k = iota((small, count), 0), iota((small, count), 1)
        block = m % part
        row = (m // part) % per_z
        tail = m // (part * per_z)
        high = 2 * (tail // 4) + 4 * ((tail // 2) % 2) + 8 * (tail % 2)
        for side in range(2):
            values = a_ref[side * part : (side + 1) * part].reshape(count, toks)
            for odd in range(2):
                dist = high + odd
                goal = jnp.bitwise_and(z + dist if side == 0 else z - dist, NZ - 1)
                pick = (block * rows + goal * per_z + row == k).astype(WIDE).astype(HALF)
                moved = dot(pick, values).astype(HALF)
                turned = jnp.concatenate([moved[:, half:], moved[:, :half]], axis=1)
                at = (1 - odd) * count + side * small
                ordered = jnp.where(c == 1, turned, moved)
                for i in range(3):
                    held[i, at : at + small, :] = ordered
        last = [pltpu.make_async_copy(held.at[i], out_refs[i], out_sems.at[i]) for i in range(3)]
        for i in range(3):
            for copy in copies[i * TILES : (i + 1) * TILES]:
                copy.wait()
            last[i].start()
        for copy in last:
            copy.wait()

    piece = (2 * count + TILES * half, toks)
    any_place = pl.BlockSpec(memory_space=pl.ANY)
    return pl.pallas_call(
        kernel,
        out_shape=[jax.ShapeDtypeStruct(piece, HALF)] * 3,
        in_specs=[
            pl.BlockSpec(memory_space=pltpu.SMEM),
            pl.BlockSpec(memory_space=pltpu.VMEM),
            any_place,
        ],
        out_specs=[any_place] * 3,
        scratch_shapes=[
            pltpu.VMEM((3, *piece), HALF),
            pltpu.SemaphoreType.DMA((3, TILES)),
            pltpu.SemaphoreType.DMA((3,)),
        ],
        compiler_params=ROOMY,
    )(place, activations, out_grads)


def own_part(piece, out_grads, place):
    toks = out_grads.shape[0]
    half = toks // NC
    width = out_grads.shape[1] // NX
    tile = width // TILES
    count = piece.shape[0] - TILES * half

    def kernel(place_ref, p_ref, b_ref, o_ref):
        c = place_ref[2]
        o_ref[:count, :] = p_ref[...]
        for n in range(TILES):
            for side, who in enumerate((c, 1 - c)):
                at = count + (2 * n + side) * half
                tok = pl.ds(pl.multiple_of(who * half, half), half)
                o_ref[at : at + half, :] = b_ref[tok, n * tile : (n + 1) * tile]

    own = (count + TILES * toks, tile)
    return pl.pallas_call(
        kernel,
        out_shape=jax.ShapeDtypeStruct(own, HALF),
        grid_spec=pltpu.PrefetchScalarGridSpec(
            num_scalar_prefetch=1,
            grid=(1,),
            in_specs=[
                pl.BlockSpec((count, tile), lambda i, place_ref: (0, 0)),
                pl.BlockSpec((toks, width), lambda i, place_ref: (0, place_ref[1])),
            ],
            out_specs=pl.BlockSpec(own, lambda i, place_ref: (0, 0)),
        ),
        compiler_params=ROOMY,
    )(place, piece, out_grads)


def partial_products(own, arrived, swapped, odd, chunk):
    toks = own.shape[1]
    half = toks // NC
    total_rows = own.shape[0] - TILES * toks
    count = total_rows // 2
    kind = HALF if odd else WIDE
    group = TILES // CHUNKS

    def kernel(*refs):
        rows_refs, own_ref, mine, other, (one_ref, two_ref) = refs[:4], refs[4], refs[5:8], refs[8:11], refs[11:]
        for n in range(group):
            at = slice(n * half, (n + 1) * half)
            total = dot(rows_refs[0][...], own_ref[n * toks : (n + 1) * toks, :])
            for rows_ref, m_ref, o_ref in zip(rows_refs[1:], mine, other):
                total += dot(rows_ref[...], jnp.concatenate([m_ref[at, :], o_ref[at, :]], axis=0))
            to = slice(n * toks, (n + 1) * toks)
            one_ref[:, to] = total[: count // 2].astype(kind)
            two_ref[:, to] = total[count // 2 :].astype(kind)

    def block(skip, size):
        first = pl.Element(size)
        return pl.BlockSpec((first, pl.Element(toks)), lambda n: (skip + chunk * size, 0))

    rows = pl.BlockSpec((count, toks), lambda n: (0 if odd else 1, 0))
    return pl.pallas_call(
        kernel,
        grid=(1,),
        out_shape=[jax.ShapeDtypeStruct((count // 2, group * toks), kind)] * 2,
        in_specs=[rows] * 4 + [block(total_rows, group * toks)] + [block(total_rows, group * half)] * 6,
        out_specs=[pl.BlockSpec((count // 2, group * toks), lambda n: (0, 0))] * 2,
        compiler_params=PARAMS,
    )(own, *arrived, own, *arrived, *swapped)


def pick_blocks(chosen, sums, block_size):
    sources, rows, width = sums.shape[0], sums.shape[1] // CHUNKS, sums.shape[2]
    columns = CHUNKS * width // block_size
    out_rows = chosen.shape[0]
    tile = out_rows // 2

    def kernel(p_ref, s_ref, o_ref):
        total = None
        for pair in range(sources // 2):
            depth = 2 * columns * rows
            pieces = []
            for x in (2 * pair, 2 * pair + 1):
                whole = jnp.concatenate([s_ref[x, k * rows : (k + 1) * rows, :] for k in range(CHUNKS)], axis=1)
                pieces += [whole[:, j * block_size : (j + 1) * block_size] for j in range(columns)]
            term = dot(p_ref[:, pair * depth : (pair + 1) * depth], jnp.concatenate(pieces, axis=0))
            total = term if total is None else total + term
        o_ref[...] = total.astype(HALF)

    return pl.pallas_call(
        kernel,
        grid=(2,),
        out_shape=jax.ShapeDtypeStruct((out_rows, block_size), HALF),
        in_specs=[
            pl.BlockSpec((tile, chosen.shape[1]), lambda n: (n, 0)),
            pl.BlockSpec(sums.shape, lambda n: (0, 0, 0)),
        ],
        out_specs=pl.BlockSpec((tile, block_size), lambda n: (n, 0)),
        compiler_params=PARAMS,
    )(chosen, sums)


def finish_sum(limits, pieces, acc):
    slots, rows, block_size = acc.shape
    per_z = rows // NZ
    total_rows = slots * rows
    piece_rows = pieces.shape[0]

    def kernel(lim_ref, p_ref, a_ref, g_ref, n_ref):
        m, k = iota((total_rows, piece_rows), 0), iota((total_rows, piece_rows), 1)
        row = k % per_z
        piece = (k // per_z) % 2
        slot = (k // (2 * per_z)) % slots
        source = k // (2 * per_z * slots)
        goal = jnp.bitwise_and(source + 8 * piece, NZ - 1)
        adds = (slot * rows + goal * per_z + row == m).astype(WIDE).astype(HALF)
        grad = dot(adds, p_ref[...])
        lane = iota((16, block_size), 1)
        extra_row = iota((16, block_size), 0)
        extra = jnp.zeros((16, block_size), WIDE)
        for s in range(slots):
            live = iota((rows, block_size), 0) < lim_ref[s]
            own = jnp.where(live, grad[s * rows : (s + 1) * rows], 0.0)
            new = a_ref[s] + own * own
            n_ref[s] = new
            grafted = own / (jnp.sqrt(new) + GRAFT_EPS)
            norm = jnp.sum(jnp.sum(grafted * grafted, axis=0, keepdims=True), axis=1, keepdims=True)
            high = norm.astype(HALF).astype(WIDE)
            middle = (norm - high).astype(HALF).astype(WIDE)
            low = norm - high - middle
            spread = jnp.where(lane == 0, high, jnp.where(lane == 1, middle, jnp.where(lane == 2, low, 0.0)))
            extra = jnp.where(extra_row == s, spread, extra)
            g_ref[s * rows : (s + 1) * rows, :] = own.astype(HALF)
        g_ref[total_rows:, :] = extra.astype(HALF)

    vmem = pl.BlockSpec(memory_space=pltpu.VMEM)
    return pl.pallas_call(
        kernel,
        out_shape=[
            jax.ShapeDtypeStruct((total_rows + 16, block_size), HALF),
            jax.ShapeDtypeStruct(acc.shape, WIDE),
        ],
        in_specs=[pl.BlockSpec(memory_space=pltpu.SMEM), vmem, vmem],
        out_specs=[vmem, vmem],
        compiler_params=PARAMS,
    )(limits, pieces, acc)


def update(facts, mine, other, roots_mine, roots_other, left_stat, right_stat):
    ny = mine.shape[0]
    slots, rows, block_size = left_stat.shape
    all_rows = mine.shape[1]

    def kernel(f_ref, m_ref, o_ref, rm_ref, ro_ref, ls_ref, rs_ref, ln_ref, rn_ref, d_ref, roots):
        s = pl.program_id(0)
        core, own_y, own_mp = f_ref[0], f_ref[1], f_ref[2]
        live, taken = f_ref[3 + s], f_ref[5 + s]
        at = pl.ds(pl.multiple_of(s * rows, rows), rows)
        for i in range(ny):
            source = jnp.bitwise_xor(own_y, i) * NC
            for ref, who in ((rm_ref, core), (ro_ref, 1 - core)):
                to = pl.ds(pl.multiple_of((source + who) * rows, rows), rows)
                for kind in range(2):
                    roots[kind, to, :] = ref[i, kind, 0]
        parts = []
        norm = jnp.zeros((1, 1), WIDE)
        tail_row = iota((16, block_size), 0) == s
        for y in range(ny):
            a, b = m_ref[y, at, :], o_ref[y, at, :]
            parts += [jnp.where(core == 0, a, b), jnp.where(core == 0, b, a)]
            for ref in (m_ref, o_ref):
                tail = jnp.where(tail_row, ref[y, slots * rows : all_rows, :].astype(WIDE), 0.0)
                norm += jnp.sum(jnp.sum(tail, axis=0, keepdims=True), axis=1, keepdims=True)
        grad = jnp.concatenate(parts, axis=0)
        prod = dot(grad, roots[1], ((1,), (1,))).astype(HALF)
        raw = dot(roots[0], prod)
        raw = jnp.where(iota(raw.shape, 0) < live, raw, 0.0)
        raw_sq = jnp.sum(jnp.sum(raw * raw, axis=0, keepdims=True), axis=1, keepdims=True)
        factor = jnp.sqrt(norm) / jnp.sqrt(raw_sq + GRAFT_EPS)
        d_ref[0] = jnp.where(taken == 1, factor * raw, 0.0).astype(HALF)
        own = m_ref[own_y, at, :]
        left_cols = dot(own, grad, ((1,), (1,)))
        own_columns = (iota((block_size, rows), 0) == own_mp * rows + iota((block_size, rows), 1)).astype(WIDE)
        columns = dot(grad, own_columns.astype(HALF)).astype(HALF)
        right_rows = dot(columns, grad, ((0,), (0,)))
        for old_ref, value, new_ref in ((ls_ref, left_cols, ln_ref), (rs_ref, right_rows, rn_ref)):
            old = old_ref[0]
            fresh = STAT_DECAY * old + (1.0 - STAT_DECAY) * value / block_size
            new_ref[0] = jnp.where(taken == 1, fresh, old)

    whole = pl.BlockSpec((ny, all_rows, block_size), lambda s: (0, 0, 0))
    square = pl.BlockSpec((1, block_size, block_size), lambda s: (s, 0, 0))
    strip = pl.BlockSpec((1, rows, block_size), lambda s: (s, 0, 0))
    return pl.pallas_call(
        kernel,
        grid=(slots,),
        out_shape=[
            jax.ShapeDtypeStruct(left_stat.shape, WIDE),
            jax.ShapeDtypeStruct(right_stat.shape, WIDE),
            jax.ShapeDtypeStruct((slots, block_size, block_size), HALF),
        ],
        in_specs=[pl.BlockSpec(memory_space=pltpu.SMEM), whole, whole]
        + [pl.BlockSpec((ny, 2, 1, rows, block_size), lambda s: (0, 0, s, 0, 0))] * 2
        + [strip, strip],
        out_specs=[strip, strip, square],
        scratch_shapes=[pltpu.VMEM((2, block_size, block_size), HALF)],
        compiler_params=PARAMS,
    )(facts, mine, other, roots_mine, roots_other, left_stat, right_stat)


def body(
    activations,
    out_grads,
    owners,
    live_rows,
    left_stat,
    right_stat,
    left_root,
    right_root,
    grad_acc,
):
    z, x, y, c = (lax.axis_index(name) for name in ("z", "x", "y", "c"))
    block_rows, rows, toks = activations.shape
    block_size = left_stat.shape[3]
    slots = left_stat.shape[1]
    block_count = owners.shape[0]
    per_z = rows // NZ
    columns = out_grads.shape[1] // block_size // NX
    half_rows = block_rows // 2
    my_owner = z * NX + x
    my_mp = y * NC + c
    my_rows = my_mp * rows

    place = jnp.stack([z, x, c] + [jnp.bitwise_and(x + step, NX - 1) for step in (2, 3, 1)]).astype(jnp.int32)
    pieces = prepare(activations, out_grads, place)
    arrived = [lax.ppermute(piece, "x", ring(NX, step)) for piece, step in zip(pieces, (2, -1, 1))]

    piece_own, owners = lax.optimization_barrier((pieces[0], owners))
    targets = slot_targets(owners, slots)
    by_block = targets.reshape(2, half_rows, NX, columns).transpose(2, 3, 0, 1)[:, :, :, None, None, :]
    shape = (NX, columns, 2, 2, per_z, half_rows)
    owner = by_block // slots
    code = (((owner // NX) * slots + by_block % slots) * 2 + iota(shape, 3)) * per_z + iota(shape, 4)
    code = jnp.where(owner % NX == x, code, -1).reshape(1, -1)
    out_rows = NZ * slots * 2 * per_z
    chosen = (code == iota((out_rows, 1), 0)).astype(HALF)
    piece_own, chosen = lax.optimization_barrier((piece_own, chosen))
    own = own_part(piece_own, out_grads, place)

    own, left_root, right_root = lax.optimization_barrier((own, left_root, right_root))
    ny = lax.axis_size("y")
    roots = jnp.stack([left_root[0], right_root[0]])[None]
    for step in (1, 2):
        if step < ny:
            came = lax.ppermute(roots, "y", [(i, i ^ step) for i in range(ny)])
            roots = jnp.concatenate([roots, came], axis=0)
    own, roots = lax.optimization_barrier((own, roots))
    swapped = [lax.ppermute(piece, "c", ring(NC, 1)) for piece in arrived]
    roots_other = lax.ppermute(roots, "c", ring(NC, 1))

    sent = [partial_products(own, arrived, swapped, True, chunk) for chunk in range(CHUNKS)]
    kept = [partial_products(own, arrived, swapped, False, chunk) for chunk in range(CHUNKS)]

    def add_along(out, keep, way):
        got = [lax.ppermute(out, "z", ring(NZ, way))]
        for step in (2, 4):
            part = got[-1].shape[0] // 2
            out = keep[part : 2 * part]
            for rows_in in got:
                out = out + rows_in[part : 2 * part]
            got.append(lax.ppermute(out.astype(HALF), "z", ring(NZ, way * step)))
        part = got[-1].shape[0]
        total = keep[:part]
        for rows_in in got:
            total = total + rows_in[:part]
        return total.astype(HALF)

    sums = [add_along(sent[k][i], kept[k][i], (1, -1)[i]) for k in range(CHUNKS) for i in range(2)]
    sums = lax.all_gather(jnp.concatenate(sums, axis=0), "x", axis=0, tiled=False)

    picked = pick_blocks(chosen, sums, block_size).reshape(NZ, out_rows // NZ, block_size)
    arrived = lax.all_to_all(picked, "z", 0, 0, tiled=True).reshape(out_rows, block_size)

    wanted = my_owner * slots + iota((slots, block_count), 0)
    matched = targets[None, :] == wanted
    occupied = jnp.any(matched, axis=1).astype(jnp.int32)
    live_mine = jnp.sum(jnp.where(matched, live_rows[None, :], 0), axis=1).astype(jnp.int32)
    own_rows, acc_next = finish_sum(live_mine - my_rows, arrived, grad_acc[0])
    rows_mine = lax.all_gather(own_rows, "y", axis=0, tiled=False)
    rows_other = lax.ppermute(rows_mine, "c", ring(NC, 1))
    facts = jnp.concatenate([jnp.stack([c, y, my_mp]).astype(jnp.int32), live_mine, occupied])
    left_next, right_next, directions = update(
        facts, rows_mine, rows_other, roots, roots_other, left_stat[0], right_stat[0]
    )
    return (left_next[None], right_next[None], acc_next[None], directions[None])


def solution(mesh):
    dp, mp = mesh.devices.shape
    parts = Mesh(mesh.devices.reshape(NZ, NX, mp // NC, NC), ("z", "x", "y", "c"))
    owner, strip = ("z", "x"), ("y", "c")
    state = P(owner, None, strip, None)
    return jax.shard_map(
        body,
        mesh=parts,
        in_specs=(P(None, strip, owner), P(owner, None), P(), P(), state, state, state, state, state),
        out_specs=(state, state, state, P(owner, None, None, None)),
        check_vma=False,
    )
```

```python
import jax
import jax.numpy as jnp
from jax import lax
from jax.experimental import pallas as pl
from jax.experimental.pallas import tpu as pltpu
from jax.sharding import Mesh, PartitionSpec as P

STAT_DECAY = 0.9
GRAFT_EPS = 1e-06
HALF = jnp.bfloat16
WIDE = jnp.float32
NZ, NX, NC = 16, 4, 2
TILES = 6
ROOMY = pltpu.CompilerParams(vmem_limit_bytes=60 * 1024 * 1024)
PARAMS = pltpu.CompilerParams(vmem_limit_bytes=8 * 1024 * 1024)


def slot_targets(owners, slot_count):
    block_count = owners.shape[0]
    same_owner = owners[:, None] == owners[None, :]
    earlier = lax.broadcasted_iota(jnp.int32, (block_count, block_count), 1) < lax.broadcasted_iota(
        jnp.int32, (block_count, block_count), 0
    )
    ranked = jnp.sum(jnp.where(same_owner & earlier, 1, 0), axis=1).astype(jnp.int32)
    return owners * slot_count + ranked


def ring(count, step):
    return [(i, (i + step) % count) for i in range(count)]


def iota(shape, dim):
    return lax.broadcasted_iota(jnp.int32, shape, dim)


def dot(a, b, dims=((1,), (0,))):
    return lax.dot_general(a, b, (dims, ((), ())), preferred_element_type=WIDE)


def prepare(activations, out_grads, place):
    block_rows, rows, toks = activations.shape
    per_z = rows // NZ
    count = block_rows * rows // 2
    half = toks // NC
    width = out_grads.shape[1] // NX
    tile = width // TILES

    def kernel(place_ref, a_ref, b_ref, *refs):
        out_refs, (held, sems, out_sems) = refs[:3], refs[3:]
        z, c = place_ref[0], place_ref[2]
        tok = pl.ds(pl.multiple_of(c * half, half), half)
        copies = []
        for i in range(3):
            begin = place_ref[3 + i] * width
            for n in range(TILES):
                at = pl.ds(pl.multiple_of(begin + n * tile, tile), tile)
                to = pl.ds(2 * count + n * half, half)
                copies.append(pltpu.make_async_copy(b_ref.at[tok, at], held.at[i, to, :], sems.at[i, n]))
        for copy in copies:
            copy.start()
        m, k = iota((count, 2 * count), 0), iota((count, 2 * count), 1)
        block = m % block_rows
        row = (m // block_rows) % per_z
        tail = m // (block_rows * per_z)
        high = 2 * (tail // 4) + 4 * ((tail // 2) % 2) + 8 * (tail % 2)
        values = a_ref[...].reshape(2 * count, toks)
        for odd in range(2):
            goal = jnp.bitwise_and(z + (1 - 2 * c) * (high + odd), NZ - 1)
            pick = (block * rows + goal * per_z + row == k).astype(WIDE).astype(HALF)
            moved = dot(pick, values).astype(HALF)
            turned = jnp.concatenate([moved[:, half:], moved[:, :half]], axis=1)
            at = (1 - odd) * count
            ordered = jnp.where(c == 1, turned, moved)
            for i in range(3):
                held[i, at : at + count, :] = ordered
        last = [pltpu.make_async_copy(held.at[i], out_refs[i], out_sems.at[i]) for i in range(3)]
        for i in range(3):
            for copy in copies[i * TILES : (i + 1) * TILES]:
                copy.wait()
            last[i].start()
        for copy in last:
            copy.wait()

    piece = (2 * count + TILES * half, toks)
    any_place = pl.BlockSpec(memory_space=pl.ANY)
    return pl.pallas_call(
        kernel,
        out_shape=[jax.ShapeDtypeStruct(piece, HALF)] * 3,
        in_specs=[
            pl.BlockSpec(memory_space=pltpu.SMEM),
            pl.BlockSpec(memory_space=pltpu.VMEM),
            any_place,
        ],
        out_specs=[any_place] * 3,
        scratch_shapes=[
            pltpu.VMEM((3, *piece), HALF),
            pltpu.SemaphoreType.DMA((3, TILES)),
            pltpu.SemaphoreType.DMA((3,)),
        ],
        compiler_params=ROOMY,
    )(place, activations, out_grads)


def own_part(piece, out_grads, place):
    toks = out_grads.shape[0]
    half = toks // NC
    width = out_grads.shape[1] // NX
    tile = width // TILES
    count = piece.shape[0] - TILES * half

    def kernel(place_ref, p_ref, b_ref, o_ref):
        c = place_ref[2]
        o_ref[:count, :] = p_ref[...]
        for n in range(TILES):
            for side, who in enumerate((c, 1 - c)):
                at = count + (2 * n + side) * half
                tok = pl.ds(pl.multiple_of(who * half, half), half)
                o_ref[at : at + half, :] = b_ref[tok, n * tile : (n + 1) * tile]

    own = (count + TILES * toks, tile)
    return pl.pallas_call(
        kernel,
        out_shape=jax.ShapeDtypeStruct(own, HALF),
        grid_spec=pltpu.PrefetchScalarGridSpec(
            num_scalar_prefetch=1,
            grid=(1,),
            in_specs=[
                pl.BlockSpec((count, tile), lambda i, place_ref: (0, 0)),
                pl.BlockSpec((toks, width), lambda i, place_ref: (0, place_ref[1])),
            ],
            out_specs=pl.BlockSpec(own, lambda i, place_ref: (0, 0)),
        ),
        compiler_params=ROOMY,
    )(place, piece, out_grads)


def partial_products(own, arrived, swapped, odd):
    toks = own.shape[1]
    half = toks // NC
    total_rows = own.shape[0] - TILES * toks
    count = total_rows // 2
    kind = HALF if odd else WIDE
    group = 2

    def kernel(*refs):
        rows_refs, own_ref, mine, other, out_ref = refs[:4], refs[4], refs[5:8], refs[8:11], refs[11]
        for n in range(group):
            at = slice(n * half, (n + 1) * half)
            total = dot(rows_refs[0][...], own_ref[n * toks : (n + 1) * toks, :])
            for rows_ref, m_ref, o_ref in zip(rows_refs[1:], mine, other):
                total += dot(rows_ref[...], jnp.concatenate([m_ref[at, :], o_ref[at, :]], axis=0))
            to = slice(n * toks, (n + 1) * toks)
            out_ref[:, to] = total.astype(kind)

    rows = pl.BlockSpec((count, toks), lambda n: (0 if odd else 1, 0))
    columns = pl.BlockSpec((group * half, toks), lambda n: (total_rows // (group * half) + n, 0))
    own_columns = pl.BlockSpec((group * toks, toks), lambda n: (total_rows // (group * toks) + n, 0))
    return pl.pallas_call(
        kernel,
        grid=(TILES // group,),
        out_shape=jax.ShapeDtypeStruct((count, TILES * toks), kind),
        in_specs=[rows] * 4 + [own_columns] + [columns] * 6,
        out_specs=pl.BlockSpec((count, group * toks), lambda n: (0, n)),
        compiler_params=PARAMS,
    )(own, *arrived, own, *arrived, *swapped)


def pick_blocks(chosen, sums, block_size):
    sources, rows, width = sums.shape
    columns = width // block_size
    out_rows = chosen.shape[0]
    tile = out_rows // 2

    def kernel(p_ref, s_ref, o_ref):
        total = None
        for pair in range(sources // 2):
            depth = 2 * columns * rows
            pieces = [
                s_ref[x, :, j * block_size : (j + 1) * block_size]
                for x in (2 * pair, 2 * pair + 1)
                for j in range(columns)
            ]
            term = dot(p_ref[:, pair * depth : (pair + 1) * depth], jnp.concatenate(pieces, axis=0))
            total = term if total is None else total + term
        o_ref[...] = total.astype(HALF)

    return pl.pallas_call(
        kernel,
        grid=(2,),
        out_shape=jax.ShapeDtypeStruct((out_rows, block_size), HALF),
        in_specs=[
            pl.BlockSpec((tile, chosen.shape[1]), lambda n: (n, 0)),
            pl.BlockSpec(sums.shape, lambda n: (0, 0, 0)),
        ],
        out_specs=pl.BlockSpec((tile, block_size), lambda n: (n, 0)),
        compiler_params=PARAMS,
    )(chosen, sums)


def finish_sum(limits, pieces, acc):
    slots, rows, block_size = acc.shape
    per_z = rows // NZ
    total_rows = slots * rows
    piece_rows = pieces.shape[0]

    def kernel(lim_ref, p_ref, a_ref, g_ref, n_ref):
        m, k = iota((total_rows, piece_rows), 0), iota((total_rows, piece_rows), 1)
        row = k % per_z
        piece = (k // per_z) % 2
        slot = (k // (2 * per_z)) % slots
        source = k // (2 * per_z * slots)
        goal = jnp.bitwise_and(source + 8 * piece, NZ - 1)
        adds = (slot * rows + goal * per_z + row == m).astype(WIDE).astype(HALF)
        grad = dot(adds, p_ref[...])
        lane = iota((16, block_size), 1)
        extra_row = iota((16, block_size), 0)
        extra = jnp.zeros((16, block_size), WIDE)
        for s in range(slots):
            live = iota((rows, block_size), 0) < lim_ref[s]
            own = jnp.where(live, grad[s * rows : (s + 1) * rows], 0.0)
            new = a_ref[s] + own * own
            n_ref[s] = new
            grafted = own / (jnp.sqrt(new) + GRAFT_EPS)
            norm = jnp.sum(jnp.sum(grafted * grafted, axis=0, keepdims=True), axis=1, keepdims=True)
            high = norm.astype(HALF).astype(WIDE)
            middle = (norm - high).astype(HALF).astype(WIDE)
            low = norm - high - middle
            spread = jnp.where(lane == 0, high, jnp.where(lane == 1, middle, jnp.where(lane == 2, low, 0.0)))
            extra = jnp.where(extra_row == s, spread, extra)
            g_ref[s * rows : (s + 1) * rows, :] = own.astype(HALF)
        g_ref[total_rows:, :] = extra.astype(HALF)

    vmem = pl.BlockSpec(memory_space=pltpu.VMEM)
    return pl.pallas_call(
        kernel,
        out_shape=[
            jax.ShapeDtypeStruct((total_rows + 16, block_size), HALF),
            jax.ShapeDtypeStruct(acc.shape, WIDE),
        ],
        in_specs=[pl.BlockSpec(memory_space=pltpu.SMEM), vmem, vmem],
        out_specs=[vmem, vmem],
        compiler_params=PARAMS,
    )(limits, pieces, acc)


def update(facts, mine, other, roots_mine, roots_other, left_stat, right_stat):
    ny = mine.shape[0]
    slots, rows, block_size = left_stat.shape
    all_rows = mine.shape[1]

    def kernel(f_ref, m_ref, o_ref, rm_ref, ro_ref, ls_ref, rs_ref, ln_ref, rn_ref, d_ref, roots):
        s = pl.program_id(0)
        core, own_y, own_mp = f_ref[0], f_ref[1], f_ref[2]
        live, taken = f_ref[3 + s], f_ref[5 + s]
        at = pl.ds(pl.multiple_of(s * rows, rows), rows)
        for i in range(ny):
            source = jnp.bitwise_xor(own_y, i) * NC
            for ref, who in ((rm_ref, core), (ro_ref, 1 - core)):
                to = pl.ds(pl.multiple_of((source + who) * rows, rows), rows)
                for kind in range(2):
                    roots[kind, to, :] = ref[i, kind, 0]
        parts = []
        norm = jnp.zeros((1, 1), WIDE)
        tail_row = iota((16, block_size), 0) == s
        for y in range(ny):
            a, b = m_ref[y, at, :], o_ref[y, at, :]
            parts += [jnp.where(core == 0, a, b), jnp.where(core == 0, b, a)]
            for ref in (m_ref, o_ref):
                tail = jnp.where(tail_row, ref[y, slots * rows : all_rows, :].astype(WIDE), 0.0)
                norm += jnp.sum(jnp.sum(tail, axis=0, keepdims=True), axis=1, keepdims=True)
        grad = jnp.concatenate(parts, axis=0)
        prod = dot(grad, roots[1], ((1,), (1,))).astype(HALF)
        raw = dot(roots[0], prod)
        raw = jnp.where(iota(raw.shape, 0) < live, raw, 0.0)
        raw_sq = jnp.sum(jnp.sum(raw * raw, axis=0, keepdims=True), axis=1, keepdims=True)
        factor = jnp.sqrt(norm) / jnp.sqrt(raw_sq + GRAFT_EPS)
        d_ref[0] = jnp.where(taken == 1, factor * raw, 0.0).astype(HALF)
        own = m_ref[own_y, at, :]
        left_cols = dot(own, grad, ((1,), (1,)))
        own_columns = (iota((block_size, rows), 0) == own_mp * rows + iota((block_size, rows), 1)).astype(WIDE)
        columns = dot(grad, own_columns.astype(HALF)).astype(HALF)
        right_rows = dot(columns, grad, ((0,), (0,)))
        for old_ref, value, new_ref in ((ls_ref, left_cols, ln_ref), (rs_ref, right_rows, rn_ref)):
            old = old_ref[0]
            fresh = STAT_DECAY * old + (1.0 - STAT_DECAY) * value / block_size
            new_ref[0] = jnp.where(taken == 1, fresh, old)

    whole = pl.BlockSpec((ny, all_rows, block_size), lambda s: (0, 0, 0))
    square = pl.BlockSpec((1, block_size, block_size), lambda s: (s, 0, 0))
    strip = pl.BlockSpec((1, rows, block_size), lambda s: (s, 0, 0))
    return pl.pallas_call(
        kernel,
        grid=(slots,),
        out_shape=[
            jax.ShapeDtypeStruct(left_stat.shape, WIDE),
            jax.ShapeDtypeStruct(right_stat.shape, WIDE),
            jax.ShapeDtypeStruct((slots, block_size, block_size), HALF),
        ],
        in_specs=[pl.BlockSpec(memory_space=pltpu.SMEM), whole, whole]
        + [pl.BlockSpec((ny, 2, 1, rows, block_size), lambda s: (0, 0, s, 0, 0))] * 2
        + [strip, strip],
        out_specs=[strip, strip, square],
        scratch_shapes=[pltpu.VMEM((2, block_size, block_size), HALF)],
        compiler_params=PARAMS,
    )(facts, mine, other, roots_mine, roots_other, left_stat, right_stat)


def body(
    activations,
    out_grads,
    owners,
    live_rows,
    left_stat,
    right_stat,
    left_root,
    right_root,
    grad_acc,
):
    z, x, y, c = (lax.axis_index(name) for name in ("z", "x", "y", "c"))
    block_rows, rows, toks = activations.shape
    block_size = left_stat.shape[3]
    slots = left_stat.shape[1]
    block_count = owners.shape[0]
    per_z = rows // NZ
    columns = out_grads.shape[1] // block_size // NX
    my_owner = z * NX + x
    my_mp = y * NC + c
    my_rows = my_mp * rows

    place = jnp.stack([z, x, c] + [jnp.bitwise_and(x + step, NX - 1) for step in (3, 2, 1)]).astype(jnp.int32)
    pieces = prepare(activations, out_grads, place)
    arrived = [lax.ppermute(piece, "x", ring(NX, step)) for piece, step in zip(pieces, (-1, 2, 1))]

    piece_own, owners = lax.optimization_barrier((pieces[0], owners))
    targets = slot_targets(owners, slots)
    by_block = targets.reshape(block_rows, NX, columns).transpose(1, 2, 0)[:, :, None, None, :]
    shape = (NX, columns, 2, per_z, block_rows)
    owner = by_block // slots
    code = (((owner // NX) * slots + by_block % slots) * 2 + iota(shape, 2)) * per_z + iota(shape, 3)
    code = jnp.where(owner % NX == x, code, -1).reshape(1, -1)
    out_rows = NZ * slots * 2 * per_z
    chosen = (code == iota((out_rows, 1), 0)).astype(HALF)
    piece_own, chosen = lax.optimization_barrier((piece_own, chosen))
    own = own_part(piece_own, out_grads, place)

    own, left_root, right_root = lax.optimization_barrier((own, left_root, right_root))
    ny = lax.axis_size("y")
    roots = jnp.stack([left_root[0], right_root[0]])[None]
    for step in (1, 2):
        if step < ny:
            came = lax.ppermute(roots, "y", [(i, i ^ step) for i in range(ny)])
            roots = jnp.concatenate([roots, came], axis=0)
    own, roots = lax.optimization_barrier((own, roots))
    swapped = [lax.ppermute(piece, "c", ring(NC, 1)) for piece in arrived]
    roots_other = lax.ppermute(roots, "c", ring(NC, 1))

    sent = partial_products(own, arrived, swapped, True)
    kept = partial_products(own, arrived, swapped, False)

    got = []
    for step in (1, 2, 4):
        goals = [((i + (1 - 2 * k) * step) % NZ) * NC + k for i in range(NZ) for k in range(NC)]
        got.append(lax.ppermute(sent, ("z", "c"), list(enumerate(goals))))
        part = got[-1].shape[0] // (2 if step < 4 else 1)
        rows_from = slice(part, 2 * part) if step < 4 else slice(0, part)
        total = kept[rows_from]
        for rows_in in got:
            total = total + rows_in[rows_from]
        sent = total.astype(HALF)
    sums = lax.all_gather(sent, "x", axis=0, tiled=False)

    picked = pick_blocks(chosen, sums, block_size).reshape(NZ, out_rows // NZ, block_size)
    arrived = lax.all_to_all(picked, "z", 0, 0, tiled=True).reshape(out_rows, block_size)

    wanted = my_owner * slots + iota((slots, block_count), 0)
    matched = targets[None, :] == wanted
    occupied = jnp.any(matched, axis=1).astype(jnp.int32)
    live_mine = jnp.sum(jnp.where(matched, live_rows[None, :], 0), axis=1).astype(jnp.int32)
    own_rows, acc_next = finish_sum(live_mine - my_rows, arrived, grad_acc[0])
    rows_mine = lax.all_gather(own_rows, "y", axis=0, tiled=False)
    rows_other = lax.ppermute(rows_mine, "c", ring(NC, 1))
    facts = jnp.concatenate([jnp.stack([c, y, my_mp]).astype(jnp.int32), live_mine, occupied])
    left_next, right_next, directions = update(
        facts, rows_mine, rows_other, roots, roots_other, left_stat[0], right_stat[0]
    )
    return (left_next[None], right_next[None], acc_next[None], directions[None])


def solution(mesh):
    dp, mp = mesh.devices.shape
    parts = Mesh(mesh.devices.reshape(NZ, NX, mp // NC, NC), ("z", "x", "y", "c"))
    owner, strip = ("z", "x"), ("y", "c")
    state = P(owner, None, strip, None)
    return jax.shard_map(
        body,
        mesh=parts,
        in_specs=(P(None, strip, owner), P(owner, None), P(), P(), state, state, state, state, state),
        out_specs=(state, state, state, P(owner, None, None, None)),
        check_vma=False,
    )
```

```python
import jax
import jax.numpy as jnp
from jax import lax
from jax.experimental import pallas as pl
from jax.experimental.pallas import tpu as pltpu
from jax.sharding import Mesh, PartitionSpec as P

STAT_DECAY = 0.9
GRAFT_EPS = 1e-06
HALF = jnp.bfloat16
WIDE = jnp.float32
NZ, NX, NC = 16, 4, 2
NL = 4
TILES = 6
ROOMY = pltpu.CompilerParams(vmem_limit_bytes=60 * 1024 * 1024)
PARAMS = pltpu.CompilerParams(vmem_limit_bytes=8 * 1024 * 1024)


def slot_targets(owners, slot_count):
    block_count = owners.shape[0]
    same_owner = owners[:, None] == owners[None, :]
    earlier = lax.broadcasted_iota(jnp.int32, (block_count, block_count), 1) < lax.broadcasted_iota(
        jnp.int32, (block_count, block_count), 0
    )
    ranked = jnp.sum(jnp.where(same_owner & earlier, 1, 0), axis=1).astype(jnp.int32)
    return owners * slot_count + ranked


def ring(count, step):
    return [(i, (i + step) % count) for i in range(count)]


def iota(shape, dim):
    return lax.broadcasted_iota(jnp.int32, shape, dim)


def dot(a, b, dims=((1,), (0,))):
    return lax.dot_general(a, b, (dims, ((), ())), preferred_element_type=WIDE)


def prepare(activations, out_grads, place):
    block_rows, rows, toks = activations.shape
    per_z = rows // NZ
    count = block_rows * rows // 2
    half = toks // NC
    width = out_grads.shape[1] // NX
    tile = width // TILES

    def kernel(place_ref, a_ref, b_ref, *refs):
        out_refs, (held, sems, out_sems) = refs[:3], refs[3:]
        z, c = place_ref[0], place_ref[2]
        tok = pl.ds(pl.multiple_of(c * half, half), half)
        copies = []
        for i in range(3):
            begin = place_ref[3 + i] * width
            for n in range(TILES):
                at = pl.ds(pl.multiple_of(begin + n * tile, tile), tile)
                to = pl.ds(2 * count + n * half, half)
                copies.append(pltpu.make_async_copy(b_ref.at[tok, at], held.at[i, to, :], sems.at[i, n]))
        for copy in copies:
            copy.start()
        m, k = iota((count, 2 * count), 0), iota((count, 2 * count), 1)
        block = m % block_rows
        row = (m // block_rows) % per_z
        tail = m // (block_rows * per_z)
        high = 2 * (tail // 4) + 4 * ((tail // 2) % 2) + 8 * (tail % 2)
        values = a_ref[...].reshape(2 * count, toks)
        for odd in range(2):
            goal = jnp.bitwise_and(z + (1 - 2 * c) * (high + odd), NZ - 1)
            pick = (block * rows + goal * per_z + row == k).astype(WIDE).astype(HALF)
            moved = dot(pick, values).astype(HALF)
            turned = jnp.concatenate([moved[:, half:], moved[:, :half]], axis=1)
            at = (1 - odd) * count
            ordered = jnp.where(c == 1, turned, moved)
            for i in range(3):
                held[i, at : at + count, :] = ordered
        last = [pltpu.make_async_copy(held.at[i], out_refs[i], out_sems.at[i]) for i in range(3)]
        for i in range(3):
            for copy in copies[i * TILES : (i + 1) * TILES]:
                copy.wait()
            last[i].start()
        for copy in last:
            copy.wait()

    piece = (2 * count + TILES * half, toks)
    any_place = pl.BlockSpec(memory_space=pl.ANY)
    return pl.pallas_call(
        kernel,
        out_shape=[jax.ShapeDtypeStruct(piece, HALF)] * 3,
        in_specs=[
            pl.BlockSpec(memory_space=pltpu.SMEM),
            pl.BlockSpec(memory_space=pltpu.VMEM),
            any_place,
        ],
        out_specs=[any_place] * 3,
        scratch_shapes=[
            pltpu.VMEM((3, *piece), HALF),
            pltpu.SemaphoreType.DMA((3, TILES)),
            pltpu.SemaphoreType.DMA((3,)),
        ],
        compiler_params=ROOMY,
    )(place, activations, out_grads)


def own_part(piece, out_grads, place):
    toks = out_grads.shape[0]
    half = toks // NC
    width = out_grads.shape[1] // NX
    tile = width // TILES
    count = piece.shape[0] - TILES * half

    def kernel(place_ref, p_ref, b_ref, o_ref):
        c = place_ref[2]
        o_ref[:count, :] = p_ref[...]
        for n in range(TILES):
            for side, who in enumerate((c, 1 - c)):
                at = count + (2 * n + side) * half
                tok = pl.ds(pl.multiple_of(who * half, half), half)
                o_ref[at : at + half, :] = b_ref[tok, n * tile : (n + 1) * tile]

    own = (count + TILES * toks, tile)
    return pl.pallas_call(
        kernel,
        out_shape=jax.ShapeDtypeStruct(own, HALF),
        grid_spec=pltpu.PrefetchScalarGridSpec(
            num_scalar_prefetch=1,
            grid=(1,),
            in_specs=[
                pl.BlockSpec((count, tile), lambda i, place_ref: (0, 0)),
                pl.BlockSpec((toks, width), lambda i, place_ref: (0, place_ref[1])),
            ],
            out_specs=pl.BlockSpec(own, lambda i, place_ref: (0, 0)),
        ),
        compiler_params=ROOMY,
    )(place, piece, out_grads)


def partial_products(own, arrived, swapped, odd):
    toks = own.shape[1]
    half = toks // NC
    total_rows = own.shape[0] - TILES * toks
    count = total_rows // 2
    kind = HALF if odd else WIDE
    group = 2

    def kernel(*refs):
        rows_refs, own_ref, mine, other, out_ref = refs[:4], refs[4], refs[5:8], refs[8:11], refs[11]
        for n in range(group):
            at = slice(n * half, (n + 1) * half)
            total = dot(rows_refs[0][...], own_ref[n * toks : (n + 1) * toks, :])
            for rows_ref, m_ref, o_ref in zip(rows_refs[1:], mine, other):
                total += dot(rows_ref[...], jnp.concatenate([m_ref[at, :], o_ref[at, :]], axis=0))
            to = slice(n * toks, (n + 1) * toks)
            out_ref[:, to] = total.astype(kind)

    rows = pl.BlockSpec((count, toks), lambda n: (0 if odd else 1, 0))
    columns = pl.BlockSpec((group * half, toks), lambda n: (total_rows // (group * half) + n, 0))
    own_columns = pl.BlockSpec((group * toks, toks), lambda n: (total_rows // (group * toks) + n, 0))
    return pl.pallas_call(
        kernel,
        grid=(TILES // group,),
        out_shape=jax.ShapeDtypeStruct((count, TILES * toks), kind),
        in_specs=[rows] * 4 + [own_columns] + [columns] * 6,
        out_specs=pl.BlockSpec((count, group * toks), lambda n: (0, n)),
        compiler_params=PARAMS,
    )(own, *arrived, own, *arrived, *swapped)


def pick_blocks(chosen, sums, block_size):
    sources, rows, width = sums.shape
    columns = width // block_size
    out_rows = chosen.shape[0]
    tile = out_rows // 2

    def kernel(p_ref, s_ref, o_ref):
        total = None
        for pair in range(sources // 2):
            depth = 2 * columns * rows
            pieces = [
                s_ref[x, :, j * block_size : (j + 1) * block_size]
                for x in (2 * pair, 2 * pair + 1)
                for j in range(columns)
            ]
            term = dot(p_ref[:, pair * depth : (pair + 1) * depth], jnp.concatenate(pieces, axis=0))
            total = term if total is None else total + term
        o_ref[...] = total.astype(HALF)

    return pl.pallas_call(
        kernel,
        grid=(2,),
        out_shape=jax.ShapeDtypeStruct((out_rows, block_size), HALF),
        in_specs=[
            pl.BlockSpec((tile, chosen.shape[1]), lambda n: (n, 0)),
            pl.BlockSpec(sums.shape, lambda n: (0, 0, 0)),
        ],
        out_specs=pl.BlockSpec((tile, block_size), lambda n: (n, 0)),
        compiler_params=PARAMS,
    )(chosen, sums)


def finish_sum(limits, pieces, acc):
    slots, rows, block_size = acc.shape
    per_z = rows // NZ
    total_rows = slots * rows
    piece_rows = pieces.shape[0]

    def kernel(lim_ref, p_ref, a_ref, g_ref, n_ref):
        m, k = iota((total_rows, piece_rows), 0), iota((total_rows, piece_rows), 1)
        row = k % per_z
        piece = (k // per_z) % 2
        slot = (k // (2 * per_z)) % slots
        source = k // (2 * per_z * slots)
        goal = jnp.bitwise_and(source + 8 * piece, NZ - 1)
        adds = (slot * rows + goal * per_z + row == m).astype(WIDE).astype(HALF)
        grad = dot(adds, p_ref[...])
        lane = iota((16, block_size), 1)
        extra_row = iota((16, block_size), 0)
        extra = jnp.zeros((16, block_size), WIDE)
        for s in range(slots):
            live = iota((rows, block_size), 0) < lim_ref[s]
            own = jnp.where(live, grad[s * rows : (s + 1) * rows], 0.0)
            new = a_ref[s] + own * own
            n_ref[s] = new
            grafted = own / (jnp.sqrt(new) + GRAFT_EPS)
            norm = jnp.sum(jnp.sum(grafted * grafted, axis=0, keepdims=True), axis=1, keepdims=True)
            high = norm.astype(HALF).astype(WIDE)
            middle = (norm - high).astype(HALF).astype(WIDE)
            low = norm - high - middle
            spread = jnp.where(lane == 0, high, jnp.where(lane == 1, middle, jnp.where(lane == 2, low, 0.0)))
            extra = jnp.where(extra_row == s, spread, extra)
            g_ref[s * rows : (s + 1) * rows, :] = own.astype(HALF)
        g_ref[total_rows:, :] = extra.astype(HALF)

    vmem = pl.BlockSpec(memory_space=pltpu.VMEM)
    return pl.pallas_call(
        kernel,
        out_shape=[
            jax.ShapeDtypeStruct((total_rows + 16, block_size), HALF),
            jax.ShapeDtypeStruct(acc.shape, WIDE),
        ],
        in_specs=[pl.BlockSpec(memory_space=pltpu.SMEM), vmem, vmem],
        out_specs=[vmem, vmem],
        compiler_params=PARAMS,
    )(limits, pieces, acc)


def update(facts, mine, other, roots_mine, roots_other, left_stat, right_stat):
    ny = mine.shape[0]
    slots, rows, block_size = left_stat.shape
    all_rows = mine.shape[1]

    def kernel(f_ref, m_ref, o_ref, rm_ref, ro_ref, ls_ref, rs_ref, ln_ref, rn_ref, d_ref, roots):
        s = pl.program_id(0)
        core, own_y, own_mp = f_ref[0], f_ref[1], f_ref[2]
        live, taken = f_ref[3 + s], f_ref[5 + s]
        at = pl.ds(pl.multiple_of(s * rows, rows), rows)
        for i in range(ny):
            source = jnp.bitwise_xor(own_y, i) * NC
            for ref, who in ((rm_ref, core), (ro_ref, 1 - core)):
                to = pl.ds(pl.multiple_of((source + who) * rows, rows), rows)
                for kind in range(2):
                    roots[kind, to, :] = ref[i, kind, 0]
        parts = []
        norm = jnp.zeros((1, 1), WIDE)
        tail_row = iota((16, block_size), 0) == s
        for y in range(ny):
            a, b = m_ref[y, at, :], o_ref[y, at, :]
            parts += [jnp.where(core == 0, a, b), jnp.where(core == 0, b, a)]
            for ref in (m_ref, o_ref):
                tail = jnp.where(tail_row, ref[y, slots * rows : all_rows, :].astype(WIDE), 0.0)
                norm += jnp.sum(jnp.sum(tail, axis=0, keepdims=True), axis=1, keepdims=True)
        grad = jnp.concatenate(parts, axis=0)
        prod = dot(grad, roots[1], ((1,), (1,))).astype(HALF)
        raw = dot(roots[0], prod)
        raw = jnp.where(iota(raw.shape, 0) < live, raw, 0.0)
        raw_sq = jnp.sum(jnp.sum(raw * raw, axis=0, keepdims=True), axis=1, keepdims=True)
        factor = jnp.sqrt(norm) / jnp.sqrt(raw_sq + GRAFT_EPS)
        d_ref[0] = jnp.where(taken == 1, factor * raw, 0.0).astype(HALF)
        own = m_ref[own_y, at, :]
        left_cols = dot(own, grad, ((1,), (1,)))
        own_columns = (iota((block_size, rows), 0) == own_mp * rows + iota((block_size, rows), 1)).astype(WIDE)
        columns = dot(grad, own_columns.astype(HALF)).astype(HALF)
        right_rows = dot(columns, grad, ((0,), (0,)))
        for old_ref, value, new_ref in ((ls_ref, left_cols, ln_ref), (rs_ref, right_rows, rn_ref)):
            old = old_ref[0]
            fresh = STAT_DECAY * old + (1.0 - STAT_DECAY) * value / block_size
            new_ref[0] = jnp.where(taken == 1, fresh, old)

    whole = pl.BlockSpec((ny, all_rows, block_size), lambda s: (0, 0, 0))
    square = pl.BlockSpec((1, block_size, block_size), lambda s: (s, 0, 0))
    strip = pl.BlockSpec((1, rows, block_size), lambda s: (s, 0, 0))
    return pl.pallas_call(
        kernel,
        grid=(slots,),
        out_shape=[
            jax.ShapeDtypeStruct(left_stat.shape, WIDE),
            jax.ShapeDtypeStruct(right_stat.shape, WIDE),
            jax.ShapeDtypeStruct((slots, block_size, block_size), HALF),
        ],
        in_specs=[pl.BlockSpec(memory_space=pltpu.SMEM), whole, whole]
        + [pl.BlockSpec((ny, 2, 1, rows, block_size), lambda s: (0, 0, s, 0, 0))] * 2
        + [strip, strip],
        out_specs=[strip, strip, square],
        scratch_shapes=[pltpu.VMEM((2, block_size, block_size), HALF)],
        compiler_params=PARAMS,
    )(facts, mine, other, roots_mine, roots_other, left_stat, right_stat)


def body(
    activations,
    out_grads,
    owners,
    live_rows,
    left_stat,
    right_stat,
    left_root,
    right_root,
    grad_acc,
):
    zh, zl, x, y, c = (lax.axis_index(name) for name in ("zh", "zl", "x", "y", "c"))
    z = zh * NL + zl
    block_rows, rows, toks = activations.shape
    block_size = left_stat.shape[3]
    slots = left_stat.shape[1]
    block_count = owners.shape[0]
    per_z = rows // NZ
    columns = out_grads.shape[1] // block_size // NX
    my_owner = z * NX + x
    my_mp = y * NC + c
    my_rows = my_mp * rows

    place = jnp.stack([z, x, c] + [jnp.bitwise_and(x + step, NX - 1) for step in (3, 2, 1)]).astype(jnp.int32)
    pieces = prepare(activations, out_grads, place)
    arrived = [lax.ppermute(piece, "x", ring(NX, step)) for piece, step in zip(pieces, (-1, 2, 1))]

    piece_own, owners = lax.optimization_barrier((pieces[0], owners))
    targets = slot_targets(owners, slots)
    by_block = targets.reshape(block_rows, NX, columns).transpose(1, 2, 0)[:, :, None, None, :]
    shape = (NX, columns, 2, per_z, block_rows)
    owner = by_block // slots
    owner_z = owner // NX
    owner_z = owner_z % NL * (NZ // NL) + owner_z // NL
    code = ((owner_z * slots + by_block % slots) * 2 + iota(shape, 2)) * per_z + iota(shape, 3)
    code = jnp.where(owner % NX == x, code, -1).reshape(1, -1)
    out_rows = NZ * slots * 2 * per_z
    chosen = (code == iota((out_rows, 1), 0)).astype(HALF)
    piece_own, chosen = lax.optimization_barrier((piece_own, chosen))
    own = own_part(piece_own, out_grads, place)

    own, left_root, right_root = lax.optimization_barrier((own, left_root, right_root))
    ny = lax.axis_size("y")
    roots = jnp.stack([left_root[0], right_root[0]])[None]
    for step in (1, 2):
        if step < ny:
            came = lax.ppermute(roots, "y", [(i, i ^ step) for i in range(ny)])
            roots = jnp.concatenate([roots, came], axis=0)
    own, roots = lax.optimization_barrier((own, roots))
    swapped = [lax.ppermute(piece, "c", ring(NC, 1)) for piece in arrived]
    roots_other = lax.ppermute(roots, "c", ring(NC, 1))

    sent = partial_products(own, arrived, swapped, True)
    kept = partial_products(own, arrived, swapped, False)

    got = []
    for step in (1, 2, 4):
        goals = [((i + (1 - 2 * k) * step) % NZ) * NC + k for i in range(NZ) for k in range(NC)]
        got.append(lax.ppermute(sent, ("zh", "zl", "c"), list(enumerate(goals))))
        part = got[-1].shape[0] // (2 if step < 4 else 1)
        rows_from = slice(part, 2 * part) if step < 4 else slice(0, part)
        total = kept[rows_from]
        for rows_in in got:
            total = total + rows_in[rows_from]
        sent = total.astype(HALF)
    sums = lax.all_gather(sent, "x", axis=0, tiled=False)

    picked = pick_blocks(chosen, sums, block_size).reshape(NL, NZ // NL, out_rows // NZ, block_size)
    picked = lax.all_to_all(picked, "zl", 0, 0, tiled=True).transpose(1, 0, 2, 3)
    arrived = lax.all_to_all(picked, "zh", 0, 0, tiled=True).reshape(out_rows, block_size)

    wanted = my_owner * slots + iota((slots, block_count), 0)
    matched = targets[None, :] == wanted
    occupied = jnp.any(matched, axis=1).astype(jnp.int32)
    live_mine = jnp.sum(jnp.where(matched, live_rows[None, :], 0), axis=1).astype(jnp.int32)
    own_rows, acc_next = finish_sum(live_mine - my_rows, arrived, grad_acc[0])
    rows_mine = lax.all_gather(own_rows, "y", axis=0, tiled=False)
    rows_other = lax.ppermute(rows_mine, "c", ring(NC, 1))
    facts = jnp.concatenate([jnp.stack([c, y, my_mp]).astype(jnp.int32), live_mine, occupied])
    left_next, right_next, directions = update(
        facts, rows_mine, rows_other, roots, roots_other, left_stat[0], right_stat[0]
    )
    return (left_next[None], right_next[None], acc_next[None], directions[None])


def solution(mesh):
    mp = mesh.devices.shape[1]
    names = ("zh", "zl", "x", "y", "c")
    parts = Mesh(mesh.devices.reshape(NZ // NL, NL, NX, mp // NC, NC), names)
    owner, strip = names[:3], names[3:]
    state = P(owner, None, strip, None)
    return jax.shard_map(
        body,
        mesh=parts,
        in_specs=(P(None, strip, owner), P(owner, None), P(), P(), state, state, state, state, state),
        out_specs=(state, state, state, P(owner, None, None, None)),
        check_vma=False,
    )
```

```python
import jax
import jax.numpy as jnp
from jax import lax
from jax.experimental import pallas as pl
from jax.experimental.pallas import tpu as pltpu
from jax.sharding import Mesh, PartitionSpec as P

STAT_DECAY = 0.9
GRAFT_EPS = 1e-06
HALF = jnp.bfloat16
WIDE = jnp.float32
NZ, NX, NC = 16, 4, 2
TILES = 6
CHUNKS = 2
ROOMY = pltpu.CompilerParams(vmem_limit_bytes=60 * 1024 * 1024)
PARAMS = pltpu.CompilerParams(vmem_limit_bytes=8 * 1024 * 1024)


def slot_targets(owners, slot_count):
    block_count = owners.shape[0]
    same_owner = owners[:, None] == owners[None, :]
    earlier = lax.broadcasted_iota(jnp.int32, (block_count, block_count), 1) < lax.broadcasted_iota(
        jnp.int32, (block_count, block_count), 0
    )
    ranked = jnp.sum(jnp.where(same_owner & earlier, 1, 0), axis=1).astype(jnp.int32)
    return owners * slot_count + ranked


def ring(count, step):
    return [(i, (i + step) % count) for i in range(count)]


def iota(shape, dim):
    return lax.broadcasted_iota(jnp.int32, shape, dim)


def dot(a, b, dims=((1,), (0,))):
    return lax.dot_general(a, b, (dims, ((), ())), preferred_element_type=WIDE)


def prepare(activations, out_grads, place):
    block_rows, rows, toks = activations.shape
    per_z = rows // NZ
    count = block_rows * rows // 2
    half = toks // NC
    width = out_grads.shape[1] // NX
    tile = width // TILES

    def kernel(place_ref, a_ref, b_ref, *refs):
        out_refs, (held, sems, out_sems) = refs[:3], refs[3:]
        z, c = place_ref[0], place_ref[2]
        tok = pl.ds(pl.multiple_of(c * half, half), half)
        copies = []
        for i in range(3):
            begin = place_ref[3 + i] * width
            for n in range(TILES):
                at = pl.ds(pl.multiple_of(begin + n * tile, tile), tile)
                to = pl.ds(2 * count + n * half, half)
                copies.append(pltpu.make_async_copy(b_ref.at[tok, at], held.at[i, to, :], sems.at[i, n]))
        for copy in copies:
            copy.start()
        m, k = iota((count, 2 * count), 0), iota((count, 2 * count), 1)
        block = m % block_rows
        row = (m // block_rows) % per_z
        tail = m // (block_rows * per_z)
        high = 2 * (tail // 4) + 4 * ((tail // 2) % 2) + 8 * (tail % 2)
        values = a_ref[...].reshape(2 * count, toks)
        for odd in range(2):
            goal = jnp.bitwise_and(z + (1 - 2 * c) * (high + odd), NZ - 1)
            pick = (block * rows + goal * per_z + row == k).astype(WIDE).astype(HALF)
            moved = dot(pick, values).astype(HALF)
            turned = jnp.concatenate([moved[:, half:], moved[:, :half]], axis=1)
            at = (1 - odd) * count
            ordered = jnp.where(c == 1, turned, moved)
            for i in range(3):
                held[i, at : at + count, :] = ordered
        last = [pltpu.make_async_copy(held.at[i], out_refs[i], out_sems.at[i]) for i in range(3)]
        for i in range(3):
            for copy in copies[i * TILES : (i + 1) * TILES]:
                copy.wait()
            last[i].start()
        for copy in last:
            copy.wait()

    piece = (2 * count + TILES * half, toks)
    any_place = pl.BlockSpec(memory_space=pl.ANY)
    return pl.pallas_call(
        kernel,
        out_shape=[jax.ShapeDtypeStruct(piece, HALF)] * 3,
        in_specs=[
            pl.BlockSpec(memory_space=pltpu.SMEM),
            pl.BlockSpec(memory_space=pltpu.VMEM),
            any_place,
        ],
        out_specs=[any_place] * 3,
        scratch_shapes=[
            pltpu.VMEM((3, *piece), HALF),
            pltpu.SemaphoreType.DMA((3, TILES)),
            pltpu.SemaphoreType.DMA((3,)),
        ],
        compiler_params=ROOMY,
    )(place, activations, out_grads)


def own_part(piece, out_grads, place):
    toks = out_grads.shape[0]
    half = toks // NC
    width = out_grads.shape[1] // NX
    tile = width // TILES
    count = piece.shape[0] - TILES * half

    def kernel(place_ref, p_ref, b_ref, o_ref):
        c = place_ref[2]
        o_ref[:count, :] = p_ref[...]
        for n in range(TILES):
            for side, who in enumerate((c, 1 - c)):
                at = count + (2 * n + side) * half
                tok = pl.ds(pl.multiple_of(who * half, half), half)
                o_ref[at : at + half, :] = b_ref[tok, n * tile : (n + 1) * tile]

    own = (count + TILES * toks, tile)
    return pl.pallas_call(
        kernel,
        out_shape=jax.ShapeDtypeStruct(own, HALF),
        grid_spec=pltpu.PrefetchScalarGridSpec(
            num_scalar_prefetch=1,
            grid=(1,),
            in_specs=[
                pl.BlockSpec((count, tile), lambda i, place_ref: (0, 0)),
                pl.BlockSpec((toks, width), lambda i, place_ref: (0, place_ref[1])),
            ],
            out_specs=pl.BlockSpec(own, lambda i, place_ref: (0, 0)),
        ),
        compiler_params=ROOMY,
    )(place, piece, out_grads)


def partial_products(own, arrived, swapped, odd, chunk):
    toks = own.shape[1]
    half = toks // NC
    total_rows = own.shape[0] - TILES * toks
    count = total_rows // 2
    kind = HALF if odd else WIDE
    group = TILES // CHUNKS

    def kernel(*refs):
        rows_refs, own_ref, mine, other, out_ref = refs[:4], refs[4], refs[5:8], refs[8:11], refs[11]
        for n in range(group):
            at = slice(n * half, (n + 1) * half)
            total = dot(rows_refs[0][...], own_ref[n * toks : (n + 1) * toks, :])
            for rows_ref, m_ref, o_ref in zip(rows_refs[1:], mine, other):
                total += dot(rows_ref[...], jnp.concatenate([m_ref[at, :], o_ref[at, :]], axis=0))
            to = slice(n * toks, (n + 1) * toks)
            out_ref[:, to] = total.astype(kind)

    def block(skip, size):
        first = pl.Element(size)
        return pl.BlockSpec((first, pl.Element(toks)), lambda n: (skip + chunk * size, 0))

    rows = pl.BlockSpec((count, toks), lambda n: (0 if odd else 1, 0))
    return pl.pallas_call(
        kernel,
        grid=(1,),
        out_shape=jax.ShapeDtypeStruct((count, group * toks), kind),
        in_specs=[rows] * 4 + [block(total_rows, group * toks)] + [block(total_rows, group * half)] * 6,
        out_specs=pl.BlockSpec((count, group * toks), lambda n: (0, 0)),
        compiler_params=PARAMS,
    )(own, *arrived, own, *arrived, *swapped)


def pick_blocks(chosen, sums, block_size):
    sources, rows, width = sums.shape[0], sums.shape[1] // CHUNKS, sums.shape[2]
    columns = CHUNKS * width // block_size
    out_rows = chosen.shape[0]
    tile = out_rows // 2

    def kernel(p_ref, s_ref, o_ref):
        total = None
        for pair in range(sources // 2):
            depth = 2 * columns * rows
            pieces = []
            for x in (2 * pair, 2 * pair + 1):
                whole = jnp.concatenate([s_ref[x, k * rows : (k + 1) * rows, :] for k in range(CHUNKS)], axis=1)
                pieces += [whole[:, j * block_size : (j + 1) * block_size] for j in range(columns)]
            term = dot(p_ref[:, pair * depth : (pair + 1) * depth], jnp.concatenate(pieces, axis=0))
            total = term if total is None else total + term
        o_ref[...] = total.astype(HALF)

    return pl.pallas_call(
        kernel,
        grid=(2,),
        out_shape=jax.ShapeDtypeStruct((out_rows, block_size), HALF),
        in_specs=[
            pl.BlockSpec((tile, chosen.shape[1]), lambda n: (n, 0)),
            pl.BlockSpec(sums.shape, lambda n: (0, 0, 0)),
        ],
        out_specs=pl.BlockSpec((tile, block_size), lambda n: (n, 0)),
        compiler_params=PARAMS,
    )(chosen, sums)


def finish_sum(limits, pieces, acc):
    slots, rows, block_size = acc.shape
    per_z = rows // NZ
    total_rows = slots * rows
    piece_rows = pieces.shape[0]

    def kernel(lim_ref, p_ref, a_ref, g_ref, n_ref):
        m, k = iota((total_rows, piece_rows), 0), iota((total_rows, piece_rows), 1)
        row = k % per_z
        piece = (k // per_z) % 2
        slot = (k // (2 * per_z)) % slots
        source = k // (2 * per_z * slots)
        goal = jnp.bitwise_and(source + 8 * piece, NZ - 1)
        adds = (slot * rows + goal * per_z + row == m).astype(WIDE).astype(HALF)
        grad = dot(adds, p_ref[...])
        lane = iota((16, block_size), 1)
        extra_row = iota((16, block_size), 0)
        extra = jnp.zeros((16, block_size), WIDE)
        for s in range(slots):
            live = iota((rows, block_size), 0) < lim_ref[s]
            own = jnp.where(live, grad[s * rows : (s + 1) * rows], 0.0)
            new = a_ref[s] + own * own
            n_ref[s] = new
            grafted = own / (jnp.sqrt(new) + GRAFT_EPS)
            norm = jnp.sum(jnp.sum(grafted * grafted, axis=0, keepdims=True), axis=1, keepdims=True)
            high = norm.astype(HALF).astype(WIDE)
            middle = (norm - high).astype(HALF).astype(WIDE)
            low = norm - high - middle
            spread = jnp.where(lane == 0, high, jnp.where(lane == 1, middle, jnp.where(lane == 2, low, 0.0)))
            extra = jnp.where(extra_row == s, spread, extra)
            g_ref[s * rows : (s + 1) * rows, :] = own.astype(HALF)
        g_ref[total_rows:, :] = extra.astype(HALF)

    vmem = pl.BlockSpec(memory_space=pltpu.VMEM)
    return pl.pallas_call(
        kernel,
        out_shape=[
            jax.ShapeDtypeStruct((total_rows + 16, block_size), HALF),
            jax.ShapeDtypeStruct(acc.shape, WIDE),
        ],
        in_specs=[pl.BlockSpec(memory_space=pltpu.SMEM), vmem, vmem],
        out_specs=[vmem, vmem],
        compiler_params=PARAMS,
    )(limits, pieces, acc)


def update(facts, mine, other, roots_mine, roots_other, left_stat, right_stat):
    ny = mine.shape[0]
    slots, rows, block_size = left_stat.shape
    all_rows = mine.shape[1]

    def kernel(f_ref, m_ref, o_ref, rm_ref, ro_ref, ls_ref, rs_ref, ln_ref, rn_ref, d_ref, roots):
        s = pl.program_id(0)
        core, own_y, own_mp = f_ref[0], f_ref[1], f_ref[2]
        live, taken = f_ref[3 + s], f_ref[5 + s]
        at = pl.ds(pl.multiple_of(s * rows, rows), rows)
        for i in range(ny):
            source = jnp.bitwise_xor(own_y, i) * NC
            for ref, who in ((rm_ref, core), (ro_ref, 1 - core)):
                to = pl.ds(pl.multiple_of((source + who) * rows, rows), rows)
                for kind in range(2):
                    roots[kind, to, :] = ref[i, kind, 0]
        parts = []
        norm = jnp.zeros((1, 1), WIDE)
        tail_row = iota((16, block_size), 0) == s
        for y in range(ny):
            a, b = m_ref[y, at, :], o_ref[y, at, :]
            parts += [jnp.where(core == 0, a, b), jnp.where(core == 0, b, a)]
            for ref in (m_ref, o_ref):
                tail = jnp.where(tail_row, ref[y, slots * rows : all_rows, :].astype(WIDE), 0.0)
                norm += jnp.sum(jnp.sum(tail, axis=0, keepdims=True), axis=1, keepdims=True)
        grad = jnp.concatenate(parts, axis=0)
        prod = dot(grad, roots[1], ((1,), (1,))).astype(HALF)
        raw = dot(roots[0], prod)
        raw = jnp.where(iota(raw.shape, 0) < live, raw, 0.0)
        raw_sq = jnp.sum(jnp.sum(raw * raw, axis=0, keepdims=True), axis=1, keepdims=True)
        factor = jnp.sqrt(norm) / jnp.sqrt(raw_sq + GRAFT_EPS)
        d_ref[0] = jnp.where(taken == 1, factor * raw, 0.0).astype(HALF)
        own = m_ref[own_y, at, :]
        left_cols = dot(own, grad, ((1,), (1,)))
        own_columns = (iota((block_size, rows), 0) == own_mp * rows + iota((block_size, rows), 1)).astype(WIDE)
        columns = dot(grad, own_columns.astype(HALF)).astype(HALF)
        right_rows = dot(columns, grad, ((0,), (0,)))
        for old_ref, value, new_ref in ((ls_ref, left_cols, ln_ref), (rs_ref, right_rows, rn_ref)):
            old = old_ref[0]
            fresh = STAT_DECAY * old + (1.0 - STAT_DECAY) * value / block_size
            new_ref[0] = jnp.where(taken == 1, fresh, old)

    whole = pl.BlockSpec((ny, all_rows, block_size), lambda s: (0, 0, 0))
    square = pl.BlockSpec((1, block_size, block_size), lambda s: (s, 0, 0))
    strip = pl.BlockSpec((1, rows, block_size), lambda s: (s, 0, 0))
    return pl.pallas_call(
        kernel,
        grid=(slots,),
        out_shape=[
            jax.ShapeDtypeStruct(left_stat.shape, WIDE),
            jax.ShapeDtypeStruct(right_stat.shape, WIDE),
            jax.ShapeDtypeStruct((slots, block_size, block_size), HALF),
        ],
        in_specs=[pl.BlockSpec(memory_space=pltpu.SMEM), whole, whole]
        + [pl.BlockSpec((ny, 2, 1, rows, block_size), lambda s: (0, 0, s, 0, 0))] * 2
        + [strip, strip],
        out_specs=[strip, strip, square],
        scratch_shapes=[pltpu.VMEM((2, block_size, block_size), HALF)],
        compiler_params=PARAMS,
    )(facts, mine, other, roots_mine, roots_other, left_stat, right_stat)


def body(
    activations,
    out_grads,
    owners,
    live_rows,
    left_stat,
    right_stat,
    left_root,
    right_root,
    grad_acc,
):
    z, x, y, c = (lax.axis_index(name) for name in ("z", "x", "y", "c"))
    block_rows, rows, toks = activations.shape
    block_size = left_stat.shape[3]
    slots = left_stat.shape[1]
    block_count = owners.shape[0]
    per_z = rows // NZ
    columns = out_grads.shape[1] // block_size // NX
    my_owner = z * NX + x
    my_mp = y * NC + c
    my_rows = my_mp * rows

    place = jnp.stack([z, x, c] + [jnp.bitwise_and(x + step, NX - 1) for step in (2, 3, 1)]).astype(jnp.int32)
    pieces = prepare(activations, out_grads, place)
    arrived = [lax.ppermute(piece, "x", ring(NX, step)) for piece, step in zip(pieces, (2, -1, 1))]

    piece_own, owners = lax.optimization_barrier((pieces[0], owners))
    targets = slot_targets(owners, slots)
    by_block = targets.reshape(block_rows, NX, columns).transpose(1, 2, 0)[:, :, None, None, :]
    shape = (NX, columns, 2, per_z, block_rows)
    owner = by_block // slots
    code = (((owner // NX) * slots + by_block % slots) * 2 + iota(shape, 2)) * per_z + iota(shape, 3)
    code = jnp.where(owner % NX == x, code, -1).reshape(1, -1)
    out_rows = NZ * slots * 2 * per_z
    chosen = (code == iota((out_rows, 1), 0)).astype(HALF)
    piece_own, chosen = lax.optimization_barrier((piece_own, chosen))
    own = own_part(piece_own, out_grads, place)

    own, left_root, right_root = lax.optimization_barrier((own, left_root, right_root))
    ny = lax.axis_size("y")
    roots = jnp.stack([left_root[0], right_root[0]])[None]
    for step in (1, 2):
        if step < ny:
            came = lax.ppermute(roots, "y", [(i, i ^ step) for i in range(ny)])
            roots = jnp.concatenate([roots, came], axis=0)
    own, roots = lax.optimization_barrier((own, roots))
    swapped = [lax.ppermute(piece, "c", ring(NC, 1)) for piece in arrived]
    roots_other = lax.ppermute(roots, "c", ring(NC, 1))

    sent = [partial_products(own, arrived, swapped, True, chunk) for chunk in range(CHUNKS)]
    kept = [partial_products(own, arrived, swapped, False, chunk) for chunk in range(CHUNKS)]

    sums = []
    for out, keep in zip(sent, kept):
        got = []
        for step in (1, 2, 4):
            goals = [((i + (1 - 2 * k) * step) % NZ) * NC + k for i in range(NZ) for k in range(NC)]
            got.append(lax.ppermute(out, ("z", "c"), list(enumerate(goals))))
            part = got[-1].shape[0] // (2 if step < 4 else 1)
            rows_from = slice(part, 2 * part) if step < 4 else slice(0, part)
            total = keep[rows_from]
            for rows_in in got:
                total = total + rows_in[rows_from]
            out = total.astype(HALF)
        sums.append(out)
    sums = lax.all_gather(jnp.concatenate(sums, axis=0), "x", axis=0, tiled=False)

    picked = pick_blocks(chosen, sums, block_size).reshape(NZ, out_rows // NZ, block_size)
    arrived = lax.all_to_all(picked, "z", 0, 0, tiled=True).reshape(out_rows, block_size)

    wanted = my_owner * slots + iota((slots, block_count), 0)
    matched = targets[None, :] == wanted
    occupied = jnp.any(matched, axis=1).astype(jnp.int32)
    live_mine = jnp.sum(jnp.where(matched, live_rows[None, :], 0), axis=1).astype(jnp.int32)
    own_rows, acc_next = finish_sum(live_mine - my_rows, arrived, grad_acc[0])
    rows_mine = lax.all_gather(own_rows, "y", axis=0, tiled=False)
    rows_other = lax.ppermute(rows_mine, "c", ring(NC, 1))
    facts = jnp.concatenate([jnp.stack([c, y, my_mp]).astype(jnp.int32), live_mine, occupied])
    left_next, right_next, directions = update(
        facts, rows_mine, rows_other, roots, roots_other, left_stat[0], right_stat[0]
    )
    return (left_next[None], right_next[None], acc_next[None], directions[None])


def solution(mesh):
    dp, mp = mesh.devices.shape
    parts = Mesh(mesh.devices.reshape(NZ, NX, mp // NC, NC), ("z", "x", "y", "c"))
    owner, strip = ("z", "x"), ("y", "c")
    state = P(owner, None, strip, None)
    return jax.shard_map(
        body,
        mesh=parts,
        in_specs=(P(None, strip, owner), P(owner, None), P(), P(), state, state, state, state, state),
        out_specs=(state, state, state, P(owner, None, None, None)),
        check_vma=False,
    )
```

```python
import jax
import jax.numpy as jnp
from jax import lax
from jax.experimental import pallas as pl
from jax.experimental.pallas import tpu as pltpu
from jax.sharding import Mesh, PartitionSpec as P

STAT_DECAY = 0.9
GRAFT_EPS = 1e-06
HALF = jnp.bfloat16
WIDE = jnp.float32
NZ, NX, NC = 16, 4, 2
TILES = 6
CHUNKS = 2
X_CHUNKS = 1
ROOMY = pltpu.CompilerParams(vmem_limit_bytes=60 * 1024 * 1024)
PARAMS = pltpu.CompilerParams(vmem_limit_bytes=8 * 1024 * 1024)


def slot_targets(owners, slot_count):
    block_count = owners.shape[0]
    same_owner = owners[:, None] == owners[None, :]
    earlier = lax.broadcasted_iota(jnp.int32, (block_count, block_count), 1) < lax.broadcasted_iota(
        jnp.int32, (block_count, block_count), 0
    )
    ranked = jnp.sum(jnp.where(same_owner & earlier, 1, 0), axis=1).astype(jnp.int32)
    return owners * slot_count + ranked


def ring(count, step):
    return [(i, (i + step) % count) for i in range(count)]


def iota(shape, dim):
    return lax.broadcasted_iota(jnp.int32, shape, dim)


def dot(a, b, dims=((1,), (0,))):
    return lax.dot_general(a, b, (dims, ((), ())), preferred_element_type=WIDE)


def ordered_rows(values, z, way, odd, block_rows, rows):
    per_z = rows // NZ
    count = block_rows * rows // 2
    m, k = iota((count, 2 * count), 0), iota((count, 2 * count), 1)
    block = m % block_rows
    row = (m // block_rows) % per_z
    tail = m // (block_rows * per_z)
    high = 2 * (tail // 4) + 4 * ((tail // 2) % 2) + 8 * (tail % 2)
    goal = jnp.bitwise_and(z + way * (high + odd), NZ - 1)
    pick = (block * rows + goal * per_z + row == k).astype(WIDE).astype(HALF)
    return dot(pick, values).astype(HALF)


def send_pieces(kernel, shapes, place, arrays, copies):
    any_place = pl.BlockSpec(memory_space=pl.ANY)
    return pl.pallas_call(
        kernel,
        out_shape=[jax.ShapeDtypeStruct(shape, HALF) for shape in shapes],
        in_specs=[pl.BlockSpec(memory_space=pltpu.SMEM)]
        + [pl.BlockSpec(memory_space=pltpu.VMEM)] * (len(arrays) - 1)
        + [any_place],
        out_specs=[any_place] * len(shapes),
        scratch_shapes=[pltpu.VMEM(shape, HALF) for shape in shapes]
        + [pltpu.SemaphoreType.DMA((copies,)), pltpu.SemaphoreType.DMA((len(shapes),))],
        compiler_params=ROOMY,
    )(place, *arrays)


def prepare(sources, out_grads, place, far):
    block_rows, rows, toks = sources[0].shape
    count = block_rows * rows // 2
    half = toks // NC
    width = out_grads.shape[1] // NX
    tile = width // TILES
    size = half if far else toks
    group = TILES // X_CHUNKS
    skip = 2 * count * (1 if far else NC)
    shapes = [((skip if k == 0 else 0) + group * size, toks) for k in range(X_CHUNKS)]

    def kernel(place_ref, *refs):
        a_refs, refs = refs[: len(sources)], refs[len(sources) :]
        b_ref, out_refs, refs = refs[0], refs[1 : 1 + X_CHUNKS], refs[1 + X_CHUNKS :]
        held, (sems, out_sems) = refs[:X_CHUNKS], refs[X_CHUNKS:]
        z, x, c = place_ref[0], place_ref[1], place_ref[2]
        goal_x = jnp.bitwise_and(x + 2 if far else x + 1 - 2 * c, NX - 1)
        tok = pl.ds(pl.multiple_of(c * half, half) if far else 0, size)
        copies = []
        for n in range(TILES):
            at = pl.ds(pl.multiple_of(goal_x * width + n * tile, tile), tile)
            first = (skip if n < group else 0) + n % group * size
            copies.append(pltpu.make_async_copy(b_ref.at[tok, at], held[n // group].at[pl.ds(first, size), :], sems.at[n]))
            copies[-1].start()
        for i, ref in enumerate(a_refs):
            core = c if i == 0 else 1 - c
            values = ref[...].reshape(2 * count, toks)
            for odd in range(2):
                moved = ordered_rows(values, z, 1 - 2 * core, odd, block_rows, rows)
                if far:
                    turned = jnp.concatenate([moved[:, half:], moved[:, :half]], axis=1)
                    held[0][(1 - odd) * count : (2 - odd) * count, :] = jnp.where(c == 1, turned, moved)
                else:
                    to = pl.ds(pl.multiple_of((2 * core + 1 - odd) * count, count), count)
                    held[0][to, :] = moved
        last = []
        for k in range(X_CHUNKS):
            for copy in copies[k * group : (k + 1) * group]:
                copy.wait()
            last.append(pltpu.make_async_copy(held[k], out_refs[k], out_sems.at[k]))
            last[k].start()
        for copy in last:
            copy.wait()

    return send_pieces(kernel, shapes, place, (*sources, out_grads), TILES)


def own_part(piece, count, out_grads, place):
    toks = out_grads.shape[0]
    half = toks // NC
    width = out_grads.shape[1] // NX
    tile = width // TILES

    def kernel(place_ref, p_ref, b_ref, o_ref):
        c = place_ref[2]
        o_ref[:count, :] = p_ref[...]
        for n in range(TILES):
            for side, who in enumerate((c, 1 - c)):
                at = count + (2 * n + side) * half
                tok = pl.ds(pl.multiple_of(who * half, half), half)
                o_ref[at : at + half, :] = b_ref[tok, n * tile : (n + 1) * tile]

    own = (count + TILES * toks, tile)
    return pl.pallas_call(
        kernel,
        out_shape=jax.ShapeDtypeStruct(own, HALF),
        grid_spec=pltpu.PrefetchScalarGridSpec(
            num_scalar_prefetch=1,
            grid=(1,),
            in_specs=[
                pl.BlockSpec((count, tile), lambda i, place_ref: (0, 0)),
                pl.BlockSpec((toks, width), lambda i, place_ref: (0, place_ref[1])),
            ],
            out_specs=pl.BlockSpec(own, lambda i, place_ref: (0, 0)),
        ),
        compiler_params=ROOMY,
    )(place, piece, out_grads)


def partial_products(place, own, far, near, odd, chunk):
    toks = own.shape[1]
    half = toks // NC
    total_rows = own.shape[0] - TILES * toks
    count = total_rows // 2
    kind = HALF if odd else WIDE
    group = TILES // CHUNKS
    row_block = 0 if odd else 1

    def kernel(place_ref, *refs):
        rows_refs, own_ref, (mine, other), near_refs, out_ref = refs[:4], refs[4], refs[5:7], refs[7:9], refs[9]
        for n in range(group):
            at = slice(n * half, (n + 1) * half)
            to = slice(n * toks, (n + 1) * toks)
            total = dot(rows_refs[0][...], own_ref[to, :])
            total += dot(rows_refs[1][...], jnp.concatenate([mine[at, :], other[at, :]], axis=0))
            for rows_ref, ref in zip(rows_refs[2:], near_refs):
                total += dot(rows_ref[...], ref[to, :])
            out_ref[:, to] = total.astype(kind)

    def block(skip, size):
        return pl.BlockSpec((pl.Element(size), pl.Element(toks)), lambda n, place_ref: (skip, 0))

    rows = pl.BlockSpec((count, toks), lambda n, place_ref: (row_block, 0))
    rows_of_core = pl.BlockSpec((count, toks), lambda n, place_ref: (2 * place_ref[2] + row_block, 0))
    return pl.pallas_call(
        kernel,
        out_shape=jax.ShapeDtypeStruct((count, group * toks), kind),
        grid_spec=pltpu.PrefetchScalarGridSpec(
            num_scalar_prefetch=1,
            grid=(1,),
            in_specs=[rows] * 2
            + [rows_of_core] * 2
            + [block(total_rows + chunk * group * toks, group * toks)]
            + [block(total_rows + chunk * group * half, group * half)] * 2
            + [block(NC * total_rows + chunk * group * toks, group * toks)] * 2,
            out_specs=pl.BlockSpec((count, group * toks), lambda n, place_ref: (0, 0)),
        ),
        compiler_params=PARAMS,
    )(place, own, far[0][0], near[0][0], near[1][0], own, *[part[0] for part in far], *[part[0] for part in near])


def pick_blocks(chosen, sums, block_size):
    sources, rows, width = sums.shape[0], sums.shape[1] // CHUNKS, sums.shape[2]
    columns = CHUNKS * width // block_size
    out_rows = chosen.shape[0]
    tile = out_rows // 2

    def kernel(p_ref, s_ref, o_ref):
        total = None
        for pair in range(sources // 2):
            depth = 2 * columns * rows
            pieces = []
            for x in (2 * pair, 2 * pair + 1):
                whole = jnp.concatenate([s_ref[x, k * rows : (k + 1) * rows, :] for k in range(CHUNKS)], axis=1)
                pieces += [whole[:, j * block_size : (j + 1) * block_size] for j in range(columns)]
            term = dot(p_ref[:, pair * depth : (pair + 1) * depth], jnp.concatenate(pieces, axis=0))
            total = term if total is None else total + term
        o_ref[...] = total.astype(HALF)

    return pl.pallas_call(
        kernel,
        grid=(2,),
        out_shape=jax.ShapeDtypeStruct((out_rows, block_size), HALF),
        in_specs=[
            pl.BlockSpec((tile, chosen.shape[1]), lambda n: (n, 0)),
            pl.BlockSpec(sums.shape, lambda n: (0, 0, 0)),
        ],
        out_specs=pl.BlockSpec((tile, block_size), lambda n: (n, 0)),
        compiler_params=PARAMS,
    )(chosen, sums)


def finish_sum(limits, pieces, acc):
    slots, rows, block_size = acc.shape
    per_z = rows // NZ
    total_rows = slots * rows
    piece_rows = pieces.shape[0]

    def kernel(lim_ref, p_ref, a_ref, g_ref, n_ref):
        m, k = iota((total_rows, piece_rows), 0), iota((total_rows, piece_rows), 1)
        row = k % per_z
        piece = (k // per_z) % 2
        slot = (k // (2 * per_z)) % slots
        source = k // (2 * per_z * slots)
        goal = jnp.bitwise_and(source + 8 * piece, NZ - 1)
        adds = (slot * rows + goal * per_z + row == m).astype(WIDE).astype(HALF)
        grad = dot(adds, p_ref[...])
        lane = iota((16, block_size), 1)
        extra_row = iota((16, block_size), 0)
        extra = jnp.zeros((16, block_size), WIDE)
        for s in range(slots):
            live = iota((rows, block_size), 0) < lim_ref[s]
            own = jnp.where(live, grad[s * rows : (s + 1) * rows], 0.0)
            new = a_ref[s] + own * own
            n_ref[s] = new
            grafted = own / (jnp.sqrt(new) + GRAFT_EPS)
            norm = jnp.sum(jnp.sum(grafted * grafted, axis=0, keepdims=True), axis=1, keepdims=True)
            high = norm.astype(HALF).astype(WIDE)
            middle = (norm - high).astype(HALF).astype(WIDE)
            low = norm - high - middle
            spread = jnp.where(lane == 0, high, jnp.where(lane == 1, middle, jnp.where(lane == 2, low, 0.0)))
            extra = jnp.where(extra_row == s, spread, extra)
            g_ref[s * rows : (s + 1) * rows, :] = own.astype(HALF)
        g_ref[total_rows:, :] = extra.astype(HALF)

    vmem = pl.BlockSpec(memory_space=pltpu.VMEM)
    return pl.pallas_call(
        kernel,
        out_shape=[
            jax.ShapeDtypeStruct((total_rows + 16, block_size), HALF),
            jax.ShapeDtypeStruct(acc.shape, WIDE),
        ],
        in_specs=[pl.BlockSpec(memory_space=pltpu.SMEM), vmem, vmem],
        out_specs=[vmem, vmem],
        compiler_params=PARAMS,
    )(limits, pieces, acc)


def update(facts, mine, other, roots_mine, roots_other, left_stat, right_stat):
    ny = mine.shape[0]
    slots, rows, block_size = left_stat.shape
    all_rows = mine.shape[1]

    def kernel(f_ref, m_ref, o_ref, rm_ref, ro_ref, ls_ref, rs_ref, ln_ref, rn_ref, d_ref, roots):
        s = pl.program_id(0)
        core, own_y, own_mp = f_ref[0], f_ref[1], f_ref[2]
        live, taken = f_ref[3 + s], f_ref[5 + s]
        at = pl.ds(pl.multiple_of(s * rows, rows), rows)
        for i in range(ny):
            source = jnp.bitwise_xor(own_y, i) * NC
            for ref, who in ((rm_ref, core), (ro_ref, 1 - core)):
                to = pl.ds(pl.multiple_of((source + who) * rows, rows), rows)
                for kind in range(2):
                    roots[kind, to, :] = ref[i, kind, 0]
        parts = []
        norm = jnp.zeros((1, 1), WIDE)
        tail_row = iota((16, block_size), 0) == s
        for y in range(ny):
            a, b = m_ref[y, at, :], o_ref[y, at, :]
            parts += [jnp.where(core == 0, a, b), jnp.where(core == 0, b, a)]
            for ref in (m_ref, o_ref):
                tail = jnp.where(tail_row, ref[y, slots * rows : all_rows, :].astype(WIDE), 0.0)
                norm += jnp.sum(jnp.sum(tail, axis=0, keepdims=True), axis=1, keepdims=True)
        grad = jnp.concatenate(parts, axis=0)
        prod = dot(grad, roots[1], ((1,), (1,))).astype(HALF)
        raw = dot(roots[0], prod)
        raw = jnp.where(iota(raw.shape, 0) < live, raw, 0.0)
        raw_sq = jnp.sum(jnp.sum(raw * raw, axis=0, keepdims=True), axis=1, keepdims=True)
        factor = jnp.sqrt(norm) / jnp.sqrt(raw_sq + GRAFT_EPS)
        d_ref[0] = jnp.where(taken == 1, factor * raw, 0.0).astype(HALF)
        own = m_ref[own_y, at, :]
        left_cols = dot(own, grad, ((1,), (1,)))
        own_columns = (iota((block_size, rows), 0) == own_mp * rows + iota((block_size, rows), 1)).astype(WIDE)
        columns = dot(grad, own_columns.astype(HALF)).astype(HALF)
        right_rows = dot(columns, grad, ((0,), (0,)))
        for old_ref, value, new_ref in ((ls_ref, left_cols, ln_ref), (rs_ref, right_rows, rn_ref)):
            old = old_ref[0]
            fresh = STAT_DECAY * old + (1.0 - STAT_DECAY) * value / block_size
            new_ref[0] = jnp.where(taken == 1, fresh, old)

    whole = pl.BlockSpec((ny, all_rows, block_size), lambda s: (0, 0, 0))
    square = pl.BlockSpec((1, block_size, block_size), lambda s: (s, 0, 0))
    strip = pl.BlockSpec((1, rows, block_size), lambda s: (s, 0, 0))
    return pl.pallas_call(
        kernel,
        grid=(slots,),
        out_shape=[
            jax.ShapeDtypeStruct(left_stat.shape, WIDE),
            jax.ShapeDtypeStruct(right_stat.shape, WIDE),
            jax.ShapeDtypeStruct((slots, block_size, block_size), HALF),
        ],
        in_specs=[pl.BlockSpec(memory_space=pltpu.SMEM), whole, whole]
        + [pl.BlockSpec((ny, 2, 1, rows, block_size), lambda s: (0, 0, s, 0, 0))] * 2
        + [strip, strip],
        out_specs=[strip, strip, square],
        scratch_shapes=[pltpu.VMEM((2, block_size, block_size), HALF)],
        compiler_params=PARAMS,
    )(facts, mine, other, roots_mine, roots_other, left_stat, right_stat)


def body(
    activations,
    out_grads,
    owners,
    live_rows,
    left_stat,
    right_stat,
    left_root,
    right_root,
    grad_acc,
):
    z, x, y, c = (lax.axis_index(name) for name in ("z", "x", "y", "c"))
    block_rows, rows, toks = activations.shape
    block_size = left_stat.shape[3]
    slots = left_stat.shape[1]
    block_count = owners.shape[0]
    per_z = rows // NZ
    columns = out_grads.shape[1] // block_size // NX
    my_owner = z * NX + x
    my_mp = y * NC + c
    my_rows = my_mp * rows

    place = jnp.stack([z, x, c]).astype(jnp.int32)
    swap = ring(NC, 1)
    other_rows = lax.ppermute(activations, "c", swap)
    goals = [(i + (1 - 2 * k)) % NX * NC + k for i in range(NX) for k in range(NC)]
    pieces = prepare((activations,), out_grads, place, True)
    far_mine = [lax.ppermute(piece, "x", ring(NX, 2)) for piece in pieces]
    near_pieces = prepare((activations, other_rows), out_grads, place, False)
    near_mine = [lax.ppermute(piece, ("x", "c"), list(enumerate(goals))) for piece in near_pieces]

    piece_own, owners = lax.optimization_barrier((pieces[0], owners))
    targets = slot_targets(owners, slots)
    by_block = targets.reshape(block_rows, NX, columns).transpose(1, 2, 0)[:, :, None, None, :]
    shape = (NX, columns, 2, per_z, block_rows)
    owner = by_block // slots
    code = (((owner // NX) * slots + by_block % slots) * 2 + iota(shape, 2)) * per_z + iota(shape, 3)
    code = jnp.where(owner % NX == x, code, -1).reshape(1, -1)
    out_rows = NZ * slots * 2 * per_z
    chosen = (code == iota((out_rows, 1), 0)).astype(HALF)
    piece_own, chosen = lax.optimization_barrier((piece_own, chosen))
    own = own_part(piece_own, block_rows * rows, out_grads, place)

    piece_far, left_root, right_root = lax.optimization_barrier((pieces[0], left_root, right_root))
    ny = lax.axis_size("y")
    roots = jnp.stack([left_root[0], right_root[0]])[None]
    for step in (1, 2):
        if step < ny:
            came = lax.ppermute(roots, "y", [(i, i ^ step) for i in range(ny)])
            roots = jnp.concatenate([roots, came], axis=0)
    own, roots = lax.optimization_barrier((own, roots))
    roots_other = lax.ppermute(roots, "c", swap)
    far = [far_mine, [lax.ppermute(piece, "c", swap) for piece in far_mine]]
    near_mine[0], own = lax.optimization_barrier((near_mine[0], own))
    near = [near_mine, [lax.ppermute(piece, "c", swap) for piece in near_mine]]
    sent = [partial_products(place, own, far, near, True, chunk) for chunk in range(CHUNKS)]
    kept = [partial_products(place, own, far, near, False, chunk) for chunk in range(CHUNKS)]

    sums = []
    for out, keep in zip(sent, kept):
        got = []
        for step in (1, 2, 4):
            goals = [((i + (1 - 2 * k) * step) % NZ) * NC + k for i in range(NZ) for k in range(NC)]
            got.append(lax.ppermute(out, ("z", "c"), list(enumerate(goals))))
            part = got[-1].shape[0] // (2 if step < 4 else 1)
            rows_from = slice(part, 2 * part) if step < 4 else slice(0, part)
            total = keep[rows_from]
            for rows_in in got:
                total = total + rows_in[rows_from]
            out = total.astype(HALF)
        sums.append(out)
    sums = lax.all_gather(jnp.concatenate(sums, axis=0), "x", axis=0, tiled=False)

    picked = pick_blocks(chosen, sums, block_size).reshape(NZ, out_rows // NZ, block_size)
    arrived = lax.all_to_all(picked, "z", 0, 0, tiled=True).reshape(out_rows, block_size)

    wanted = my_owner * slots + iota((slots, block_count), 0)
    matched = targets[None, :] == wanted
    occupied = jnp.any(matched, axis=1).astype(jnp.int32)
    live_mine = jnp.sum(jnp.where(matched, live_rows[None, :], 0), axis=1).astype(jnp.int32)
    own_rows, acc_next = finish_sum(live_mine - my_rows, arrived, grad_acc[0])
    rows_mine = lax.all_gather(own_rows, "y", axis=0, tiled=False)
    rows_other = lax.ppermute(rows_mine, "c", ring(NC, 1))
    facts = jnp.concatenate([jnp.stack([c, y, my_mp]).astype(jnp.int32), live_mine, occupied])
    left_next, right_next, directions = update(
        facts, rows_mine, rows_other, roots, roots_other, left_stat[0], right_stat[0]
    )
    return (left_next[None], right_next[None], acc_next[None], directions[None])


def solution(mesh):
    dp, mp = mesh.devices.shape
    parts = Mesh(mesh.devices.reshape(NZ, NX, mp // NC, NC), ("z", "x", "y", "c"))
    owner, strip = ("z", "x"), ("y", "c")
    state = P(owner, None, strip, None)
    return jax.shard_map(
        body,
        mesh=parts,
        in_specs=(P(None, strip, owner), P(owner, None), P(), P(), state, state, state, state, state),
        out_specs=(state, state, state, P(owner, None, None, None)),
        check_vma=False,
    )
```

```python
import jax
import jax.numpy as jnp
from jax import lax
from jax.experimental import pallas as pl
from jax.experimental.pallas import tpu as pltpu
from jax.sharding import Mesh, PartitionSpec as P

STAT_DECAY = 0.9
GRAFT_EPS = 1e-06
HALF = jnp.bfloat16
WIDE = jnp.float32
NZ, NX, NC = 16, 4, 2
TILES = 6
CHUNKS = 2
ROOMY = pltpu.CompilerParams(vmem_limit_bytes=60 * 1024 * 1024)
PARAMS = pltpu.CompilerParams(vmem_limit_bytes=8 * 1024 * 1024)


def slot_targets(owners, slot_count):
    block_count = owners.shape[0]
    same_owner = owners[:, None] == owners[None, :]
    earlier = lax.broadcasted_iota(jnp.int32, (block_count, block_count), 1) < lax.broadcasted_iota(
        jnp.int32, (block_count, block_count), 0
    )
    ranked = jnp.sum(jnp.where(same_owner & earlier, 1, 0), axis=1).astype(jnp.int32)
    return owners * slot_count + ranked


def position(place_ref, ny):
    index = place_ref[0]
    return index // (NX * ny * NC), index // (ny * NC) % NX, index % NC


def ring(count, step):
    return [(i, (i + step) % count) for i in range(count)]


def iota(shape, dim):
    return lax.broadcasted_iota(jnp.int32, shape, dim)


def dot(a, b, dims=((1,), (0,))):
    return lax.dot_general(a, b, (dims, ((), ())), preferred_element_type=WIDE)


def prepare(activations, out_grads, place, ny):
    block_rows, rows, toks = activations.shape
    per_z = rows // NZ
    count = block_rows * rows // 2
    half = toks // NC
    width = out_grads.shape[1] // NX
    tile = width // TILES

    def kernel(place_ref, a_ref, b_ref, *refs):
        out_refs, (held, rows_in, sems, out_sems, rows_sem) = refs[:3], refs[3:]
        z, x, c = position(place_ref, ny)
        rows_copy = pltpu.make_async_copy(a_ref, rows_in, rows_sem)
        rows_copy.start()
        tok = pl.ds(pl.multiple_of(c * half, half), half)
        copies = []
        for i in range(3):
            begin = jnp.bitwise_and(x + (2, 3, 1)[i], NX - 1) * width
            for n in range(TILES):
                at = pl.ds(pl.multiple_of(begin + n * tile, tile), tile)
                to = pl.ds(2 * count + n * half, half)
                copies.append(pltpu.make_async_copy(b_ref.at[tok, at], held.at[i, to, :], sems.at[i, n]))
        for copy in copies:
            copy.start()
        m, k = iota((count, 2 * count), 0), iota((count, 2 * count), 1)
        block = m % block_rows
        row = (m // block_rows) % per_z
        tail = m // (block_rows * per_z)
        high = 2 * (tail // 4) + 4 * ((tail // 2) % 2) + 8 * (tail % 2)
        picks = []
        for odd in range(2):
            goal = jnp.bitwise_and(z + (1 - 2 * c) * (high + odd), NZ - 1)
            picks.append((block * rows + goal * per_z + row == k).astype(WIDE).astype(HALF))
        rows_copy.wait()
        values = rows_in[...].reshape(2 * count, toks)
        for odd in range(2):
            moved = dot(picks[odd], values).astype(HALF)
            turned = jnp.concatenate([moved[:, half:], moved[:, :half]], axis=1)
            at = (1 - odd) * count
            ordered = jnp.where(c == 1, turned, moved)
            for i in range(3):
                held[i, at : at + count, :] = ordered
        last = [pltpu.make_async_copy(held.at[i], out_refs[i], out_sems.at[i]) for i in range(3)]
        for i in range(3):
            for copy in copies[i * TILES : (i + 1) * TILES]:
                copy.wait()
            last[i].start()
        for copy in last:
            copy.wait()

    piece = (2 * count + TILES * half, toks)
    any_place = pl.BlockSpec(memory_space=pl.ANY)
    return pl.pallas_call(
        kernel,
        out_shape=[jax.ShapeDtypeStruct(piece, HALF)] * 3,
        in_specs=[
            pl.BlockSpec(memory_space=pltpu.SMEM),
            any_place,
            any_place,
        ],
        out_specs=[any_place] * 3,
        scratch_shapes=[
            pltpu.VMEM((3, *piece), HALF),
            pltpu.VMEM(activations.shape, HALF),
            pltpu.SemaphoreType.DMA((3, TILES)),
            pltpu.SemaphoreType.DMA((3,)),
            pltpu.SemaphoreType.DMA,
        ],
        compiler_params=ROOMY,
    )(place, activations, out_grads)


def own_part(piece, out_grads, place, ny):
    toks = out_grads.shape[0]
    half = toks // NC
    width = out_grads.shape[1] // NX
    tile = width // TILES
    count = piece.shape[0] - TILES * half

    def kernel(place_ref, p_ref, b_ref, o_ref):
        c = position(place_ref, ny)[2]
        o_ref[:count, :] = p_ref[...]
        for n in range(TILES):
            for side, who in enumerate((c, 1 - c)):
                at = count + (2 * n + side) * half
                tok = pl.ds(pl.multiple_of(who * half, half), half)
                o_ref[at : at + half, :] = b_ref[tok, n * tile : (n + 1) * tile]

    own = (count + TILES * toks, tile)
    return pl.pallas_call(
        kernel,
        out_shape=jax.ShapeDtypeStruct(own, HALF),
        grid_spec=pltpu.PrefetchScalarGridSpec(
            num_scalar_prefetch=1,
            grid=(1,),
            in_specs=[
                pl.BlockSpec((count, tile), lambda i, place_ref: (0, 0)),
                pl.BlockSpec((toks, width), lambda i, place_ref: (0, position(place_ref, ny)[1])),
            ],
            out_specs=pl.BlockSpec(own, lambda i, place_ref: (0, 0)),
        ),
        compiler_params=ROOMY,
    )(place, piece, out_grads)


def partial_products(own, arrived, swapped, odd, chunk):
    toks = own.shape[1]
    half = toks // NC
    total_rows = own.shape[0] - TILES * toks
    count = total_rows // 2
    kind = HALF if odd else WIDE
    group = TILES // CHUNKS

    def kernel(*refs):
        rows_refs, own_ref, mine, other, out_ref = refs[:4], refs[4], refs[5:8], refs[8:11], refs[11]
        for n in range(group):
            at = slice(n * half, (n + 1) * half)
            total = dot(rows_refs[0][...], own_ref[n * toks : (n + 1) * toks, :])
            for rows_ref, m_ref, o_ref in zip(rows_refs[1:], mine, other):
                total += dot(rows_ref[...], jnp.concatenate([m_ref[at, :], o_ref[at, :]], axis=0))
            to = slice(n * toks, (n + 1) * toks)
            out_ref[:, to] = total.astype(kind)

    def block(skip, size):
        first = pl.Element(size)
        return pl.BlockSpec((first, pl.Element(toks)), lambda n: (skip + chunk * size, 0))

    rows = pl.BlockSpec((count, toks), lambda n: (0 if odd else 1, 0))
    return pl.pallas_call(
        kernel,
        grid=(1,),
        out_shape=jax.ShapeDtypeStruct((count, group * toks), kind),
        in_specs=[rows] * 4 + [block(total_rows, group * toks)] + [block(total_rows, group * half)] * 6,
        out_specs=pl.BlockSpec((count, group * toks), lambda n: (0, 0)),
        compiler_params=PARAMS,
    )(own, *arrived, own, *arrived, *swapped)


def pick_blocks(chosen, sums, block_size):
    sources, rows, width = sums.shape[0], sums.shape[1] // CHUNKS, sums.shape[2]
    columns = CHUNKS * width // block_size
    out_rows = chosen.shape[0]
    tile = out_rows // 2

    def kernel(p_ref, s_ref, o_ref):
        total = None
        for pair in range(sources // 2):
            depth = 2 * columns * rows
            pieces = []
            for x in (2 * pair, 2 * pair + 1):
                whole = jnp.concatenate([s_ref[x, k * rows : (k + 1) * rows, :] for k in range(CHUNKS)], axis=1)
                pieces += [whole[:, j * block_size : (j + 1) * block_size] for j in range(columns)]
            term = dot(p_ref[:, pair * depth : (pair + 1) * depth], jnp.concatenate(pieces, axis=0))
            total = term if total is None else total + term
        o_ref[...] = total.astype(HALF)

    return pl.pallas_call(
        kernel,
        grid=(2,),
        out_shape=jax.ShapeDtypeStruct((out_rows, block_size), HALF),
        in_specs=[
            pl.BlockSpec((tile, chosen.shape[1]), lambda n: (n, 0)),
            pl.BlockSpec(sums.shape, lambda n: (0, 0, 0)),
        ],
        out_specs=pl.BlockSpec((tile, block_size), lambda n: (n, 0)),
        compiler_params=PARAMS,
    )(chosen, sums)


def finish_sum(limits, pieces, acc):
    slots, rows, block_size = acc.shape
    per_z = rows // NZ
    total_rows = slots * rows
    piece_rows = pieces.shape[0]

    def kernel(lim_ref, p_ref, a_ref, g_ref, n_ref):
        m, k = iota((total_rows, piece_rows), 0), iota((total_rows, piece_rows), 1)
        row = k % per_z
        piece = (k // per_z) % 2
        slot = (k // (2 * per_z)) % slots
        source = k // (2 * per_z * slots)
        goal = jnp.bitwise_and(source + 8 * piece, NZ - 1)
        adds = (slot * rows + goal * per_z + row == m).astype(WIDE).astype(HALF)
        grad = dot(adds, p_ref[...])
        lane = iota((16, block_size), 1)
        extra_row = iota((16, block_size), 0)
        extra = jnp.zeros((16, block_size), WIDE)
        for s in range(slots):
            live = iota((rows, block_size), 0) < lim_ref[s]
            own = jnp.where(live, grad[s * rows : (s + 1) * rows], 0.0)
            new = a_ref[s] + own * own
            n_ref[s] = new
            grafted = own / (jnp.sqrt(new) + GRAFT_EPS)
            norm = jnp.sum(jnp.sum(grafted * grafted, axis=0, keepdims=True), axis=1, keepdims=True)
            high = norm.astype(HALF).astype(WIDE)
            middle = (norm - high).astype(HALF).astype(WIDE)
            low = norm - high - middle
            spread = jnp.where(lane == 0, high, jnp.where(lane == 1, middle, jnp.where(lane == 2, low, 0.0)))
            extra = jnp.where(extra_row == s, spread, extra)
            g_ref[s * rows : (s + 1) * rows, :] = own.astype(HALF)
        g_ref[total_rows:, :] = extra.astype(HALF)

    vmem = pl.BlockSpec(memory_space=pltpu.VMEM)
    return pl.pallas_call(
        kernel,
        out_shape=[
            jax.ShapeDtypeStruct((total_rows + 16, block_size), HALF),
            jax.ShapeDtypeStruct(acc.shape, WIDE),
        ],
        in_specs=[pl.BlockSpec(memory_space=pltpu.SMEM), vmem, vmem],
        out_specs=[vmem, vmem],
        compiler_params=PARAMS,
    )(limits, pieces, acc)


def update(facts, mine, other, roots_mine, roots_other, left_stat, right_stat):
    ny = mine.shape[0]
    slots, rows, block_size = left_stat.shape
    all_rows = mine.shape[1]

    def kernel(f_ref, m_ref, o_ref, rm_ref, ro_ref, ls_ref, rs_ref, ln_ref, rn_ref, d_ref, roots):
        s = pl.program_id(0)
        core, own_y, own_mp = f_ref[0], f_ref[1], f_ref[2]
        live, taken = f_ref[3 + s], f_ref[5 + s]
        at = pl.ds(pl.multiple_of(s * rows, rows), rows)
        for i in range(ny):
            source = jnp.bitwise_xor(own_y, i) * NC
            for ref, who in ((rm_ref, core), (ro_ref, 1 - core)):
                to = pl.ds(pl.multiple_of((source + who) * rows, rows), rows)
                for kind in range(2):
                    roots[kind, to, :] = ref[i, kind, 0]
        parts = []
        norm = jnp.zeros((1, 1), WIDE)
        tail_row = iota((16, block_size), 0) == s
        for y in range(ny):
            a, b = m_ref[y, at, :], o_ref[y, at, :]
            parts += [jnp.where(core == 0, a, b), jnp.where(core == 0, b, a)]
            for ref in (m_ref, o_ref):
                tail = jnp.where(tail_row, ref[y, slots * rows : all_rows, :].astype(WIDE), 0.0)
                norm += jnp.sum(jnp.sum(tail, axis=0, keepdims=True), axis=1, keepdims=True)
        grad = jnp.concatenate(parts, axis=0)
        prod = dot(grad, roots[1], ((1,), (1,))).astype(HALF)
        raw = dot(roots[0], prod)
        raw = jnp.where(iota(raw.shape, 0) < live, raw, 0.0)
        raw_sq = jnp.sum(jnp.sum(raw * raw, axis=0, keepdims=True), axis=1, keepdims=True)
        factor = jnp.sqrt(norm) / jnp.sqrt(raw_sq + GRAFT_EPS)
        d_ref[0] = jnp.where(taken == 1, factor * raw, 0.0).astype(HALF)
        own = m_ref[own_y, at, :]
        left_cols = dot(own, grad, ((1,), (1,)))
        own_columns = (iota((block_size, rows), 0) == own_mp * rows + iota((block_size, rows), 1)).astype(WIDE)
        columns = dot(grad, own_columns.astype(HALF)).astype(HALF)
        right_rows = dot(columns, grad, ((0,), (0,)))
        for old_ref, value, new_ref in ((ls_ref, left_cols, ln_ref), (rs_ref, right_rows, rn_ref)):
            old = old_ref[0]
            fresh = STAT_DECAY * old + (1.0 - STAT_DECAY) * value / block_size
            new_ref[0] = jnp.where(taken == 1, fresh, old)

    whole = pl.BlockSpec((ny, all_rows, block_size), lambda s: (0, 0, 0))
    square = pl.BlockSpec((1, block_size, block_size), lambda s: (s, 0, 0))
    strip = pl.BlockSpec((1, rows, block_size), lambda s: (s, 0, 0))
    return pl.pallas_call(
        kernel,
        grid=(slots,),
        out_shape=[
            jax.ShapeDtypeStruct(left_stat.shape, WIDE),
            jax.ShapeDtypeStruct(right_stat.shape, WIDE),
            jax.ShapeDtypeStruct((slots, block_size, block_size), HALF),
        ],
        in_specs=[pl.BlockSpec(memory_space=pltpu.SMEM), whole, whole]
        + [pl.BlockSpec((ny, 2, 1, rows, block_size), lambda s: (0, 0, s, 0, 0))] * 2
        + [strip, strip],
        out_specs=[strip, strip, square],
        scratch_shapes=[pltpu.VMEM((2, block_size, block_size), HALF)],
        compiler_params=PARAMS,
    )(facts, mine, other, roots_mine, roots_other, left_stat, right_stat)


def body(
    activations,
    out_grads,
    owners,
    live_rows,
    left_stat,
    right_stat,
    left_root,
    right_root,
    grad_acc,
):
    z, x, y, c = (lax.axis_index(name) for name in ("z", "x", "y", "c"))
    block_rows, rows, toks = activations.shape
    block_size = left_stat.shape[3]
    slots = left_stat.shape[1]
    block_count = owners.shape[0]
    per_z = rows // NZ
    columns = out_grads.shape[1] // block_size // NX
    my_owner = z * NX + x
    my_mp = y * NC + c
    my_rows = my_mp * rows

    ny = lax.axis_size("y")
    place = lax.axis_index(("z", "x", "y", "c")).reshape(1).astype(jnp.int32)
    pieces = prepare(activations, out_grads, place, ny)
    arrived = [lax.ppermute(piece, "x", ring(NX, step)) for piece, step in zip(pieces, (2, -1, 1))]

    piece_own, owners = lax.optimization_barrier((pieces[0], owners))
    targets = slot_targets(owners, slots)
    by_block = targets.reshape(block_rows, NX, columns).transpose(1, 2, 0)[:, :, None, None, :]
    shape = (NX, columns, 2, per_z, block_rows)
    owner = by_block // slots
    code = (((owner // NX) * slots + by_block % slots) * 2 + iota(shape, 2)) * per_z + iota(shape, 3)
    code = jnp.where(owner % NX == x, code, -1).reshape(1, -1)
    out_rows = NZ * slots * 2 * per_z
    chosen = (code == iota((out_rows, 1), 0)).astype(HALF)
    piece_own, chosen = lax.optimization_barrier((piece_own, chosen))
    own = own_part(piece_own, out_grads, place, ny)

    own, left_root, right_root = lax.optimization_barrier((own, left_root, right_root))
    roots = jnp.stack([left_root[0], right_root[0]])[None]
    for step in (1, 2):
        if step < ny:
            came = lax.ppermute(roots, "y", [(i, i ^ step) for i in range(ny)])
            roots = jnp.concatenate([roots, came], axis=0)
    own, roots = lax.optimization_barrier((own, roots))
    swapped = [lax.ppermute(piece, "c", ring(NC, 1)) for piece in arrived]
    roots_other = lax.ppermute(roots, "c", ring(NC, 1))

    sent = [partial_products(own, arrived, swapped, True, chunk) for chunk in range(CHUNKS)]
    kept = [partial_products(own, arrived, swapped, False, chunk) for chunk in range(CHUNKS)]

    def along(out, step):
        goals = [((i + (1 - 2 * k) * step) % NZ) * NC + k for i in range(NZ) for k in range(NC)]
        return lax.ppermute(out, ("z", "c"), list(enumerate(goals)))

    lasts, sums = [], []
    for out, keep in zip(sent, kept):
        first = along(out, 1)
        part = first.shape[0] // 2
        second = along((keep[part:] + first[part:]).astype(HALF), 2)
        half = part // 2
        lasts.append((keep[half:part] + first[half:part] + second[half:]).astype(HALF))
        sums.append((keep[:half], first[:half], second[:half]))
    third = along(jnp.concatenate(lasts, axis=0), 4)
    sums = [
        (a + b + d + third[k * half : (k + 1) * half]).astype(HALF) for k, (a, b, d) in enumerate(sums)
    ]
    sums = jnp.concatenate(sums, axis=0)
    sums = lax.all_gather(sums, "x", axis=0, tiled=False)

    picked = pick_blocks(chosen, sums, block_size).reshape(NZ, out_rows // NZ, block_size)
    arrived = lax.all_to_all(picked, "z", 0, 0, tiled=True).reshape(out_rows, block_size)

    wanted = my_owner * slots + iota((slots, block_count), 0)
    matched = targets[None, :] == wanted
    occupied = jnp.any(matched, axis=1).astype(jnp.int32)
    live_mine = jnp.sum(jnp.where(matched, live_rows[None, :], 0), axis=1).astype(jnp.int32)
    own_rows, acc_next = finish_sum(live_mine - my_rows, arrived, grad_acc[0])
    rows_mine = lax.all_gather(own_rows, "y", axis=0, tiled=False)
    rows_other = lax.ppermute(rows_mine, "c", ring(NC, 1))
    facts = jnp.concatenate([jnp.stack([c, y, my_mp]).astype(jnp.int32), live_mine, occupied])
    left_next, right_next, directions = update(
        facts, rows_mine, rows_other, roots, roots_other, left_stat[0], right_stat[0]
    )
    return (left_next[None], right_next[None], acc_next[None], directions[None])


def solution(mesh):
    dp, mp = mesh.devices.shape
    parts = Mesh(mesh.devices.reshape(NZ, NX, mp // NC, NC), ("z", "x", "y", "c"))
    owner, strip = ("z", "x"), ("y", "c")
    state = P(owner, None, strip, None)
    return jax.shard_map(
        body,
        mesh=parts,
        in_specs=(P(None, strip, owner), P(owner, None), P(), P(), state, state, state, state, state),
        out_specs=(state, state, state, P(owner, None, None, None)),
        check_vma=False,
    )
```

```python
import jax
import jax.numpy as jnp
from jax import lax
from jax.experimental import pallas as pl
from jax.experimental.pallas import tpu as pltpu
from jax.sharding import Mesh, PartitionSpec as P

STAT_DECAY = 0.9
GRAFT_EPS = 1e-06
HALF = jnp.bfloat16
WIDE = jnp.float32
NZ, NX, NC = 16, 4, 2
TILES = 6
CHUNKS = 2
ROOMY = pltpu.CompilerParams(vmem_limit_bytes=60 * 1024 * 1024)
PARAMS = pltpu.CompilerParams(vmem_limit_bytes=8 * 1024 * 1024)


def slot_targets(owners, slot_count):
    block_count = owners.shape[0]
    same_owner = owners[:, None] == owners[None, :]
    earlier = lax.broadcasted_iota(jnp.int32, (block_count, block_count), 1) < lax.broadcasted_iota(
        jnp.int32, (block_count, block_count), 0
    )
    ranked = jnp.sum(jnp.where(same_owner & earlier, 1, 0), axis=1).astype(jnp.int32)
    return owners * slot_count + ranked


def position(place_ref, ny):
    index = place_ref[0]
    return index // (NX * ny * NC), index // (ny * NC) % NX, index % NC


def ring(count, step):
    return [(i, (i + step) % count) for i in range(count)]


def iota(shape, dim):
    return lax.broadcasted_iota(jnp.int32, shape, dim)


def dot(a, b, dims=((1,), (0,))):
    return lax.dot_general(a, b, (dims, ((), ())), preferred_element_type=WIDE)


def prepare(activations, out_grads, place, ny):
    block_rows, rows, toks = activations.shape
    per_z = rows // NZ
    count = block_rows * rows // 2
    half = toks // NC
    width = out_grads.shape[1] // NX
    tile = width // TILES

    def kernel(place_ref, a_ref, b_ref, *refs):
        out_refs, (held, rows_in, sems, out_sems, rows_sem) = refs[:3], refs[3:]
        z, x, c = position(place_ref, ny)
        rows_copy = pltpu.make_async_copy(a_ref, rows_in, rows_sem)
        rows_copy.start()
        tok = pl.ds(pl.multiple_of(c * half, half), half)
        copies = []
        for i in range(3):
            begin = jnp.bitwise_and(x + (2, 3, 1)[i], NX - 1) * width
            for n in range(TILES):
                at = pl.ds(pl.multiple_of(begin + n * tile, tile), tile)
                to = pl.ds(2 * count + n * half, half)
                copies.append(pltpu.make_async_copy(b_ref.at[tok, at], held.at[i, to, :], sems.at[i, n]))
        for copy in copies:
            copy.start()
        m, k = iota((count, 2 * count), 0), iota((count, 2 * count), 1)
        block = m % block_rows
        row = (m // block_rows) % per_z
        tail = m // (block_rows * per_z)
        high = 2 * (tail // 4) + 4 * ((tail // 2) % 2) + 8 * (tail % 2)
        picks = []
        for odd in range(2):
            goal = jnp.bitwise_and(z + (1 - 2 * c) * (high + odd), NZ - 1)
            picks.append((block * rows + goal * per_z + row == k).astype(WIDE).astype(HALF))
        rows_copy.wait()
        values = rows_in[...].reshape(2 * count, toks)
        for odd in range(2):
            moved = dot(picks[odd], values).astype(HALF)
            turned = jnp.concatenate([moved[:, half:], moved[:, :half]], axis=1)
            at = (1 - odd) * count
            ordered = jnp.where(c == 1, turned, moved)
            for i in range(3):
                held[i, at : at + count, :] = ordered
        last = [pltpu.make_async_copy(held.at[i], out_refs[i], out_sems.at[i]) for i in range(3)]
        for i in range(3):
            for copy in copies[i * TILES : (i + 1) * TILES]:
                copy.wait()
            last[i].start()
        for copy in last:
            copy.wait()

    piece = (2 * count + TILES * half, toks)
    any_place = pl.BlockSpec(memory_space=pl.ANY)
    return pl.pallas_call(
        kernel,
        out_shape=[jax.ShapeDtypeStruct(piece, HALF)] * 3,
        in_specs=[
            pl.BlockSpec(memory_space=pltpu.SMEM),
            any_place,
            any_place,
        ],
        out_specs=[any_place] * 3,
        scratch_shapes=[
            pltpu.VMEM((3, *piece), HALF),
            pltpu.VMEM(activations.shape, HALF),
            pltpu.SemaphoreType.DMA((3, TILES)),
            pltpu.SemaphoreType.DMA((3,)),
            pltpu.SemaphoreType.DMA,
        ],
        compiler_params=ROOMY,
    )(place, activations, out_grads)


def own_part(piece, out_grads, place, ny):
    toks = out_grads.shape[0]
    half = toks // NC
    width = out_grads.shape[1] // NX
    tile = width // TILES
    count = piece.shape[0] - TILES * half

    def kernel(place_ref, p_ref, b_ref, o_ref):
        c = position(place_ref, ny)[2]
        o_ref[:count, :] = p_ref[...]
        for n in range(TILES):
            for side, who in enumerate((c, 1 - c)):
                at = count + (2 * n + side) * half
                tok = pl.ds(pl.multiple_of(who * half, half), half)
                o_ref[at : at + half, :] = b_ref[tok, n * tile : (n + 1) * tile]

    own = (count + TILES * toks, tile)
    return pl.pallas_call(
        kernel,
        out_shape=jax.ShapeDtypeStruct(own, HALF),
        grid_spec=pltpu.PrefetchScalarGridSpec(
            num_scalar_prefetch=1,
            grid=(1,),
            in_specs=[
                pl.BlockSpec((count, tile), lambda i, place_ref: (0, 0)),
                pl.BlockSpec((toks, width), lambda i, place_ref: (0, position(place_ref, ny)[1])),
            ],
            out_specs=pl.BlockSpec(own, lambda i, place_ref: (0, 0)),
        ),
        compiler_params=ROOMY,
    )(place, piece, out_grads)


def partial_products(own, arrived, swapped, odd, chunk):
    toks = own.shape[1]
    half = toks // NC
    total_rows = own.shape[0] - TILES * toks
    count = total_rows // 2
    kind = HALF if odd else WIDE
    group = TILES // CHUNKS

    def kernel(*refs):
        rows_refs, own_ref, mine, other, out_ref = refs[:4], refs[4], refs[5:8], refs[8:11], refs[11]
        for n in range(group):
            at = slice(n * half, (n + 1) * half)
            total = dot(rows_refs[0][...], own_ref[n * toks : (n + 1) * toks, :])
            for rows_ref, m_ref, o_ref in zip(rows_refs[1:], mine, other):
                total += dot(rows_ref[...], jnp.concatenate([m_ref[at, :], o_ref[at, :]], axis=0))
            to = slice(n * toks, (n + 1) * toks)
            out_ref[:, to] = total.astype(kind)

    def block(skip, size):
        first = pl.Element(size)
        return pl.BlockSpec((first, pl.Element(toks)), lambda n: (skip + chunk * size, 0))

    rows = pl.BlockSpec((count, toks), lambda n: (0 if odd else 1, 0))
    return pl.pallas_call(
        kernel,
        grid=(1,),
        out_shape=jax.ShapeDtypeStruct((count, group * toks), kind),
        in_specs=[rows] * 4 + [block(total_rows, group * toks)] + [block(total_rows, group * half)] * 6,
        out_specs=pl.BlockSpec((count, group * toks), lambda n: (0, 0)),
        compiler_params=PARAMS,
    )(own, *arrived, own, *arrived, *swapped)


def pick_blocks(chosen, sums, block_size):
    sources, rows, width = sums.shape[0], sums.shape[1] // CHUNKS, sums.shape[2]
    columns = CHUNKS * width // block_size
    out_rows = chosen.shape[0]
    tile = out_rows // 2

    def kernel(p_ref, s_ref, o_ref):
        total = None
        for pair in range(sources // 2):
            depth = 2 * columns * rows
            pieces = []
            for x in (2 * pair, 2 * pair + 1):
                whole = jnp.concatenate([s_ref[x, k * rows : (k + 1) * rows, :] for k in range(CHUNKS)], axis=1)
                pieces += [whole[:, j * block_size : (j + 1) * block_size] for j in range(columns)]
            term = dot(p_ref[:, pair * depth : (pair + 1) * depth], jnp.concatenate(pieces, axis=0))
            total = term if total is None else total + term
        o_ref[...] = total.astype(HALF)

    return pl.pallas_call(
        kernel,
        grid=(2,),
        out_shape=jax.ShapeDtypeStruct((out_rows, block_size), HALF),
        in_specs=[
            pl.BlockSpec((tile, chosen.shape[1]), lambda n: (n, 0)),
            pl.BlockSpec(sums.shape, lambda n: (0, 0, 0)),
        ],
        out_specs=pl.BlockSpec((tile, block_size), lambda n: (n, 0)),
        compiler_params=PARAMS,
    )(chosen, sums)


def finish_sum(limits, pieces, acc):
    slots, rows, block_size = acc.shape
    per_z = rows // NZ
    total_rows = slots * rows
    piece_rows = pieces.shape[0]

    def kernel(lim_ref, p_ref, a_ref, g_ref, n_ref):
        m, k = iota((total_rows, piece_rows), 0), iota((total_rows, piece_rows), 1)
        row = k % per_z
        piece = (k // per_z) % 2
        slot = (k // (2 * per_z)) % slots
        source = k // (2 * per_z * slots)
        goal = jnp.bitwise_and(source + 8 * piece, NZ - 1)
        adds = (slot * rows + goal * per_z + row == m).astype(WIDE).astype(HALF)
        grad = dot(adds, p_ref[...])
        lane = iota((16, block_size), 1)
        extra_row = iota((16, block_size), 0)
        extra = jnp.zeros((16, block_size), WIDE)
        for s in range(slots):
            live = iota((rows, block_size), 0) < lim_ref[s]
            own = jnp.where(live, grad[s * rows : (s + 1) * rows], 0.0)
            new = a_ref[s] + own * own
            n_ref[s] = new
            grafted = own / (jnp.sqrt(new) + GRAFT_EPS)
            norm = jnp.sum(jnp.sum(grafted * grafted, axis=0, keepdims=True), axis=1, keepdims=True)
            high = norm.astype(HALF).astype(WIDE)
            middle = (norm - high).astype(HALF).astype(WIDE)
            low = norm - high - middle
            spread = jnp.where(lane == 0, high, jnp.where(lane == 1, middle, jnp.where(lane == 2, low, 0.0)))
            extra = jnp.where(extra_row == s, spread, extra)
            g_ref[s * rows : (s + 1) * rows, :] = own.astype(HALF)
        g_ref[total_rows:, :] = extra.astype(HALF)

    vmem = pl.BlockSpec(memory_space=pltpu.VMEM)
    return pl.pallas_call(
        kernel,
        out_shape=[
            jax.ShapeDtypeStruct((total_rows + 16, block_size), HALF),
            jax.ShapeDtypeStruct(acc.shape, WIDE),
        ],
        in_specs=[pl.BlockSpec(memory_space=pltpu.SMEM), vmem, vmem],
        out_specs=[vmem, vmem],
        compiler_params=PARAMS,
    )(limits, pieces, acc)


def update(facts, mine, other, roots_mine, roots_other, left_stat, right_stat):
    ny = mine.shape[0]
    slots, rows, block_size = left_stat.shape
    all_rows = mine.shape[1]

    def kernel(f_ref, m_ref, o_ref, rm_ref, ro_ref, ls_ref, rs_ref, ln_ref, rn_ref, d_ref, roots):
        s = pl.program_id(0)
        core, own_y, own_mp = f_ref[0], f_ref[1], f_ref[2]
        live, taken = f_ref[3 + s], f_ref[5 + s]
        at = pl.ds(pl.multiple_of(s * rows, rows), rows)
        for i in range(ny):
            source = jnp.bitwise_xor(own_y, i) * NC
            for ref, who in ((rm_ref, core), (ro_ref, 1 - core)):
                to = pl.ds(pl.multiple_of((source + who) * rows, rows), rows)
                for kind in range(2):
                    roots[kind, to, :] = ref[i, kind, 0]
        parts = []
        norm = jnp.zeros((1, 1), WIDE)
        tail_row = iota((16, block_size), 0) == s
        for y in range(ny):
            a, b = m_ref[y, at, :], o_ref[y, at, :]
            parts += [jnp.where(core == 0, a, b), jnp.where(core == 0, b, a)]
            for ref in (m_ref, o_ref):
                tail = jnp.where(tail_row, ref[y, slots * rows : all_rows, :].astype(WIDE), 0.0)
                norm += jnp.sum(jnp.sum(tail, axis=0, keepdims=True), axis=1, keepdims=True)
        grad = jnp.concatenate(parts, axis=0)
        prod = dot(grad, roots[1], ((1,), (1,))).astype(HALF)
        raw = dot(roots[0], prod)
        raw = jnp.where(iota(raw.shape, 0) < live, raw, 0.0)
        raw_sq = jnp.sum(jnp.sum(raw * raw, axis=0, keepdims=True), axis=1, keepdims=True)
        factor = jnp.sqrt(norm) / jnp.sqrt(raw_sq + GRAFT_EPS)
        d_ref[0] = jnp.where(taken == 1, factor * raw, 0.0).astype(HALF)
        own = m_ref[own_y, at, :]
        left_cols = dot(own, grad, ((1,), (1,)))
        own_columns = (iota((block_size, rows), 0) == own_mp * rows + iota((block_size, rows), 1)).astype(WIDE)
        columns = dot(grad, own_columns.astype(HALF)).astype(HALF)
        right_rows = dot(columns, grad, ((0,), (0,)))
        for old_ref, value, new_ref in ((ls_ref, left_cols, ln_ref), (rs_ref, right_rows, rn_ref)):
            old = old_ref[0]
            fresh = STAT_DECAY * old + (1.0 - STAT_DECAY) * value / block_size
            new_ref[0] = jnp.where(taken == 1, fresh, old)

    whole = pl.BlockSpec((ny, all_rows, block_size), lambda s: (0, 0, 0))
    square = pl.BlockSpec((1, block_size, block_size), lambda s: (s, 0, 0))
    strip = pl.BlockSpec((1, rows, block_size), lambda s: (s, 0, 0))
    return pl.pallas_call(
        kernel,
        grid=(slots,),
        out_shape=[
            jax.ShapeDtypeStruct(left_stat.shape, WIDE),
            jax.ShapeDtypeStruct(right_stat.shape, WIDE),
            jax.ShapeDtypeStruct((slots, block_size, block_size), HALF),
        ],
        in_specs=[pl.BlockSpec(memory_space=pltpu.SMEM), whole, whole]
        + [pl.BlockSpec((ny, 2, 1, rows, block_size), lambda s: (0, 0, s, 0, 0))] * 2
        + [strip, strip],
        out_specs=[strip, strip, square],
        scratch_shapes=[pltpu.VMEM((2, block_size, block_size), HALF)],
        compiler_params=PARAMS,
    )(facts, mine, other, roots_mine, roots_other, left_stat, right_stat)


def body(
    activations,
    out_grads,
    owners,
    live_rows,
    left_stat,
    right_stat,
    left_root,
    right_root,
    grad_acc,
):
    z, x, y, c = (lax.axis_index(name) for name in ("z", "x", "y", "c"))
    block_rows, rows, toks = activations.shape
    block_size = left_stat.shape[3]
    slots = left_stat.shape[1]
    block_count = owners.shape[0]
    per_z = rows // NZ
    columns = out_grads.shape[1] // block_size // NX
    my_owner = z * NX + x
    my_mp = y * NC + c
    my_rows = my_mp * rows

    ny = lax.axis_size("y")
    place = lax.axis_index(("z", "x", "y", "c")).reshape(1).astype(jnp.int32)
    pieces = prepare(activations, out_grads, place, ny)
    arrived = [lax.ppermute(piece, "x", ring(NX, step)) for piece, step in zip(pieces, (2, -1, 1))]

    piece_own, owners = lax.optimization_barrier((pieces[0], owners))
    targets = slot_targets(owners, slots)
    by_block = targets.reshape(block_rows, NX, columns).transpose(1, 2, 0)[:, :, None, None, :]
    shape = (NX, columns, 2, per_z, block_rows)
    owner = by_block // slots
    code = (((owner // NX) * slots + by_block % slots) * 2 + iota(shape, 2)) * per_z + iota(shape, 3)
    code = jnp.where(owner % NX == x, code, -1).reshape(1, -1)
    out_rows = NZ * slots * 2 * per_z
    chosen = (code == iota((out_rows, 1), 0)).astype(HALF)
    piece_own, chosen = lax.optimization_barrier((piece_own, chosen))
    own = own_part(piece_own, out_grads, place, ny)

    own, left_root, right_root = lax.optimization_barrier((own, left_root, right_root))
    roots = jnp.stack([left_root[0], right_root[0]])[None]
    for step in (1, 2):
        if step < ny:
            came = lax.ppermute(roots, "y", [(i, i ^ step) for i in range(ny)])
            roots = jnp.concatenate([roots, came], axis=0)
    own, roots = lax.optimization_barrier((own, roots))
    swapped = [lax.ppermute(piece, "c", ring(NC, 1)) for piece in arrived]
    roots_other = lax.ppermute(roots, "c", ring(NC, 1))

    sent = [partial_products(own, arrived, swapped, True, chunk) for chunk in range(CHUNKS)]
    kept = [partial_products(own, arrived, swapped, False, chunk) for chunk in range(CHUNKS)]

    sums = []
    for out, keep in zip(sent, kept):
        got = []
        for step in (1, 2, 4):
            goals = [((i + (1 - 2 * k) * step) % NZ) * NC + k for i in range(NZ) for k in range(NC)]
            got.append(lax.ppermute(out, ("z", "c"), list(enumerate(goals))))
            part = got[-1].shape[0] // (2 if step < 4 else 1)
            rows_from = slice(part, 2 * part) if step < 4 else slice(0, part)
            total = keep[rows_from]
            for rows_in in got:
                total = total + rows_in[rows_from]
            out = total.astype(HALF)
        sums.append(out)
    sums = lax.all_gather(jnp.concatenate(sums, axis=0), "x", axis=0, tiled=False)

    picked = pick_blocks(chosen, sums, block_size).reshape(NZ, out_rows // NZ, block_size)
    arrived = lax.all_to_all(picked, "z", 0, 0, tiled=True).reshape(out_rows, block_size)

    wanted = my_owner * slots + iota((slots, block_count), 0)
    matched = targets[None, :] == wanted
    occupied = jnp.any(matched, axis=1).astype(jnp.int32)
    live_mine = jnp.sum(jnp.where(matched, live_rows[None, :], 0), axis=1).astype(jnp.int32)
    own_rows, acc_next = finish_sum(live_mine - my_rows, arrived, grad_acc[0])
    rows_mine = lax.all_gather(own_rows, "y", axis=0, tiled=False)
    rows_other = lax.ppermute(rows_mine, "c", ring(NC, 1))
    facts = jnp.concatenate([jnp.stack([c, y, my_mp]).astype(jnp.int32), live_mine, occupied])
    left_next, right_next, directions = update(
        facts, rows_mine, rows_other, roots, roots_other, left_stat[0], right_stat[0]
    )
    return (left_next[None], right_next[None], acc_next[None], directions[None])


def solution(mesh):
    dp, mp = mesh.devices.shape
    parts = Mesh(mesh.devices.reshape(NZ, NX, mp // NC, NC), ("z", "x", "y", "c"))
    owner, strip = ("z", "x"), ("y", "c")
    state = P(owner, None, strip, None)
    return jax.shard_map(
        body,
        mesh=parts,
        in_specs=(P(None, strip, owner), P(owner, None), P(), P(), state, state, state, state, state),
        out_specs=(state, state, state, P(owner, None, None, None)),
        check_vma=False,
    )
```

```python
import jax
import jax.numpy as jnp
from jax import lax
from jax.experimental import pallas as pl
from jax.experimental.pallas import tpu as pltpu
from jax.sharding import Mesh, PartitionSpec as P

STAT_DECAY = 0.9
GRAFT_EPS = 1e-06
HALF = jnp.bfloat16
WIDE = jnp.float32
NZ, NX, NC = 16, 4, 2
TILES = 6
CHUNKS = 2
ROOMY = pltpu.CompilerParams(vmem_limit_bytes=60 * 1024 * 1024)
PARAMS = pltpu.CompilerParams(vmem_limit_bytes=8 * 1024 * 1024)


def slot_targets(owners, slot_count):
    block_count = owners.shape[0]
    same_owner = owners[:, None] == owners[None, :]
    earlier = lax.broadcasted_iota(jnp.int32, (block_count, block_count), 1) < lax.broadcasted_iota(
        jnp.int32, (block_count, block_count), 0
    )
    ranked = jnp.sum(jnp.where(same_owner & earlier, 1, 0), axis=1).astype(jnp.int32)
    return owners * slot_count + ranked


def position(place_ref, ny):
    index = place_ref[0]
    return index // (NX * ny * NC), index // (ny * NC) % NX, index % NC


def ring(count, step):
    return [(i, (i + step) % count) for i in range(count)]


def iota(shape, dim):
    return lax.broadcasted_iota(jnp.int32, shape, dim)


def dot(a, b, dims=((1,), (0,))):
    return lax.dot_general(a, b, (dims, ((), ())), preferred_element_type=WIDE)


def prepare(activations, out_grads, place, ny):
    block_rows, rows, toks = activations.shape
    per_z = rows // NZ
    count = block_rows * rows // 2
    half = toks // NC
    width = out_grads.shape[1] // NX
    tile = width // TILES

    def kernel(place_ref, a_ref, b_ref, *refs):
        out_refs, (held, rows_in, sems, out_sems, rows_sem) = refs[:3], refs[3:]
        z, x, c = position(place_ref, ny)
        rows_copy = pltpu.make_async_copy(a_ref, rows_in, rows_sem)
        rows_copy.start()
        tok = pl.ds(pl.multiple_of(c * half, half), half)
        copies = []
        for i in range(3):
            begin = jnp.bitwise_and(x + (2, 3, 1)[i], NX - 1) * width
            for n in range(TILES):
                at = pl.ds(pl.multiple_of(begin + n * tile, tile), tile)
                to = pl.ds(2 * count + n * half, half)
                copies.append(pltpu.make_async_copy(b_ref.at[tok, at], held.at[i, to, :], sems.at[i, n]))
        for copy in copies:
            copy.start()
        m, k = iota((count, 2 * count), 0), iota((count, 2 * count), 1)
        block = m % block_rows
        row = (m // block_rows) % per_z
        tail = m // (block_rows * per_z)
        high = 2 * (tail // 4) + 4 * ((tail // 2) % 2) + 8 * (tail % 2)
        picks = []
        for odd in range(2):
            goal = jnp.bitwise_and(z + (1 - 2 * c) * (high + odd), NZ - 1)
            picks.append((block * rows + goal * per_z + row == k).astype(WIDE).astype(HALF))
        rows_copy.wait()
        values = rows_in[...].reshape(2 * count, toks)
        for odd in range(2):
            moved = dot(picks[odd], values).astype(HALF)
            turned = jnp.concatenate([moved[:, half:], moved[:, :half]], axis=1)
            at = (1 - odd) * count
            ordered = jnp.where(c == 1, turned, moved)
            for i in range(3):
                held[i, at : at + count, :] = ordered
        last = [pltpu.make_async_copy(held.at[i], out_refs[i], out_sems.at[i]) for i in range(3)]
        for i in range(3):
            for copy in copies[i * TILES : (i + 1) * TILES]:
                copy.wait()
            last[i].start()
        for copy in last:
            copy.wait()

    piece = (2 * count + TILES * half, toks)
    any_place = pl.BlockSpec(memory_space=pl.ANY)
    return pl.pallas_call(
        kernel,
        out_shape=[jax.ShapeDtypeStruct(piece, HALF)] * 3,
        in_specs=[
            pl.BlockSpec(memory_space=pltpu.SMEM),
            any_place,
            any_place,
        ],
        out_specs=[any_place] * 3,
        scratch_shapes=[
            pltpu.VMEM((3, *piece), HALF),
            pltpu.VMEM(activations.shape, HALF),
            pltpu.SemaphoreType.DMA((3, TILES)),
            pltpu.SemaphoreType.DMA((3,)),
            pltpu.SemaphoreType.DMA,
        ],
        compiler_params=ROOMY,
    )(place, activations, out_grads)


def own_part(piece, out_grads, place, ny):
    toks = out_grads.shape[0]
    half = toks // NC
    width = out_grads.shape[1] // NX
    tile = width // TILES
    count = piece.shape[0] - TILES * half

    def kernel(place_ref, p_ref, b_ref, o_ref):
        c = position(place_ref, ny)[2]
        o_ref[:count, :] = p_ref[...]
        for n in range(TILES):
            for side, who in enumerate((c, 1 - c)):
                at = count + (2 * n + side) * half
                tok = pl.ds(pl.multiple_of(who * half, half), half)
                o_ref[at : at + half, :] = b_ref[tok, n * tile : (n + 1) * tile]

    own = (count + TILES * toks, tile)
    return pl.pallas_call(
        kernel,
        out_shape=jax.ShapeDtypeStruct(own, HALF),
        grid_spec=pltpu.PrefetchScalarGridSpec(
            num_scalar_prefetch=1,
            grid=(1,),
            in_specs=[
                pl.BlockSpec((count, tile), lambda i, place_ref: (0, 0)),
                pl.BlockSpec((toks, width), lambda i, place_ref: (0, position(place_ref, ny)[1])),
            ],
            out_specs=pl.BlockSpec(own, lambda i, place_ref: (0, 0)),
        ),
        compiler_params=ROOMY,
    )(place, piece, out_grads)


def partial_products(own, arrived, swapped, odd, chunk):
    toks = own.shape[1]
    half = toks // NC
    total_rows = own.shape[0] - TILES * toks
    count = total_rows // 2
    kind = HALF if odd else WIDE
    group = TILES // CHUNKS

    def kernel(*refs):
        rows_refs, own_ref, mine, other, out_ref = refs[:4], refs[4], refs[5:8], refs[8:11], refs[11]
        for n in range(group):
            at = slice(n * half, (n + 1) * half)
            total = dot(rows_refs[0][...], own_ref[n * toks : (n + 1) * toks, :])
            for rows_ref, m_ref, o_ref in zip(rows_refs[1:], mine, other):
                total += dot(rows_ref[...], jnp.concatenate([m_ref[at, :], o_ref[at, :]], axis=0))
            to = slice(n * toks, (n + 1) * toks)
            out_ref[:, to] = total.astype(kind)

    def block(skip, size):
        first = pl.Element(size)
        return pl.BlockSpec((first, pl.Element(toks)), lambda n: (skip + chunk * size, 0))

    rows = pl.BlockSpec((count, toks), lambda n: (0 if odd else 1, 0))
    return pl.pallas_call(
        kernel,
        grid=(1,),
        out_shape=jax.ShapeDtypeStruct((count, group * toks), kind),
        in_specs=[rows] * 4 + [block(total_rows, group * toks)] + [block(total_rows, group * half)] * 6,
        out_specs=pl.BlockSpec((count, group * toks), lambda n: (0, 0)),
        compiler_params=PARAMS,
    )(own, *arrived, own, *arrived, *swapped)


def pick_blocks(chosen, sums, block_size):
    sources, rows, width = sums.shape[0], sums.shape[1] // CHUNKS, sums.shape[2]
    columns = CHUNKS * width // block_size
    out_rows = chosen.shape[0]
    tile = out_rows // 2

    def kernel(p_ref, s_ref, o_ref):
        total = None
        for pair in range(sources // 2):
            depth = 2 * columns * rows
            pieces = []
            for x in (2 * pair, 2 * pair + 1):
                whole = jnp.concatenate([s_ref[x, k * rows : (k + 1) * rows, :] for k in range(CHUNKS)], axis=1)
                pieces += [whole[:, j * block_size : (j + 1) * block_size] for j in range(columns)]
            term = dot(p_ref[:, pair * depth : (pair + 1) * depth], jnp.concatenate(pieces, axis=0))
            total = term if total is None else total + term
        o_ref[...] = total.astype(HALF)

    return pl.pallas_call(
        kernel,
        grid=(2,),
        out_shape=jax.ShapeDtypeStruct((out_rows, block_size), HALF),
        in_specs=[
            pl.BlockSpec((tile, chosen.shape[1]), lambda n: (n, 0)),
            pl.BlockSpec(sums.shape, lambda n: (0, 0, 0)),
        ],
        out_specs=pl.BlockSpec((tile, block_size), lambda n: (n, 0)),
        compiler_params=PARAMS,
    )(chosen, sums)


def finish_sum(limits, pieces, acc):
    slots, rows, block_size = acc.shape
    per_z = rows // NZ
    total_rows = slots * rows
    piece_rows = pieces.shape[0]

    def kernel(lim_ref, p_ref, a_ref, g_ref, n_ref):
        m, k = iota((total_rows, piece_rows), 0), iota((total_rows, piece_rows), 1)
        row = k % per_z
        piece = (k // per_z) % 2
        slot = (k // (2 * per_z)) % slots
        source = k // (2 * per_z * slots)
        goal = jnp.bitwise_and(source + 8 * piece, NZ - 1)
        adds = (slot * rows + goal * per_z + row == m).astype(WIDE).astype(HALF)
        grad = dot(adds, p_ref[...])
        lane = iota((16, block_size), 1)
        extra_row = iota((16, block_size), 0)
        extra = jnp.zeros((16, block_size), WIDE)
        for s in range(slots):
            live = iota((rows, block_size), 0) < lim_ref[s]
            own = jnp.where(live, grad[s * rows : (s + 1) * rows], 0.0)
            new = a_ref[s] + own * own
            n_ref[s] = new
            grafted = own / (jnp.sqrt(new) + GRAFT_EPS)
            norm = jnp.sum(jnp.sum(grafted * grafted, axis=0, keepdims=True), axis=1, keepdims=True)
            high = norm.astype(HALF).astype(WIDE)
            middle = (norm - high).astype(HALF).astype(WIDE)
            low = norm - high - middle
            spread = jnp.where(lane == 0, high, jnp.where(lane == 1, middle, jnp.where(lane == 2, low, 0.0)))
            extra = jnp.where(extra_row == s, spread, extra)
            g_ref[s * rows : (s + 1) * rows, :] = own.astype(HALF)
        g_ref[total_rows:, :] = extra.astype(HALF)

    vmem = pl.BlockSpec(memory_space=pltpu.VMEM)
    return pl.pallas_call(
        kernel,
        out_shape=[
            jax.ShapeDtypeStruct((total_rows + 16, block_size), HALF),
            jax.ShapeDtypeStruct(acc.shape, WIDE),
        ],
        in_specs=[pl.BlockSpec(memory_space=pltpu.SMEM), vmem, vmem],
        out_specs=[vmem, vmem],
        compiler_params=PARAMS,
    )(limits, pieces, acc)


def update(facts, mine, other, roots_mine, roots_other, left_stat, right_stat):
    ny = mine.shape[0]
    slots, rows, block_size = left_stat.shape
    all_rows = mine.shape[1]

    def kernel(f_ref, m_ref, o_ref, rm_ref, ro_ref, ls_ref, rs_ref, ln_ref, rn_ref, d_ref, roots):
        s = pl.program_id(0)
        core, own_y, own_mp = f_ref[0], f_ref[1], f_ref[2]
        live, taken = f_ref[3 + s], f_ref[5 + s]
        at = pl.ds(pl.multiple_of(s * rows, rows), rows)
        for i in range(ny):
            source = jnp.bitwise_xor(own_y, i) * NC
            for ref, who in ((rm_ref, core), (ro_ref, 1 - core)):
                to = pl.ds(pl.multiple_of((source + who) * rows, rows), rows)
                for kind in range(2):
                    roots[kind, to, :] = ref[i, kind, 0]
        parts = []
        norm = jnp.zeros((1, 1), WIDE)
        tail_row = iota((16, block_size), 0) == s
        for y in range(ny):
            a, b = m_ref[y, at, :], o_ref[y, at, :]
            parts += [jnp.where(core == 0, a, b), jnp.where(core == 0, b, a)]
            for ref in (m_ref, o_ref):
                tail = jnp.where(tail_row, ref[y, slots * rows : all_rows, :].astype(WIDE), 0.0)
                norm += jnp.sum(jnp.sum(tail, axis=0, keepdims=True), axis=1, keepdims=True)
        grad = jnp.concatenate(parts, axis=0)
        prod = dot(grad, roots[1], ((1,), (1,))).astype(HALF)
        raw = dot(roots[0], prod)
        raw = jnp.where(iota(raw.shape, 0) < live, raw, 0.0)
        raw_sq = jnp.sum(jnp.sum(raw * raw, axis=0, keepdims=True), axis=1, keepdims=True)
        factor = jnp.sqrt(norm) / jnp.sqrt(raw_sq + GRAFT_EPS)
        d_ref[0] = jnp.where(taken == 1, factor * raw, 0.0).astype(HALF)
        own = m_ref[own_y, at, :]
        left_cols = dot(own, grad, ((1,), (1,)))
        own_columns = (iota((block_size, rows), 0) == own_mp * rows + iota((block_size, rows), 1)).astype(WIDE)
        columns = dot(grad, own_columns.astype(HALF)).astype(HALF)
        right_rows = dot(columns, grad, ((0,), (0,)))
        for old_ref, value, new_ref in ((ls_ref, left_cols, ln_ref), (rs_ref, right_rows, rn_ref)):
            old = old_ref[0]
            fresh = STAT_DECAY * old + (1.0 - STAT_DECAY) * value / block_size
            new_ref[0] = jnp.where(taken == 1, fresh, old)

    whole = pl.BlockSpec((ny, all_rows, block_size), lambda s: (0, 0, 0))
    square = pl.BlockSpec((1, block_size, block_size), lambda s: (s, 0, 0))
    strip = pl.BlockSpec((1, rows, block_size), lambda s: (s, 0, 0))
    return pl.pallas_call(
        kernel,
        grid=(slots,),
        out_shape=[
            jax.ShapeDtypeStruct(left_stat.shape, WIDE),
            jax.ShapeDtypeStruct(right_stat.shape, WIDE),
            jax.ShapeDtypeStruct((slots, block_size, block_size), HALF),
        ],
        in_specs=[pl.BlockSpec(memory_space=pltpu.SMEM), whole, whole]
        + [pl.BlockSpec((ny, 2, 1, rows, block_size), lambda s: (0, 0, s, 0, 0))] * 2
        + [strip, strip],
        out_specs=[strip, strip, square],
        scratch_shapes=[pltpu.VMEM((2, block_size, block_size), HALF)],
        compiler_params=PARAMS,
    )(facts, mine, other, roots_mine, roots_other, left_stat, right_stat)


def body(
    activations,
    out_grads,
    owners,
    live_rows,
    left_stat,
    right_stat,
    left_root,
    right_root,
    grad_acc,
):
    z, x, y, c = (lax.axis_index(name) for name in ("z", "x", "y", "c"))
    block_rows, rows, toks = activations.shape
    block_size = left_stat.shape[3]
    slots = left_stat.shape[1]
    block_count = owners.shape[0]
    per_z = rows // NZ
    columns = out_grads.shape[1] // block_size // NX
    my_owner = z * NX + x
    my_mp = y * NC + c
    my_rows = my_mp * rows

    ny = lax.axis_size("y")
    place = lax.axis_index(("z", "x", "y", "c")).reshape(1).astype(jnp.int32)
    pieces = prepare(activations, out_grads, place, ny)
    arrived = [lax.ppermute(piece, "x", ring(NX, step)) for piece, step in zip(pieces, (2, -1, 1))]

    piece_own, owners = lax.optimization_barrier((pieces[0], owners))
    targets = slot_targets(owners, slots)
    by_block = targets.reshape(block_rows, NX, columns).transpose(1, 2, 0)[:, :, None, None, :]
    shape = (NX, columns, 2, per_z, block_rows)
    owner = by_block // slots
    code = (((owner // NX) * slots + by_block % slots) * 2 + iota(shape, 2)) * per_z + iota(shape, 3)
    code = jnp.where(owner % NX == x, code, -1).reshape(1, -1)
    out_rows = NZ * slots * 2 * per_z
    chosen = (code == iota((out_rows, 1), 0)).astype(HALF)
    piece_own, chosen = lax.optimization_barrier((piece_own, chosen))
    own = own_part(piece_own, out_grads, place, ny)

    own, left_root, right_root = lax.optimization_barrier((own, left_root, right_root))
    roots = jnp.stack([left_root[0], right_root[0]])[None]
    for step in (1, 2):
        if step < ny:
            came = lax.ppermute(roots, "y", [(i, i ^ step) for i in range(ny)])
            own, came = lax.optimization_barrier((own, came)) if step == 2 else (own, came)
            roots = jnp.concatenate([roots, came], axis=0)
    swapped = [lax.ppermute(piece, "c", ring(NC, 1)) for piece in arrived]
    roots_other = lax.ppermute(roots, "c", ring(NC, 1))

    sent = [partial_products(own, arrived, swapped, True, chunk) for chunk in range(CHUNKS)]
    kept = [partial_products(own, arrived, swapped, False, chunk) for chunk in range(CHUNKS)]

    sums = []
    for out, keep in zip(sent, kept):
        got = []
        for step in (1, 2, 4):
            goals = [((i + (1 - 2 * k) * step) % NZ) * NC + k for i in range(NZ) for k in range(NC)]
            got.append(lax.ppermute(out, ("z", "c"), list(enumerate(goals))))
            part = got[-1].shape[0] // (2 if step < 4 else 1)
            rows_from = slice(part, 2 * part) if step < 4 else slice(0, part)
            total = keep[rows_from]
            for rows_in in got:
                total = total + rows_in[rows_from]
            out = total.astype(HALF)
        sums.append(out)
    sums = lax.all_gather(jnp.concatenate(sums, axis=0), "x", axis=0, tiled=False)

    picked = pick_blocks(chosen, sums, block_size).reshape(NZ, out_rows // NZ, block_size)
    arrived = lax.all_to_all(picked, "z", 0, 0, tiled=True).reshape(out_rows, block_size)

    wanted = my_owner * slots + iota((slots, block_count), 0)
    matched = targets[None, :] == wanted
    occupied = jnp.any(matched, axis=1).astype(jnp.int32)
    live_mine = jnp.sum(jnp.where(matched, live_rows[None, :], 0), axis=1).astype(jnp.int32)
    own_rows, acc_next = finish_sum(live_mine - my_rows, arrived, grad_acc[0])
    rows_mine = lax.all_gather(own_rows, "y", axis=0, tiled=False)
    rows_other = lax.ppermute(rows_mine, "c", ring(NC, 1))
    facts = jnp.concatenate([jnp.stack([c, y, my_mp]).astype(jnp.int32), live_mine, occupied])
    left_next, right_next, directions = update(
        facts, rows_mine, rows_other, roots, roots_other, left_stat[0], right_stat[0]
    )
    return (left_next[None], right_next[None], acc_next[None], directions[None])


def solution(mesh):
    dp, mp = mesh.devices.shape
    parts = Mesh(mesh.devices.reshape(NZ, NX, mp // NC, NC), ("z", "x", "y", "c"))
    owner, strip = ("z", "x"), ("y", "c")
    state = P(owner, None, strip, None)
    return jax.shard_map(
        body,
        mesh=parts,
        in_specs=(P(None, strip, owner), P(owner, None), P(), P(), state, state, state, state, state),
        out_specs=(state, state, state, P(owner, None, None, None)),
        check_vma=False,
    )
```
